32 devices in a mesh: dp: 8 (over z, y), mp: 4 (over x, core).
Axes of the slice: x: 2, y: 2, z: 4, core: 2. Of those that a mesh axis runs over, the one named last changes fastest.
Arguments:
- tokens: bfloat16 [32768, 768], P('dp'), may hold values from -6 to 6
- cotangent: bfloat16 [32768, 768], P('dp'), may hold values from -6 to 6
- attention_norm_gain: bfloat16 [768], replicated, may hold values from 0.099609375 to 1.8984375
- feedforward_norm_gain: bfloat16 [768], replicated, may hold values from 0.099609375 to 1.8984375
- query_projection_weight: bfloat16 [768, 768], P(None, 'mp'), may hold values from -0.03125 to 0.03125
- key_value_weight: bfloat16 [2, 768, 768], P(None, None, 'mp'), may hold values from -0.21875 to 0.21875
- attention_output_weight: bfloat16 [768, 768], P('mp'), may hold values from -0.625 to 0.625
- ffn_input_weight: bfloat16 [768, 3072], P(None, 'mp'), may hold values from -0.21875 to 0.21875
- ffn_output_weight: bfloat16 [3072, 768], P('mp'), may hold values from -0.109375 to 0.109375
- projection_down_weight: bfloat16 [3, 768, 40], replicated, may hold values from -0.21875 to 0.21875
- query_up_weight: bfloat16 [40, 768], P(None, 'mp'), may hold values from -1.5 to 1.5
- key_value_up_weight: bfloat16 [2, 40, 768], P(None, None, 'mp'), may hold values from -9 to 9
- attention_output_down_weight: bfloat16 [768, 40], replicated, may hold values from -0.625 to 0.625
- attention_output_up_weight: bfloat16 [40, 768], replicated, may hold values from -9 to 9
- ffn_input_down_weight: bfloat16 [768, 40], replicated, may hold values from -0.21875 to 0.21875
- ffn_input_up_weight: bfloat16 [40, 3072], P(None, 'mp'), may hold values from -9 to 9
- ffn_output_down_weight: bfloat16 [3072, 40], replicated, may hold values from -0.109375 to 0.109375
- ffn_output_up_weight: bfloat16 [40, 768], replicated, may hold values from -12 to 12
- attention_router_weight: bfloat16 [768, 10], replicated, may hold values from -0.109375 to 0.109375
- feedforward_router_weight: bfloat16 [768, 10], replicated, may hold values from -0.109375 to 0.109375
- bucket_bias_table: bfloat16 [32, 12], P(None, 'mp'), may hold values from -3 to 3
- offset_bucket_map: int32 [1023], replicated, may hold values from 0 to 31
- sequence_length_list: int32 [160], P('dp'), may hold values from 32 to 512, as said below
Outputs:
- output: bfloat16 [32768, 768], P('dp')
- grad_tokens: bfloat16 [32768, 768], P('dp')
- grad_attn_gain: float32 [768], replicated
- grad_ffn_gain: float32 [768], replicated
- grad_lora_a_qkv: float32 [3, 768, 40], replicated
- grad_lora_b_query: float32 [40, 768], P(None, 'mp')
- grad_lora_b_keyval: float32 [2, 40, 768], P(None, None, 'mp')
- grad_lora_a_out: float32 [768, 40], replicated
- grad_lora_b_out: float32 [40, 768], replicated
- grad_lora_a_in: float32 [768, 40], replicated
- grad_lora_b_in: float32 [40, 3072], P(None, 'mp')
- grad_lora_a_ffout: float32 [3072, 40], replicated
- grad_lora_b_ffout: float32 [40, 768], replicated
- grad_router_attn: float32 [768, 10], replicated
- grad_router_ffn: float32 [768, 10], replicated
- grad_bias_table: float32 [32, 12], P(None, 'mp')
The draws below stay inside these ranges and needn't reach their ends.
Inputs may be any that keep to these rules, and one draw needn't show every extreme that they name: `sequence_length_list`: block by block of 20: 16 lengths of short sequences, the first equal to 128 and the others from 32 to 128, then 4 lengths of long sequences from 128 to 512; the first long sequence of every fourth block has length 512.
All inputs are finite; a program needn't handle non-finite values.
Results may differ from the reference program's by a relative error of at most 0.022.
The reference program's roundings to bfloat16 on the way count: a program that leaves them out, or rounds other values in their place, can miss the bound.
Values may be sent and summed in bfloat16 or wider, within the bound.
No kernel may reach another device: no remote copies, remote signals or barrier semaphores. Data moves between devices by JAX's collectives and lax.ppermute only.
A program may use at most 320 MiB of HBM per device.

```python
import jax
import jax.numpy as jnp
from jax import lax

MODEL_WIDTH = 768
HIDDEN_UNITS = 3072
ATTENTION_HEADS = 12
HEAD_WIDTH = 64
BUCKETS = 32
ADAPTER_EXPERTS = 10
ADAPTER_RANK = 4
SHORT_LEN = 128
LONG_LEN = 512
LONG_SEQS = 4
SHORT_SEQS = 16
SEQ_DEV = 20
TOK_DEV = 4096
TOKENS = 32768
NSEQ = 160


def draw_sequence_length_list(key, part):
    blocks_dp = NSEQ // SEQ_DEV
    key_short, key_long = jax.random.split(key)
    short_lens = jax.random.randint(key_short, (blocks_dp, SHORT_SEQS), SHORT_LEN // 4, SHORT_LEN + 1)
    short_lens = short_lens.at[:, 0].set(SHORT_LEN)
    long_lens = jax.random.randint(key_long, (blocks_dp, LONG_SEQS), LONG_LEN // 4, LONG_LEN + 1)
    long_lens = long_lens.at[::4, 0].set(LONG_LEN)
    return jnp.concatenate([short_lens, long_lens], 1).reshape(-1).astype(jnp.int32)


def with_ends(entries, key, smallest, high):
    spot = [jax.random.randint(jax.random.fold_in(key, axis), (), 0, length) for axis, length in enumerate(entries.shape)]
    widest = entries.shape.index(max(entries.shape))
    beside = spot[:widest] + [(spot[widest] + 1) % entries.shape[widest]] + spot[widest + 1:]
    return entries.at[tuple(spot)].set(smallest).at[tuple(beside)].set(high)


def block_levels(stream_key, shape, cuts, low, high):
    level = 1.0
    for axis_at, blocks in cuts:
        draws = jax.random.uniform(jax.random.fold_in(jax.random.fold_in(stream_key, 6), axis_at), (blocks,), jnp.float32, low / len(cuts), high / len(cuts))
        level = level * jnp.repeat(jnp.exp(draws), shape[axis_at] // blocks).reshape((-1,) + (1,) * (len(shape) - 1 - axis_at))
    return level


def bell_draw(stream_key, shape, scale, reach, cuts=(), held_as=jnp.bfloat16):
    array = jax.random.normal(stream_key, shape, jnp.float32) * scale
    if len(cuts) > 0:
        array = block_levels(stream_key, shape, cuts, -0.22, 0.18) * array
    return jnp.clip(array, min=-reach, max=reach).astype(held_as)


def setup_inputs(seed: int = 0) -> dict:
    streams_of = jax.random.split(jax.random.key(seed), 24)
    tokens = bell_draw(streams_of[0], (TOKENS, MODEL_WIDTH), 1.0, 6.0, ((0, 8),))
    cotangent = bell_draw(streams_of[1], (TOKENS, MODEL_WIDTH), 1.0, 6.0, ((0, 8),))
    attention_norm_gain = jnp.clip(1.0 + 0.18 * jax.random.normal(streams_of[2], (MODEL_WIDTH,), jnp.float32), 0.099609375, 1.8984375).astype(jnp.bfloat16)
    feedforward_norm_gain = jnp.clip(1.0 + 0.18 * jax.random.normal(streams_of[3], (MODEL_WIDTH,), jnp.float32), 0.099609375, 1.8984375).astype(jnp.bfloat16)
    query_projection_weight = bell_draw(streams_of[4], (MODEL_WIDTH, ATTENTION_HEADS * HEAD_WIDTH), (48 * MODEL_WIDTH) ** -0.5, 0.03125, ((1, 4),))
    key_value_weight = bell_draw(streams_of[5], (2, MODEL_WIDTH, ATTENTION_HEADS * HEAD_WIDTH), MODEL_WIDTH ** -0.5, 0.21875, ((2, 4),))
    attention_output_weight = bell_draw(streams_of[6], (ATTENTION_HEADS * HEAD_WIDTH, MODEL_WIDTH), (ATTENTION_HEADS * HEAD_WIDTH // 8) ** -0.5, 0.625, ((0, 4),))
    ffn_input_weight = bell_draw(streams_of[7], (MODEL_WIDTH, HIDDEN_UNITS), MODEL_WIDTH ** -0.5, 0.21875, ((1, 4),))
    ffn_output_weight = bell_draw(streams_of[8], (HIDDEN_UNITS, MODEL_WIDTH), HIDDEN_UNITS ** -0.5, 0.109375, ((0, 4),))
    projection_down_weight = bell_draw(streams_of[9], (3, MODEL_WIDTH, ADAPTER_EXPERTS * ADAPTER_RANK), MODEL_WIDTH ** -0.5, 0.21875)
    query_up_weight = bell_draw(streams_of[10], (ADAPTER_EXPERTS * ADAPTER_RANK, ATTENTION_HEADS * HEAD_WIDTH), 0.25, 1.5, ((1, 4),))
    key_value_up_weight = bell_draw(streams_of[11], (2, ADAPTER_EXPERTS * ADAPTER_RANK, ATTENTION_HEADS * HEAD_WIDTH), 1.5, 9.0, ((2, 4),))
    attention_output_down_weight = bell_draw(streams_of[12], (ATTENTION_HEADS * HEAD_WIDTH, ADAPTER_EXPERTS * ADAPTER_RANK), (ATTENTION_HEADS * HEAD_WIDTH // 8) ** -0.5, 0.625)
    attention_output_up_weight = bell_draw(streams_of[13], (ADAPTER_EXPERTS * ADAPTER_RANK, MODEL_WIDTH), 1.5, 9.0)
    ffn_input_down_weight = bell_draw(streams_of[14], (MODEL_WIDTH, ADAPTER_EXPERTS * ADAPTER_RANK), MODEL_WIDTH ** -0.5, 0.21875)
    ffn_input_up_weight = bell_draw(streams_of[15], (ADAPTER_EXPERTS * ADAPTER_RANK, HIDDEN_UNITS), 1.5, 9.0, ((1, 4),))
    ffn_output_down_weight = bell_draw(streams_of[16], (HIDDEN_UNITS, ADAPTER_EXPERTS * ADAPTER_RANK), HIDDEN_UNITS ** -0.5, 0.109375)
    ffn_output_up_weight = bell_draw(streams_of[17], (ADAPTER_EXPERTS * ADAPTER_RANK, MODEL_WIDTH), 2.0, 12.0)
    attention_router_weight = bell_draw(streams_of[18], (MODEL_WIDTH, ADAPTER_EXPERTS), (4 * MODEL_WIDTH) ** -0.5, 0.109375)
    feedforward_router_weight = bell_draw(streams_of[19], (MODEL_WIDTH, ADAPTER_EXPERTS), (4 * MODEL_WIDTH) ** -0.5, 0.109375)
    bucket_bias_table = bell_draw(streams_of[20], (BUCKETS, ATTENTION_HEADS), 0.5, 3.0, ((1, 4),))
    offset_bucket_map = with_ends(jax.random.randint(streams_of[21], (2 * LONG_LEN - 1,), 0, BUCKETS), jax.random.fold_in(streams_of[21], 1), 0, BUCKETS - 1).astype(jnp.int32)
    sequence_length_list = draw_sequence_length_list(jax.random.fold_in(streams_of[23], 71), 0)
    return {"tokens": tokens, "cotangent": cotangent, "attention_norm_gain": attention_norm_gain, "feedforward_norm_gain": feedforward_norm_gain, "query_projection_weight": query_projection_weight, "key_value_weight": key_value_weight, "attention_output_weight": attention_output_weight, "ffn_input_weight": ffn_input_weight, "ffn_output_weight": ffn_output_weight, "projection_down_weight": projection_down_weight, "query_up_weight": query_up_weight, "key_value_up_weight": key_value_up_weight, "attention_output_down_weight": attention_output_down_weight, "attention_output_up_weight": attention_output_up_weight, "ffn_input_down_weight": ffn_input_down_weight, "ffn_input_up_weight": ffn_input_up_weight, "ffn_output_down_weight": ffn_output_down_weight, "ffn_output_up_weight": ffn_output_up_weight, "attention_router_weight": attention_router_weight, "feedforward_router_weight": feedforward_router_weight, "bucket_bias_table": bucket_bias_table, "offset_bucket_map": offset_bucket_map, "sequence_length_list": sequence_length_list}


@jax.custom_vjp
def low(v):
    return lax.optimization_barrier(v.astype(jnp.bfloat16)).astype(jnp.float32)

@jax.custom_vjp
def low_back(v):
    return v

def low_keep(v):
    return (low(v), None)

def low_pass(kept, grad):
    return (grad,)

def back_keep(v):
    return (v, None)

def back_low(kept, grad):
    return (low(grad),)
low.defvjp(low_keep, low_pass)
low_back.defvjp(back_keep, back_low)
highest = lax.Precision.HIGHEST

def matrix_product(left_op, right_op):
    return jnp.dot(left_op, right_op, precision=highest)

def normed(values, gain_vec):
    return values * lax.rsqrt(lax.optimization_barrier(jnp.mean(values * values, -1, keepdims=True)) + 1e-06) * gain_vec

def adapter_delta(inputs, down_map, up_map, gate_probs):
    projected = low_back(matrix_product(inputs, down_map))
    mixed = low(jnp.repeat(gate_probs, ADAPTER_RANK, axis=1) * projected)
    return matrix_product(mixed, up_map)

def attend(query_matrix_rows, key_matrix_rows, value_matrix_rows, table, offset_bucket_map, lengths, seq_span):
    positions = jnp.arange(seq_span, dtype=jnp.int32)
    offsets = (positions[None, :] - positions[:, None] + (LONG_LEN - 1)).astype(jnp.int32)
    bucket_ids = jnp.take(offset_bucket_map.astype(jnp.int32), offsets.reshape(-1), axis=0).astype(jnp.int32)
    pos_bias = jnp.take(table, bucket_ids, axis=0).reshape(seq_span, seq_span, -1)
    scores = jnp.einsum('sqhd,skhd->shqk', query_matrix_rows, key_matrix_rows, precision=highest)
    scores = low_back(scores + jnp.transpose(pos_bias, (2, 0, 1))[None])
    key_valid = positions[None, :] < lengths.astype(jnp.int32)[:, None]
    masked_fill = jnp.full(scores.shape, -1000000000.0, scores.dtype)
    scores = jnp.where(key_valid[:, None, None, :], scores, masked_fill)
    weight_collection = low(jax.nn.softmax(scores, axis=-1))
    return jnp.einsum('shqk,skhd->sqhd', weight_collection, value_matrix_rows, precision=highest)

def device_layer(x_rows, parameter_tree, frozen, offset_bucket_map, lengths):
    attention_norm_gain, feedforward_norm_gain, projection_down_weight, query_up_weight, key_value_up_weight, attention_output_down_weight, attention_output_up_weight, ffn_input_down_weight, ffn_input_up_weight, ffn_output_down_weight, ffn_output_up_weight, attention_router_weight, feedforward_router_weight, bucket_bias_table = parameter_tree
    query_projection_weight, key_value_weight, attention_output_weight, ffn_input_weight, ffn_output_weight = frozen
    first_normalized = low(normed(x_rows, attention_norm_gain))
    first_gates = jax.nn.softmax(low_back(matrix_product(first_normalized, attention_router_weight)), axis=-1)
    query_matrix_rows = low(low_back(matrix_product(first_normalized, query_projection_weight) + adapter_delta(first_normalized, projection_down_weight[0], query_up_weight, first_gates)))
    key_matrix_rows = low(low_back(matrix_product(first_normalized, key_value_weight[0]) + adapter_delta(first_normalized, projection_down_weight[1], key_value_up_weight[0], first_gates)))
    value_matrix_rows = low(low_back(matrix_product(first_normalized, key_value_weight[1]) + adapter_delta(first_normalized, projection_down_weight[2], key_value_up_weight[1], first_gates)))
    short_rows = SHORT_SEQS * SHORT_LEN

    def split_heads(tensor, row_start, seq_count, seq_span):
        return tensor[row_start:row_start + seq_count * seq_span].reshape(seq_count, seq_span, ATTENTION_HEADS, HEAD_WIDTH)
    short_part = attend(split_heads(query_matrix_rows, 0, SHORT_SEQS, SHORT_LEN), split_heads(key_matrix_rows, 0, SHORT_SEQS, SHORT_LEN), split_heads(value_matrix_rows, 0, SHORT_SEQS, SHORT_LEN), bucket_bias_table, offset_bucket_map, lengths[:SHORT_SEQS], SHORT_LEN)
    long_part = attend(split_heads(query_matrix_rows, short_rows, LONG_SEQS, LONG_LEN), split_heads(key_matrix_rows, short_rows, LONG_SEQS, LONG_LEN), split_heads(value_matrix_rows, short_rows, LONG_SEQS, LONG_LEN), bucket_bias_table, offset_bucket_map, lengths[SHORT_SEQS:], LONG_LEN)
    attended_rows = jnp.concatenate([short_part.reshape(short_rows, ATTENTION_HEADS * HEAD_WIDTH), long_part.reshape(LONG_SEQS * LONG_LEN, ATTENTION_HEADS * HEAD_WIDTH)], 0)
    attended_rows = low(low_back(attended_rows))
    first_branch = low_back(matrix_product(attended_rows, attention_output_weight) + adapter_delta(attended_rows, attention_output_down_weight, attention_output_up_weight, first_gates))
    hidden_units_rows = x_rows + first_branch
    second_normalized = low(normed(hidden_units_rows, feedforward_norm_gain))
    second_gates = jax.nn.softmax(low_back(matrix_product(second_normalized, feedforward_router_weight)), axis=-1)
    before_residual = low_back(matrix_product(second_normalized, ffn_input_weight) + adapter_delta(second_normalized, ffn_input_down_weight, ffn_input_up_weight, second_gates))
    active_values = low(low_back(jax.nn.silu(before_residual)))
    second_branch = low_back(matrix_product(active_values, ffn_output_weight) + adapter_delta(active_values, ffn_output_down_weight, ffn_output_up_weight, second_gates))
    return hidden_units_rows + second_branch

def reference(tokens, cotangent, attention_norm_gain, feedforward_norm_gain, query_projection_weight, key_value_weight, attention_output_weight, ffn_input_weight, ffn_output_weight, projection_down_weight, query_up_weight, key_value_up_weight, attention_output_down_weight, attention_output_up_weight, ffn_input_down_weight, ffn_input_up_weight, ffn_output_down_weight, ffn_output_up_weight, attention_router_weight, feedforward_router_weight, bucket_bias_table, offset_bucket_map, sequence_length_list):
    frozen = tuple((weight_matrix.astype(jnp.float32) for weight_matrix in (query_projection_weight, key_value_weight, attention_output_weight, ffn_input_weight, ffn_output_weight)))
    trainable_weights = tuple((weight_matrix.astype(jnp.float32) for weight_matrix in (attention_norm_gain, feedforward_norm_gain, projection_down_weight, query_up_weight, key_value_up_weight, attention_output_down_weight, attention_output_up_weight, ffn_input_down_weight, ffn_input_up_weight, ffn_output_down_weight, ffn_output_up_weight, attention_router_weight, feedforward_router_weight, bucket_bias_table)))
    token_blocks = tokens.astype(jnp.float32).reshape(-1, TOK_DEV, MODEL_WIDTH)
    cot_blocks = cotangent.astype(jnp.float32).reshape(-1, TOK_DEV, MODEL_WIDTH)
    length_blocks = sequence_length_list.astype(jnp.int32).reshape(-1, SEQ_DEV)
    bucket_map = offset_bucket_map.astype(jnp.int32)

    def per_device(totals, inputs_dev):
        block_of_rows, cot_block, lengths = inputs_dev

        def layer_of(x_rows, *parameter_tree):
            return device_layer(x_rows, parameter_tree, frozen, bucket_map, lengths)
        result, pullback = jax.vjp(layer_of, block_of_rows, *trainable_weights)
        grads = pullback(cot_block)
        new_totals = tuple((left_op + right_op.astype(left_op.dtype) for left_op, right_op in zip(totals, grads[1:])))
        return (new_totals, (result.astype(jnp.bfloat16), grads[0].astype(jnp.bfloat16)))
    zero_totals = tuple((jnp.zeros(weight_matrix.shape, jnp.float32) for weight_matrix in trainable_weights))
    totals, (results, input_grads) = lax.scan(per_device, zero_totals, (token_blocks, cot_blocks, length_blocks))
    return (results.reshape(-1, MODEL_WIDTH), input_grads.reshape(-1, MODEL_WIDTH), totals[0], totals[1], totals[2], totals[3], totals[4], totals[5], totals[6], totals[7], totals[8], totals[9], totals[10], totals[11], totals[12], totals[13])
```

```python
import functools

import jax
import jax.numpy as jnp
import numpy as np
from jax import lax
from jax.experimental import pallas as pl
from jax.experimental.pallas import tpu as pltpu
from jax.sharding import PartitionSpec as P

HEAD_WIDTH = 64
BUCKETS = 32
ADAPTER_RANK = 4
SHORT_LEN = 128
LONG_LEN = 512
LONG_SEQS = 4
SHORT_SEQS = 16
MODEL_WIDTH = 768
LORA = 40
EXPERTS = 10
LANES = 128
HALF_ROWS = 512
ROWS = 1024
EPS = 1e-06
NEG = -1e9

bf16 = jnp.bfloat16
f32 = jnp.float32
VMEM_LIMIT = 56 * 1024 * 1024


def nn(a, b):
    return jnp.dot(a, b, preferred_element_type=f32)


def nt(a, b):
    return lax.dot_general(a, b, (((1,), (1,)), ((), ())), preferred_element_type=f32)


def tn(a, b):
    return lax.dot_general(a, b, (((0,), (0,)), ((), ())), preferred_element_type=f32)


def lane_index(shape):
    return lax.broadcasted_iota(jnp.int32, shape, 1)


def softmax_repeated(logits, valid, repeats):
    logits = jnp.where(lane_index(logits.shape) < valid, logits, -1e30)
    raised = jnp.exp(logits - jnp.max(logits, -1, keepdims=True))
    return raised * (repeats / jnp.sum(raised, -1, keepdims=True))


def logit_gradient(products, gates, group, pick):
    high = products.astype(bf16)
    low = (products - high.astype(f32)).astype(bf16)
    gate_grad = nn(high, group) + nn(low, group)
    inner = jnp.sum(gates * gate_grad, -1, keepdims=True) * (1.0 / ADAPTER_RANK)
    logit_grad = (gates * (gate_grad - inner)).astype(bf16)
    return nn(logit_grad, pick).astype(bf16)


PACK_ROWS = 864


def pack_kernel(q_ref, kv_ref, wo_ref, qup_ref, kvup_ref, table_ref, up_ref, pack_ref):
    pack_ref[0:192, :] = q_ref[...]
    pack_ref[192:384, :] = kv_ref[0]
    pack_ref[384:576, :] = kv_ref[1]
    pack_ref[576:768, :] = wo_ref[...]
    ups = jnp.concatenate([qup_ref[...], kvup_ref[0], kvup_ref[1], jnp.zeros((LORA, 192), bf16)], 1).astype(f32)
    table = jnp.pad(table_ref[...].astype(f32), ((0, 5), (0, MODEL_WIDTH - BUCKETS)))
    pack_ref[768:816, :] = jnp.concatenate([ups, table], 0).astype(bf16)
    pack_ref[816:864, :] = jnp.pad(up_ref[...].astype(f32), ((0, 8), (0, 0))).astype(bf16)


def pad_to(rows, count):
    if rows.shape[0] == count:
        return rows
    return jnp.concatenate([rows, jnp.zeros((count - rows.shape[0], rows.shape[1]), rows.dtype)], 0)


def repeated_router(router, copies):
    rows = lax.broadcasted_iota(jnp.int32, (LANES, EXPERTS), 0)
    first = ADAPTER_RANK * lax.broadcasted_iota(jnp.int32, (LANES, EXPERTS), 1)
    hot = jnp.zeros((LANES, EXPERTS), jnp.bool_)
    for c in range(copies):
        hot = hot | ((rows >= LORA * c + first) & (rows < LORA * c + first + ADAPTER_RANK))
    return nn(hot.astype(bf16), router).astype(bf16)


def down_rows(downs, router_rows):
    downs = pad_to(jnp.concatenate([part.astype(f32) for part in downs], 0), LANES)
    return jnp.concatenate([downs, pad_to(router_rows.astype(f32), LANES)], 0).astype(bf16)


def join_packs(one_ref, two_ref, ups_one, ups_two, joined_ref, ups_ref):
    ups = []
    for part in range(3):
        joined_ref[384 * part : 384 * part + 192, :] = one_ref[192 * part : 192 * part + 192, :]
        joined_ref[384 * part + 192 : 384 * part + 384, :] = two_ref[192 * part : 192 * part + 192, :]
        cols = slice(192 * part, 192 * part + 192)
        piece = jnp.concatenate([ups_one[:LORA, cols], ups_two[:LORA, cols]], 1).astype(f32)
        zero = jnp.zeros((LORA, 384), f32)
        ups.append(jnp.concatenate([piece if p == part else zero for p in range(3)], 1))
    ups_ref[...] = pad_to(jnp.concatenate(ups, 0), LANES).astype(bf16)


def project(normed, mixed, joined_ref, ups_ref, q_ref, k_ref, v_ref):
    result = nt(normed, joined_ref[...]) + nn(mixed, ups_ref[...])
    result = result.astype(bf16)
    q_ref[...] = result[:, :384]
    k_ref[...] = result[:, 384:768]
    v_ref[...] = result[:, 768:]


def first_kernel(
    place, x_ref, gain_ref, downs_in, router_ref, one_ref, ups_one, two_ref, ups_two,
    normed_ref, mixed_ref, spread_ref, downs_ref, q_ref, k_ref, v_ref, joined_ref, ups_ref, down_scr,
):
    @pl.when(pl.program_id(0) == 0)
    def _():
        join_packs(one_ref, two_ref, ups_one, ups_two, joined_ref, ups_ref)
        down_scr[...] = down_rows([downs_in[0], downs_in[1], downs_in[2]], repeated_router(router_ref[...], 3))

    x = x_ref[...].astype(f32)
    scale = lax.rsqrt(jnp.mean(x * x, -1, keepdims=True) + EPS)
    normed = (x * scale * gain_ref[...].astype(f32)).astype(bf16)
    normed_ref[...] = normed
    both = nt(normed, down_scr[...])
    downs = both[:, :LANES]
    spread = softmax_repeated(both[:, LANES:], 3 * LORA, 3.0 * ADAPTER_RANK)
    mixed = (spread * downs).astype(bf16)
    mixed_ref[...] = mixed
    spread_ref[...] = spread
    downs_ref[...] = downs
    project(normed, mixed, joined_ref, ups_ref, q_ref, k_ref, v_ref)


def second_kernel(
    normed_ref, mixed_ref, one_ref, ups_one, two_ref, ups_two, q_ref, k_ref, v_ref, joined_ref, ups_ref
):
    @pl.when(pl.program_id(0) == 0)
    def _():
        join_packs(one_ref, two_ref, ups_one, ups_two, joined_ref, ups_ref)

    project(normed_ref[...], mixed_ref[...], joined_ref, ups_ref, q_ref, k_ref, v_ref)


def split_pair(rows):
    lanes = lane_index(rows.shape)
    zero = jnp.zeros_like(rows)
    return jnp.concatenate([jnp.where(lanes < HEAD_WIDTH, rows, zero), jnp.where(lanes < HEAD_WIDTH, zero, rows)], 0)


def merge_pair(turned):
    return jnp.concatenate([turned[:HEAD_WIDTH, :LANES], turned[HEAD_WIDTH:, LANES:]], 0).T


def bucket_hot(map_ref):
    rows = lax.broadcasted_iota(jnp.int32, (BUCKETS, 2 * LONG_LEN), 0)
    return rows == map_ref[...]


def build_tiles(one_ref, two_ref, map_ref, tile_ref):
    pair = pl.program_id(0)
    hot = bucket_hot(map_ref).astype(bf16)
    table = jnp.concatenate(
        [one_ref[LORA : LORA + 8, :BUCKETS].astype(f32), two_ref[LORA : LORA + 8, :BUCKETS].astype(f32)], 0
    )
    by_offset = nn(table.astype(bf16), hot)
    heads = lax.broadcasted_iota(jnp.int32, (16, 1), 0)
    heads = jnp.where(heads < 8, heads, heads - 5)
    used = lax.broadcasted_iota(jnp.int32, (16, 1), 0)
    heads = jnp.where((used < 3) | ((used >= 8) & (used < 11)), heads, -1)
    rows_in = lax.broadcasted_iota(jnp.int32, (LANES, LANES), 0)
    lanes = lane_index((LANES, LANES))
    for t in range(2):
        row = jnp.sum(jnp.where(heads == 2 * pair + t, by_offset, 0.0), 0, keepdims=True)
        for d in range(7):
            block = 6 - d
            low = jnp.broadcast_to(row[:, LANES * block : LANES * block + LANES], (LANES, LANES))
            high = jnp.broadcast_to(row[:, LANES * block + LANES : LANES * block + 2 * LANES], (LANES, LANES))
            low = pltpu.roll(low, 1, 1, stride=1, stride_axis=0)
            high = pltpu.roll(high, 1, 1, stride=1, stride_axis=0)
            tile_ref[d, :, LANES * t : LANES * t + LANES] = jnp.where(lanes <= rows_in, low, high).astype(bf16)


def chunk_scores(keys, pair_queries, tiles, length):
    scores = nt(keys, pair_queries) + tiles
    positions = lax.broadcasted_iota(jnp.int32, scores.shape, 0)
    return jnp.where(positions < length, scores, NEG)


def chunk_layout():
    chunks = []
    for c in range(LONG_LEN // LANES):
        chunks.append((HALF_ROWS, LONG_LEN, HALF_ROWS + LANES * c, 3 - c, 4))
    for s in range(HALF_ROWS // SHORT_LEN):
        chunks.append((LANES * s, SHORT_LEN, LANES * s, 3, s))
    return chunks


def length_of(place, lengths, which):
    m = place[0]
    if which == 4:
        return lengths[SHORT_SEQS + m]
    return lengths[4 * m + which]


def tiles_of(tile_ref, first, span):
    return jnp.concatenate([tile_ref[first + b].astype(f32) for b in range(span // LANES)], 0)


def forward_attention(place, lengths, q_ref, k_ref, v_ref, one_ref, two_ref, map_ref, o_ref, lse_ref, tile_ref):
    tiles = tile_ref.at[0]
    build_tiles(one_ref, two_ref, map_ref, tiles)
    for number, (key_row, span, query_row, first, which) in enumerate(chunk_layout()):
        keys = k_ref[key_row : key_row + span, :]
        values_turned = v_ref[key_row : key_row + span, :].T
        queries = split_pair(q_ref[query_row : query_row + LANES, :])
        scores = chunk_scores(keys, queries, tiles_of(tiles, first, span), length_of(place, lengths, which))
        peak = jnp.max(scores, 0, keepdims=True)
        raised = jnp.exp(scores - peak)
        total = jnp.sum(raised, 0, keepdims=True)
        lse_ref[0, number : number + 1, :] = peak + jnp.log(total)
        weights = (raised * (1.0 / total)).astype(bf16)
        o_ref[query_row : query_row + LANES, :] = merge_pair(nn(values_turned, weights)).astype(bf16)


def backward_attention(
    place, lengths, q_ref, k_ref, v_ref, do_ref, lse_ref, tile_ref, map_ref, turn_ref,
    dq_ref, dk_ref, dv_ref, table_ref, weights_all, grads_all, queries_all, douts_all, diagonal,
):
    diagonal[...] = jnp.zeros_like(diagonal)
    turn = turn_ref[...]
    for number, (key_row, span, query_row, first, which) in enumerate(chunk_layout()):
        long = which == 4
        keys = k_ref[key_row : key_row + span, :]
        values = v_ref[key_row : key_row + span, :]
        queries = split_pair(q_ref[query_row : query_row + LANES, :])
        douts = split_pair(do_ref[query_row : query_row + LANES, :])
        scores = chunk_scores(keys, queries, tiles_of(tile_ref.at[0], first, span), length_of(place, lengths, which))
        probs = jnp.exp(scores - lse_ref[0, number : number + 1, :])
        weights = probs.astype(bf16)
        grad_probs = nt(values, douts)
        inner = jnp.sum(probs * grad_probs, 0, keepdims=True)
        grads = (probs * (grad_probs - inner)).astype(bf16)
        dq_ref[query_row : query_row + LANES, :] = merge_pair(nn(keys.T, grads)).astype(bf16)
        for b in range(span // LANES):
            diagonal[first + b] += nn(turn, grads[LANES * b : LANES * b + LANES, :])
        if long:
            at = 2 * LANES * number
            weights_all[:, at : at + 2 * LANES] = weights
            grads_all[:, at : at + 2 * LANES] = grads
            queries_all[at : at + 2 * LANES, :] = queries
            douts_all[at : at + 2 * LANES, :] = douts
        else:
            dv_ref[key_row : key_row + span, :] = nn(weights, douts).astype(bf16)
            dk_ref[key_row : key_row + span, :] = nn(grads, queries).astype(bf16)
    dv_ref[HALF_ROWS:, :] = nn(weights_all[...], douts_all[...]).astype(bf16)
    dk_ref[HALF_ROWS:, :] = nn(grads_all[...], queries_all[...]).astype(bf16)
    rows_in = lax.broadcasted_iota(jnp.int32, (LANES, LANES), 0)
    lanes = lane_index((LANES, LANES))
    hot = bucket_hot(map_ref).astype(f32)
    sums = []
    for t in range(2):
        pieces = [jnp.zeros((1, LANES), f32) for _ in range(8)]
        for d in range(7):
            block = 6 - d
            rolled = pltpu.roll(diagonal[d, :, LANES * t : LANES * t + LANES], 0, 1, stride=1, stride_axis=0)
            low = jnp.where(lanes >= rows_in, rolled, 0.0)
            pieces[block] = pieces[block] + jnp.sum(low, 0, keepdims=True)
            pieces[block + 1] = pieces[block + 1] + jnp.sum(rolled - low, 0, keepdims=True)
        sums.append(jnp.concatenate(pieces, 1))
    sums = jnp.concatenate(sums + [jnp.zeros((6, 2 * LONG_LEN), f32)], 0)
    table = lax.dot_general(
        sums, hot, (((1,), (1,)), ((), ())), precision=lax.Precision.HIGHEST, preferred_element_type=f32
    )
    table_ref[0] = jnp.concatenate([table, jnp.zeros((8, LANES - BUCKETS), f32)], 1)


def feedforward_shard(normed, cot, mixed, grad_down, win_ref, up, wout_ref, low):
    before = nn(normed, win_ref[...]) + nn(mixed, up)
    sig = jax.nn.sigmoid(before)
    active = (before * sig).astype(bf16)
    out = nn(active, wout_ref[...])
    down = nt(active, low)
    grad_active = (nt(cot, wout_ref[...]) + nn(grad_down, low)).astype(bf16).astype(f32)
    grad_before = (sig * (1.0 + before * (1.0 - sig)) * grad_active).astype(bf16)
    back = nt(grad_before, win_ref[...])
    side = nt(grad_before, up)
    grad_up = tn(mixed, grad_before)[:LORA]
    grad_low = tn(grad_down, active)[:LORA]
    return out, down, back, side, grad_up, grad_low


def fill_output_maps(place, ao_in, bo_in, wos, ao_scr, bo_scr, wo_scr):
    for j, wo in enumerate(wos):
        wo_scr[192 * j : 192 * j + 192, :] = wo[...]
    bo_scr[...] = pad_to(bo_in[...].astype(f32), LANES).astype(bf16)
    for at in range(4):

        @pl.when(place[0] == at)
        def _():
            pieces = [ao_in[:, 192 * (at ^ j) : 192 * (at ^ j) + 192] for j in range(4)]
            ao_scr[...] = pad_to(jnp.concatenate(pieces, 1).astype(f32), LANES).astype(bf16)


def fill_padded(scr, sources):
    for j, source in enumerate(sources):
        scr[j] = pad_to(source[:LORA, :].astype(f32), LANES).astype(bf16)


def middle_kernel(
    place, x_ref, cot_ref, aa_ref, ab_ref, wo0, wo1, wo2, wo3, ao_in, bo_in, spread1_ref, gain_ref,
    down_in, router_ref, bf_in, win0, up0, wout0, low0, win1, up1, wout1, low1,
    hidden_ref, normed_ref, spread_ref, gdown_ref, mixed_ref, downi_ref, sidef_ref, downo_ref, mixo_ref,
    out_ref, down_ref, back_ref, side_ref, shard_ref,
    ao_scr, bo_scr, wo_scr, down_scr, bf_scr, up_scr, low_scr,
):
    first = pl.program_id(0) == 0

    @pl.when(first)
    def _():
        fill_output_maps(place, ao_in, bo_in, (wo0, wo1, wo2, wo3), ao_scr, bo_scr, wo_scr)
        down_scr[...] = down_rows([down_in[...]], repeated_router(router_ref[...], 1))
        bf_scr[...] = pad_to(bf_in[...].astype(f32), LANES).astype(bf16)
        fill_padded(up_scr, (up0, up1))
        fill_padded(low_scr, (low0, low1))
        shard_ref[...] = jnp.zeros_like(shard_ref)

    attended = jnp.concatenate([aa_ref[...], ab_ref[...]], 1)
    downo = nt(attended, ao_scr[...])
    mixo = (spread1_ref[...] * downo).astype(bf16)
    hidden = x_ref[...].astype(f32) + (nn(attended, wo_scr[...]) + nn(mixo, bo_scr[...]))
    downo_ref[...] = downo
    mixo_ref[...] = mixo
    hidden_ref[...] = hidden
    scale = lax.rsqrt(jnp.mean(hidden * hidden, -1, keepdims=True) + EPS)
    normed = (hidden * scale * gain_ref[...].astype(f32)).astype(bf16)
    normed_ref[...] = normed
    both = nt(normed, down_scr[...])
    downi = both[:, :LANES]
    spread = softmax_repeated(both[:, LANES:], LORA, 1.0 * ADAPTER_RANK)
    mixed = (spread * downi).astype(bf16)
    cot = cot_ref[...]
    sidef = nt(cot, bf_scr[...])
    gdown = (spread * sidef).astype(bf16)
    spread_ref[...] = spread
    downi_ref[...] = downi
    mixed_ref[...] = mixed
    sidef_ref[...] = sidef
    gdown_ref[...] = gdown
    for j, (win, wout) in enumerate(((win0, wout0), (win1, wout1))):
        out, down, back, side, grad_up, grad_low = feedforward_shard(
            normed, cot, mixed, gdown, win, up_scr[j], wout, low_scr[j]
        )
        if j == 0:
            out_ref[...] = out
            down_ref[...] = down
            back_ref[...] = back
            side_ref[...] = side
        else:
            out_ref[...] += out
            down_ref[...] += down
            back_ref[...] += back
            side_ref[...] += side
        shard_ref[j, 0] += grad_up
        shard_ref[j, 1] += grad_low


def send_pieces(pieces, own_ref, sent_refs):
    own_ref[...] = pieces[0]
    for j, sent in enumerate(sent_refs):
        sent[...] = pieces[j + 1].astype(bf16)


def post_kernel(
    place, cot_ref, aa_ref, ab_ref, wo0, wo1, wo2, wo3, ao_in, bo_in, spread1_ref, gain_ref,
    down_in, router_ref, bf_in, win0, up0, wout0, low0, win1, up1, wout1, low1, group_ref, pick_ref,
    hidden_ref, normed_ref, spread_ref, gdown_ref, mixed_ref, downi_ref, sidef_ref, downo_ref, mixo_ref,
    out_ref, down_ref, back_ref, side_ref, shard_ref,
    result_ref, ghidden_ref, ga_ref, gb_ref, prod_ref, ao_grad, own_ref, sent1, sent2, sent3,
    ao_scr, bo_scr, wo_scr, down_scr, bf_scr, up_scr, low_scr,
    shard_acc, pair_acc, bff_acc, bo_acc, ao_acc, gain_acc, pieces,
):
    step = pl.program_id(0)

    @pl.when(step == 0)
    def _():
        fill_output_maps(place, ao_in, bo_in, (wo0, wo1, wo2, wo3), ao_scr, bo_scr, wo_scr)
        down_scr[...] = down_rows([down_in[...]], router_ref[...])
        bf_scr[...] = pad_to(bf_in[...].astype(f32), LANES).astype(bf16)
        fill_padded(up_scr, (up0, up1))
        fill_padded(low_scr, (low0, low1))
        shard_acc[...] = jnp.zeros_like(shard_acc)
        pair_acc[...] = jnp.zeros_like(pair_acc)
        bff_acc[...] = jnp.zeros_like(bff_acc)
        bo_acc[...] = jnp.zeros_like(bo_acc)
        ao_acc[...] = jnp.zeros_like(ao_acc)
        gain_acc[...] = jnp.zeros_like(gain_acc)

    normed, cot, mixed, gdown = normed_ref[...], cot_ref[...], mixed_ref[...], gdown_ref[...]
    total, downf, back, sidei = out_ref[...], down_ref[...], back_ref[...], side_ref[...]
    for j, (win, wout) in enumerate(((win0, wout0), (win1, wout1))):
        out, down, more, side, grad_up, grad_low = feedforward_shard(
            normed, cot, mixed, gdown, win, up_scr[j], wout, low_scr[j]
        )
        total = total + out
        downf = downf + down
        back = back + more
        sidei = sidei + side
        shard_acc[j, 0] += grad_up
        shard_acc[j, 1] += grad_low
    spread = spread_ref[...]
    hidden = hidden_ref[...]
    mixf = (spread * downf).astype(bf16)
    result_ref[...] = (hidden + (total + nn(mixf, bf_scr[...]))).astype(bf16)
    gdowni = (spread * sidei).astype(bf16)
    logit = logit_gradient(downf * sidef_ref[...] + downi_ref[...] * sidei, spread, group_ref[...], pick_ref[...])
    pair = jnp.concatenate([gdowni, logit], 1)
    grad_normed = back + nn(pair, down_scr[...])
    scale = lax.rsqrt(jnp.mean(hidden * hidden, -1, keepdims=True) + EPS)
    weighted = grad_normed * gain_ref[...].astype(f32)
    inner = jnp.mean(weighted * hidden, -1, keepdims=True)
    ghidden = cot.astype(f32) + scale * weighted - hidden * (scale * scale * scale * inner)
    ghidden_ref[...] = ghidden
    branch = ghidden.astype(bf16)
    attended = jnp.concatenate([aa_ref[...], ab_ref[...]], 1)
    sideo = nt(branch, bo_scr[...])
    gdowno = (spread1_ref[...] * sideo).astype(bf16)
    prod_ref[...] = downo_ref[...] * sideo
    gatt = (nt(branch, wo_scr[...]) + nn(gdowno, ao_scr[...])).astype(bf16)
    ga_ref[...] = gatt[:, :384]
    gb_ref[...] = gatt[:, 384:]
    pair_acc[...] += tn(pair, normed)
    bff_acc[...] += tn(mixf, cot)
    bo_acc[...] += tn(mixo_ref[...], branch)
    ao_acc[...] += tn(gdowno, attended)
    gain_acc[...] += jnp.sum(grad_normed * hidden * scale, 0, keepdims=True)

    @pl.when(step == pl.num_programs(0) - 1)
    def _():
        ao_grad[...] = ao_acc[:LORA]
        quarters = (pair_acc[:LORA], bff_acc[:LORA], bo_acc[:LORA], router_quarter(pair_acc, gain_acc))
        for j in range(4):
            source, at = (shard_ref, j) if j < 2 else (shard_acc, j - 2)
            pieces[j, 0:LORA] = source[at, 0]
            pieces[j, LORA : 2 * LORA] = source[at, 1]
            pieces[jnp.bitwise_xor(place[0], j), 2 * LORA : 3 * LORA] = quarters[j]
        send_pieces(pieces, own_ref, (sent1, sent2, sent3))


def router_quarter(pair_acc, gain_acc):
    gain = jnp.broadcast_to(gain_acc[...], (8, MODEL_WIDTH))
    return jnp.concatenate([pair_acc[LANES : LANES + 16, :], gain, jnp.zeros((16, MODEL_WIDTH), f32)], 0)


def last_kernel(
    place, x_ref, gain_ref, normed_ref, mixed_ref, spread_ref, downs_ref, prod_ref, ghidden_ref, downs_in, router_ref,
    dqa, dka, dva, dqb, dkb, dvb, joined_a, ups_a, joined_b, ups_b, group_ref, pick_ref, ta_ref, tb_ref, ao_grad,
    before_ref,
    gtokens_ref, own_ref, sent1, sent2, sent3, down_scr, pair_acc, up_acc, gain_acc, pieces,
):
    step = pl.program_id(0)

    @pl.when(step == 0)
    def _():
        down_scr[...] = down_rows([downs_in[0], downs_in[1], downs_in[2]], router_ref[...])
        pair_acc[...] = jnp.zeros_like(pair_acc)
        up_acc[...] = jnp.zeros_like(up_acc)
        gain_acc[...] = jnp.zeros_like(gain_acc)

    side_a = jnp.concatenate([dqa[...], dka[...], dva[...]], 1)
    side_b = jnp.concatenate([dqb[...], dkb[...], dvb[...]], 1)
    normed = normed_ref[...]
    mixed = mixed_ref[...]
    side = nt(side_a, ups_a[...]) + nt(side_b, ups_b[...])
    spread = spread_ref[...]
    gdown = (spread * side).astype(bf16)
    gates = jnp.where(lane_index(spread.shape) < LORA, spread, 0.0)
    logit = logit_gradient(downs_ref[...] * side + prod_ref[...], gates, group_ref[...], pick_ref[...])
    pair = jnp.concatenate([gdown, logit], 1)
    grad_normed = nn(side_a, joined_a[...]) + nn(side_b, joined_b[...]) + nn(pair, down_scr[...])
    x = x_ref[...].astype(f32)
    scale = lax.rsqrt(jnp.mean(x * x, -1, keepdims=True) + EPS)
    weighted = grad_normed * gain_ref[...].astype(f32)
    inner = jnp.mean(weighted * x, -1, keepdims=True)
    gtokens_ref[...] = (ghidden_ref[...] + scale * weighted - x * (scale * scale * scale * inner)).astype(bf16)
    pair_acc[...] += tn(pair, normed)
    up_acc[0] += tn(mixed, side_a)
    up_acc[1] += tn(mixed, side_b)
    gain_acc[...] += jnp.sum(grad_normed * x * scale, 0, keepdims=True)

    @pl.when(step == pl.num_programs(0) - 1)
    def _():
        quarters = (
            pair_acc[0:LORA],
            pair_acc[LORA : 2 * LORA],
            pair_acc[2 * LORA : 3 * LORA],
            router_quarter(pair_acc, gain_acc),
        )
        for j in range(4):
            half, odd = j // 2, j % 2
            parts = [ao_grad[:, 192 * j : 192 * j + 192]]
            for part in range(3):
                first = 384 * part + 192 * odd
                parts.append(up_acc[half, LORA * part : LORA * part + LORA, first : first + 192])
            pieces[j, 0:LORA] = jnp.concatenate(parts, 1)
            pieces[jnp.bitwise_xor(place[0], j), LORA : 2 * LORA] = quarters[j]
            table_ref = ta_ref if half == 0 else tb_ref
            rows = [table_ref[(3 * odd + i) // 2, (3 * odd + i) % 2 : (3 * odd + i) % 2 + 1, :] for i in range(3)]
            rows = jnp.concatenate(rows + [jnp.zeros((5, LANES), f32)], 0)
            pieces[j, 2 * LORA : 2 * LORA + 8] = jnp.concatenate([rows, jnp.zeros((8, MODEL_WIDTH - LANES), f32)], 1)
        send_pieces(pieces, own_ref, (sent1, sent2, sent3))


FF_ROWS, AT_ROWS, FLAT_ROWS = 120, 88, 1280
CHUNK = FLAT_ROWS // 8


def spread_kernel(place, own, one, two, three, out_ref):
    j = pl.program_id(0)
    for k, source in enumerate((own, one, two, three)):

        @pl.when(j == k)
        def _():
            out_ref[...] = source[...]


def scatter_kernel(spot, ff0, ff1, ff2, ff3, at0, at1, at2, at3, *refs):
    outs, flat = refs[:8], refs[8]
    ff = ff0[...] + ff1[...].astype(f32) + ff2[...].astype(f32) + ff3[...].astype(f32)
    at = at0[...] + at1[...].astype(f32) + at2[...].astype(f32) + at3[...].astype(f32)
    rows = FF_ROWS + AT_ROWS
    for t in range(6):
        flat[rows * t : rows * t + FF_ROWS, :] = ff[:, LANES * t : LANES * t + LANES]
        flat[rows * t + FF_ROWS : rows * t + rows, :] = at[:, LANES * t : LANES * t + LANES]
    flat[6 * rows :, :] = jnp.zeros((FLAT_ROWS - 6 * rows, LANES), f32)
    for k, out in enumerate(outs):
        first = pl.multiple_of(CHUNK * jnp.bitwise_xor(spot[0], k), CHUNK)
        out[...] = flat[pl.ds(first, CHUNK), :].astype(out.dtype)


def gather_kernel(spot, *refs):
    pieces, out = refs[:8], refs[8]
    for k, piece in enumerate(pieces):
        first = pl.multiple_of(CHUNK * jnp.bitwise_xor(spot[0], k), CHUNK)
        out[pl.ds(first, CHUNK), :] = piece[...]


def unpack_kernel(
    place, own, one, two, three, gain1_ref, gain2_ref, qkv_ref, bq_ref, bkv_ref, ao_ref, bo_ref, ai_ref, bi_ref,
    aff_ref, bff_ref, r1_ref, r2_ref, table_ref, quarters2, quarters1,
):
    rows = FF_ROWS + AT_ROWS

    def piece(ref, first, count):
        return jnp.concatenate([ref[rows * t + first : rows * t + first + count, :] for t in range(6)], 1).astype(f32)

    m = place[0]
    bi_ref[...] = piece(own, 0, LORA)
    mine = piece(own, FF_ROWS, LORA)
    bq_ref[...] = mine[:, 192:384]
    bkv_ref[0] = mine[:, 384:576]
    bkv_ref[1] = mine[:, 576:768]
    table_ref[...] = own[FF_ROWS + 2 * LORA : FF_ROWS + 2 * LORA + 8, :].astype(f32)[:3, :BUCKETS]
    for j, ref in enumerate((own, one, two, three)):
        there = jnp.bitwise_xor(m, j)
        quarters2[there] = piece(ref, 2 * LORA, LORA)
        quarters1[there] = piece(ref, FF_ROWS + LORA, LORA)
        low = piece(ref, LORA, LORA)
        out = piece(ref, FF_ROWS, LORA)[:, :192]
        for at in range(4):

            @pl.when(there == at)
            def _():
                aff_ref[:, MODEL_WIDTH * at : MODEL_WIDTH * at + MODEL_WIDTH] = low
                ao_ref[:, 192 * at : 192 * at + 192] = out

    for part in range(3):
        qkv_ref[part] = quarters1[part]
    ai_ref[...] = quarters2[0]
    bff_ref[...] = quarters2[1]
    bo_ref[...] = quarters2[2]
    r1_ref[...] = quarters1[3, :EXPERTS]
    r2_ref[...] = quarters2[3, :EXPERTS]
    gain1_ref[...] = quarters1[3, 16:17]
    gain2_ref[...] = quarters2[3, 16:17]


def whole(array):
    return pl.BlockSpec(array.shape, lambda *_: (0,) * array.ndim)


def rows_block(array):
    return pl.BlockSpec((HALF_ROWS, array.shape[1]), lambda i, *_: (i, 0))


def token_block():
    return pl.BlockSpec((HALF_ROWS, MODEL_WIDTH), lambda i, place, *_: (place[0] + 4 * i, 0))


def pair_block():
    return pl.BlockSpec((ROWS, LANES), lambda p, *_: (0, p))


def shape(dims, dtype):
    return jax.ShapeDtypeStruct(dims, dtype)


def call(kernel, grid, scalars, inputs, in_specs, outs, out_specs, scratch=(), flops=0, moved=0):
    return pl.pallas_call(
        kernel,
        grid_spec=pltpu.PrefetchScalarGridSpec(
            num_scalar_prefetch=len(scalars),
            grid=grid,
            in_specs=in_specs,
            out_specs=out_specs,
            scratch_shapes=list(scratch),
        ),
        out_shape=outs,
        compiler_params=pltpu.CompilerParams(vmem_limit_bytes=VMEM_LIMIT),
        cost_estimate=pl.CostEstimate(flops=flops, bytes_accessed=moved, transcendentals=0),
    )(*scalars, *inputs)


def exchange(value, axis, size, mask):
    return lax.ppermute(value, axis, [(i, i ^ mask) for i in range(size)])


def sum_over(value, axis, size, index, first_bit):
    def digits(v, low):
        if (1 << low) >= size:
            return v
        bits = min(3, size.bit_length() - 1 - low)
        count = 1 << bits
        digit = (index >> low) & (count - 1)
        parts = v.reshape(count, -1, v.shape[-1])
        mine = lax.dynamic_index_in_dim(parts, digit, 0, False)
        for k in range(1, count):
            piece = lax.dynamic_index_in_dim(parts, digit ^ k, 0, False)
            mine = mine + exchange(piece, axis, size, k << low)
        mine = digits(mine, low + bits)
        pieces = [mine] + [exchange(mine, axis, size, k << low) for k in range(1, count)]
        stacked = jnp.stack(pieces)
        order = digit ^ jnp.arange(count)
        return jnp.take(stacked, order, axis=0).reshape(v.shape)

    return digits(value, first_bit)


def constants():
    group1 = np.zeros((LANES, LANES), np.float32)
    for i in range(3 * LORA):
        for j in range(LORA):
            group1[i, j] = float((i % LORA) // ADAPTER_RANK == j // ADAPTER_RANK)
    pick = np.zeros((LANES, LANES), np.float32)
    for e in range(EXPERTS):
        pick[ADAPTER_RANK * e, e] = 1.0
    turn = np.eye(LANES, dtype=np.float32)[::-1].copy()
    return tuple(jnp.asarray(c, bf16) for c in (group1, pick, turn))


def local(
    dp_size,
    mp_size,
    tokens,
    cotangent,
    attention_norm_gain,
    feedforward_norm_gain,
    query_projection_weight,
    key_value_weight,
    attention_output_weight,
    ffn_input_weight,
    ffn_output_weight,
    projection_down_weight,
    query_up_weight,
    key_value_up_weight,
    attention_output_down_weight,
    attention_output_up_weight,
    ffn_input_down_weight,
    ffn_input_up_weight,
    ffn_output_down_weight,
    ffn_output_up_weight,
    attention_router_weight,
    feedforward_router_weight,
    bucket_bias_table,
    offset_bucket_map,
    sequence_length_list,
):
    m = lax.axis_index("mp").astype(jnp.int32)
    d = lax.axis_index("dp").astype(jnp.int32)
    place = m.reshape(1)
    spot = (d & 7).reshape(1)
    group, pick, turn = constants()

    def mp_swap(value, mask):
        return exchange(value, "mp", mp_size, mask)

    def pack_part(rows, index):
        return pl.BlockSpec((rows, MODEL_WIDTH), lambda *_: (index, 0))

    inputs = [
        query_projection_weight.T,
        jnp.transpose(key_value_weight, (0, 2, 1)),
        attention_output_weight,
        query_up_weight,
        key_value_up_weight,
        bucket_bias_table.T,
        ffn_input_up_weight,
    ]
    pack_shape = shape((PACK_ROWS, MODEL_WIDTH), bf16)
    pack0 = call(
        pack_kernel, (1,), [], inputs, [whole(a) for a in inputs], pack_shape, whole(pack_shape), moved=3_000_000
    )
    pack2 = mp_swap(pack0, 2)
    pack1 = mp_swap(pack0, 1)
    win0, wout0 = ffn_input_weight, ffn_output_weight
    win2, wout2 = mp_swap(win0, 2), mp_swap(wout0, 2)
    pack3 = mp_swap(pack2, 1)
    win1, wout1 = mp_swap(win0, 1), mp_swap(wout0, 1)
    win3, wout3 = mp_swap(win2, 1), mp_swap(wout2, 1)

    gain1 = attention_norm_gain.reshape(1, -1)
    gain2 = feedforward_norm_gain.reshape(1, -1)
    downs_in = jnp.transpose(projection_down_weight, (0, 2, 1))
    router1, router2 = attention_router_weight.T, feedforward_router_weight.T
    rev_map = jnp.concatenate([offset_bucket_map[::-1], jnp.full((1,), -1, jnp.int32)]).reshape(1, -1)

    wide, narrow = shape((ROWS, MODEL_WIDTH), bf16), shape((ROWS, LANES), f32)
    narrow16, half16 = shape((ROWS, LANES), bf16), shape((ROWS, 384), bf16)
    joined_shape, ups_shape = shape((1152, MODEL_WIDTH), bf16), shape((LANES, 1152), bf16)

    outs = [wide, narrow16, narrow, narrow, half16, half16, half16, joined_shape, ups_shape]
    normed1, mixed1, spread1, downs1, qa, ka, va, joined_a, ups_a = call(
        first_kernel,
        (2,),
        [place],
        [tokens, gain1, downs_in, router1, pack0, pack0, pack1, pack1],
        [token_block(), whole(gain1), whole(downs_in), whole(router1)] + [pack_part(576, 0), pack_part(48, 16)] * 2,
        outs,
        [rows_block(o) for o in outs[:-2]] + [whole(o) for o in outs[-2:]],
        scratch=[pltpu.VMEM((256, MODEL_WIDTH), bf16)],
        flops=2 * ROWS * 768 * 1536,
        moved=10_000_000,
    )

    def attend(q, k, v, one, two):
        return call(
            forward_attention,
            (3,),
            [place, sequence_length_list],
            [q, k, v, one, two, rev_map],
            [pair_block(), pair_block(), pair_block(), pack_part(48, 16), pack_part(48, 16), whole(rev_map)],
            [half16, shape((3, 8, 256), f32), shape((3, 7, LANES, 256), bf16)],
            [
                pair_block(),
                pl.BlockSpec((1, 8, 256), lambda p, *_: (p, 0, 0)),
                pl.BlockSpec((1, 7, LANES, 256), lambda p, *_: (p, 0, 0, 0)),
            ],
            flops=2 * 2 * 6 * 64 * (512 * 512 + 4 * 128 * 128) * 3,
            moved=6_000_000,
        )

    attended_a, lse_a, tiles_a = attend(qa, ka, va, pack0, pack1)
    outs = [half16, half16, half16, joined_shape, ups_shape]
    qb, kb, vb, joined_b, ups_b = call(
        second_kernel,
        (2,),
        [],
        [normed1, mixed1, pack2, pack2, pack3, pack3],
        [rows_block(normed1), rows_block(mixed1)] + [pack_part(576, 0), pack_part(48, 16)] * 2,
        outs,
        [rows_block(o) for o in outs[:-2]] + [whole(o) for o in outs[-2:]],
        flops=2 * ROWS * 768 * 1280,
        moved=8_000_000,
    )
    attended_b, lse_b, tiles_b = attend(qb, kb, vb, pack2, pack3)

    packs = [pack0, pack1, pack2, pack3]
    ao_in, bo_in, bf_in = attention_output_down_weight.T, attention_output_up_weight, ffn_output_up_weight
    down_in, low_in = ffn_input_down_weight.T, ffn_output_down_weight.T

    def low_block(j):
        return pl.BlockSpec((LORA, MODEL_WIDTH), lambda i, place, *_: (0, jnp.bitwise_xor(place[0], j)))

    def shard_inputs(first, wins, wouts):
        values, specs = [], []
        for j in range(2):
            values += [wins[j], packs[first + j], wouts[j], low_in]
            specs += [whole(wins[j]), pack_part(48, 17), whole(wouts[j]), low_block(first + j)]
        return values, specs

    shards_shape = shape((2, 2, LORA, MODEL_WIDTH), f32)
    wide_f32 = shape((ROWS, MODEL_WIDTH), f32)
    states = [wide_f32, wide, narrow, narrow16, narrow16, narrow, narrow, narrow, narrow16]
    states += [wide_f32, narrow, wide_f32, narrow]
    map_scratch = [
        pltpu.VMEM((LANES, MODEL_WIDTH), bf16),
        pltpu.VMEM((LANES, MODEL_WIDTH), bf16),
        pltpu.VMEM((MODEL_WIDTH, MODEL_WIDTH), bf16),
        pltpu.VMEM((256, MODEL_WIDTH), bf16),
        pltpu.VMEM((LANES, MODEL_WIDTH), bf16),
        pltpu.VMEM((2, LANES, MODEL_WIDTH), bf16),
        pltpu.VMEM((2, LANES, MODEL_WIDTH), bf16),
    ]
    maps = packs + [ao_in, bo_in, spread1, gain2, down_in, router2, bf_in]
    map_specs = [pack_part(192, 3)] * 4 + [whole(ao_in), whole(bo_in), rows_block(spread1), whole(gain2)]
    map_specs += [whole(down_in), whole(router2), whole(bf_in)]
    values, specs = shard_inputs(0, (win0, win1), (wout0, wout1))
    state = call(
        middle_kernel,
        (2,),
        [place],
        [tokens, cotangent, attended_a, attended_b] + maps + values,
        [token_block(), token_block(), rows_block(attended_a), rows_block(attended_b)] + map_specs + specs,
        states + [shards_shape],
        [rows_block(s) for s in states] + [whole(shards_shape)],
        scratch=map_scratch,
        flops=12_000_000_000,
        moved=30_000_000,
    )
    state, shard_grads = state[:-1], state[-1]

    values, specs = shard_inputs(2, (win2, win3), (wout2, wout3))
    ao_shape = shape((LORA, MODEL_WIDTH), f32)
    ff_shapes = [shape((FF_ROWS, MODEL_WIDTH), f32)] + [shape((FF_ROWS, MODEL_WIDTH), bf16)] * 3
    outs = [wide, wide_f32, half16, half16, narrow, ao_shape] + ff_shapes
    result, ghidden, ga, gb, prod, ao_grad, *ff_pieces = call(
        post_kernel,
        (2,),
        [place],
        [cotangent, attended_a, attended_b] + maps + values + [group, pick] + list(state) + [shard_grads],
        [token_block(), rows_block(attended_a), rows_block(attended_b)]
        + map_specs
        + specs
        + [whole(group), whole(pick)]
        + [rows_block(s) for s in state]
        + [whole(shard_grads)],
        outs,
        [rows_block(o) for o in outs[:5]] + [whole(o) for o in outs[5:]],
        scratch=map_scratch
        + [
            pltpu.VMEM((2, 2, LORA, MODEL_WIDTH), f32),
            pltpu.VMEM((256, MODEL_WIDTH), f32),
            pltpu.VMEM((LANES, MODEL_WIDTH), f32),
            pltpu.VMEM((LANES, MODEL_WIDTH), f32),
            pltpu.VMEM((LANES, MODEL_WIDTH), f32),
            pltpu.VMEM((1, MODEL_WIDTH), f32),
            pltpu.VMEM((4, FF_ROWS, MODEL_WIDTH), f32),
        ],
        flops=14_000_000_000,
        moved=40_000_000,
    )
    result2 = mp_swap(result, 2)
    ff_parts = [ff_pieces[0]] + [mp_swap(ff_pieces[j], j) for j in (1, 2, 3)]

    def attend_back(q, k, v, do, lse, tiles):
        return call(
            backward_attention,
            (3,),
            [place, sequence_length_list],
            [q, k, v, do, lse, tiles, rev_map, turn],
            [pair_block()] * 4
            + [
                pl.BlockSpec((1, 8, 256), lambda p, *_: (p, 0, 0)),
                pl.BlockSpec((1, 7, LANES, 256), lambda p, *_: (p, 0, 0, 0)),
                whole(rev_map),
                whole(turn),
            ],
            [half16, half16, half16, shape((3, 8, LANES), f32)],
            [pair_block()] * 3 + [pl.BlockSpec((1, 8, LANES), lambda p, *_: (p, 0, 0))],
            scratch=[
                pltpu.VMEM((LONG_LEN, 1024), bf16),
                pltpu.VMEM((LONG_LEN, 1024), bf16),
                pltpu.VMEM((1024, LANES), bf16),
                pltpu.VMEM((1024, LANES), bf16),
                pltpu.VMEM((7, LANES, 256), f32),
            ],
            flops=2 * 5 * 6 * 64 * (512 * 512 + 4 * 128 * 128) * 3,
            moved=8_000_000,
        )

    dqa, dka, dva, table_a = attend_back(qa, ka, va, ga, lse_a, tiles_a)
    dqb, dkb, dvb, table_b = attend_back(qb, kb, vb, gb, lse_b, tiles_b)

    rows_in = [normed1, mixed1, spread1, downs1, prod, ghidden]
    grads_in = [dqa, dka, dva, dqb, dkb, dvb]
    fixed = [joined_a, ups_a, joined_b, ups_b, group, pick, table_a, table_b, ao_grad]
    at_shapes = [shape((AT_ROWS, MODEL_WIDTH), f32)] + [shape((AT_ROWS, MODEL_WIDTH), bf16)] * 3
    gtokens, *at_pieces = call(
        last_kernel,
        (2,),
        [place],
        [tokens, gain1] + rows_in + [downs_in, router1] + grads_in + fixed + [result2],
        [token_block(), whole(gain1)]
        + [rows_block(a) for a in rows_in]
        + [whole(downs_in), whole(router1)]
        + [rows_block(a) for a in grads_in]
        + [whole(a) for a in fixed]
        + [pl.BlockSpec(memory_space=pl.ANY)],
        [wide] + at_shapes,
        [rows_block(wide)] + [whole(o) for o in at_shapes],
        scratch=[
            pltpu.VMEM((256, MODEL_WIDTH), bf16),
            pltpu.VMEM((256, MODEL_WIDTH), f32),
            pltpu.VMEM((2, LANES, 1152), f32),
            pltpu.VMEM((1, MODEL_WIDTH), f32),
            pltpu.VMEM((4, AT_ROWS, MODEL_WIDTH), f32),
        ],
        flops=6_000_000_000,
        moved=20_000_000,
    )
    gtokens2 = mp_swap(gtokens, 2)
    at_parts = [at_pieces[0]] + [mp_swap(at_pieces[j], j) for j in (1, 2, 3)]

    def spread_rows(own, two):
        one = mp_swap(own, 1)
        three = mp_swap(two, 1)

        def source(k):
            return pl.BlockSpec(
                (HALF_ROWS, MODEL_WIDTH), lambda j, part, *_: (jnp.where(j == k, part, jnp.where(j < k, 0, 1)), 0)
            )

        return call(
            spread_kernel,
            (4, 2),
            [place],
            [own, one, two, three],
            [source(k) for k in range(4)],
            shape((4 * ROWS, MODEL_WIDTH), bf16),
            pl.BlockSpec(
                (HALF_ROWS, MODEL_WIDTH), lambda j, part, place, *_: (4 * part + jnp.bitwise_xor(place[0], j), 0)
            ),
            moved=12_000_000,
        )

    output = spread_rows(result, result2)
    grad_tokens = spread_rows(gtokens, gtokens2)

    chunk, chunk16 = shape((CHUNK, LANES), f32), shape((CHUNK, LANES), bf16)
    flat_shape = shape((FLAT_ROWS, LANES), bf16)
    parts = ff_parts + at_parts
    mine, *others = call(
        scatter_kernel,
        (1,),
        [spot],
        parts,
        [whole(a) for a in parts],
        [chunk] + [chunk16] * 7,
        [whole(chunk)] * 8,
        scratch=[pltpu.VMEM((FLAT_ROWS, LANES), f32)],
        moved=3_000_000,
    )
    for k in range(1, 8):
        mine = mine + exchange(others[k - 1], "dp", dp_size, k).astype(f32)
    mine = sum_over(mine, "dp", dp_size, d, 3).astype(bf16)
    pieces = [mine] + [exchange(mine, "dp", dp_size, k) for k in range(1, 8)]
    own = call(
        gather_kernel, (1,), [spot], pieces, [whole(a) for a in pieces], flat_shape, whole(flat_shape), moved=700_000
    )
    two = mp_swap(own, 2)
    one = mp_swap(own, 1)
    three = mp_swap(two, 1)
    outs = [
        shape((1, MODEL_WIDTH), f32),
        shape((1, MODEL_WIDTH), f32),
        shape((3, LORA, MODEL_WIDTH), f32),
        shape((LORA, 192), f32),
        shape((2, LORA, 192), f32),
        shape((LORA, MODEL_WIDTH), f32),
        shape((LORA, MODEL_WIDTH), f32),
        shape((LORA, MODEL_WIDTH), f32),
        shape((LORA, MODEL_WIDTH), f32),
        shape((LORA, 4 * MODEL_WIDTH), f32),
        shape((LORA, MODEL_WIDTH), f32),
        shape((EXPERTS, MODEL_WIDTH), f32),
        shape((EXPERTS, MODEL_WIDTH), f32),
        shape((3, BUCKETS), f32),
    ]
    flats = [own, one, two, three]
    grads = call(
        unpack_kernel,
        (1,),
        [place],
        flats,
        [whole(a) for a in flats],
        outs,
        [whole(o) for o in outs],
        scratch=[pltpu.VMEM((4, LORA, MODEL_WIDTH), f32)] * 2,
        moved=3_000_000,
    )
    g1, g2, g_qkv, g_bq, g_bkv, g_ao, g_bo, g_ai, g_bi, g_aff, g_bff, g_r1, g_r2, g_table = grads
    return (
        output,
        grad_tokens,
        g1.reshape(-1),
        g2.reshape(-1),
        jnp.transpose(g_qkv, (0, 2, 1)),
        g_bq,
        g_bkv,
        g_ao.T,
        g_bo,
        g_ai.T,
        g_bi,
        g_aff.T,
        g_bff,
        g_r1.T,
        g_r2.T,
        g_table.T,
    )


def solution(mesh):
    in_specs = (
        P("dp", None),
        P("dp", None),
        P(),
        P(),
        P(None, "mp"),
        P(None, None, "mp"),
        P("mp", None),
        P(None, "mp"),
        P("mp", None),
        P(),
        P(None, "mp"),
        P(None, None, "mp"),
        P(),
        P(),
        P(),
        P(None, "mp"),
        P(),
        P(),
        P(),
        P(),
        P(None, "mp"),
        P(),
        P("dp"),
    )
    out_specs = (
        P("dp", None),
        P("dp", None),
        P(),
        P(),
        P(),
        P(None, "mp"),
        P(None, None, "mp"),
        P(),
        P(),
        P(),
        P(None, "mp"),
        P(),
        P(),
        P(),
        P(),
        P(None, "mp"),
    )
    step = functools.partial(local, mesh.shape["dp"], mesh.shape["mp"])
    return jax.shard_map(step, mesh=mesh, in_specs=in_specs, out_specs=out_specs, check_vma=False)
```

```python
import functools

import jax
import jax.numpy as jnp
import numpy as np
from jax import lax
from jax.experimental import pallas as pl
from jax.experimental.pallas import tpu as pltpu
from jax.sharding import PartitionSpec as P

HEAD_WIDTH = 64
BUCKETS = 32
ADAPTER_RANK = 4
SHORT_LEN = 128
LONG_LEN = 512
LONG_SEQS = 4
SHORT_SEQS = 16
MODEL_WIDTH = 768
LORA = 40
EXPERTS = 10
LANES = 128
HALF_ROWS = 512
ROWS = 1024
EPS = 1e-06
NEG = -1e9

bf16 = jnp.bfloat16
f32 = jnp.float32
VMEM_LIMIT = 56 * 1024 * 1024


def nn(a, b):
    return jnp.dot(a, b, preferred_element_type=f32)


def nt(a, b):
    return lax.dot_general(a, b, (((1,), (1,)), ((), ())), preferred_element_type=f32)


def tn(a, b):
    return lax.dot_general(a, b, (((0,), (0,)), ((), ())), preferred_element_type=f32)


def lane_index(shape):
    return lax.broadcasted_iota(jnp.int32, shape, 1)


def softmax_repeated(logits, valid, repeats):
    logits = jnp.where(lane_index(logits.shape) < valid, logits, -1e30)
    raised = jnp.exp(logits - jnp.max(logits, -1, keepdims=True))
    return raised * (repeats / jnp.sum(raised, -1, keepdims=True))


def logit_gradient(products, gates, group, pick):
    high = products.astype(bf16)
    low = (products - high.astype(f32)).astype(bf16)
    gate_grad = nn(high, group) + nn(low, group)
    inner = jnp.sum(gates * gate_grad, -1, keepdims=True) * (1.0 / ADAPTER_RANK)
    logit_grad = (gates * (gate_grad - inner)).astype(bf16)
    return nn(logit_grad, pick).astype(bf16)


FIRST_ROWS, SECOND_ROWS, HALF_SHARD = 624, 240, 384


def first_pack_kernel(q_ref, kv_ref, qup_ref, kvup_ref, table_ref, first_ref):
    first_ref[0:192, :] = q_ref[...]
    first_ref[192:384, :] = kv_ref[0]
    first_ref[384:576, :] = kv_ref[1]
    ups = jnp.concatenate([qup_ref[...], kvup_ref[0], kvup_ref[1], jnp.zeros((LORA, 192), bf16)], 1).astype(f32)
    table = jnp.pad(table_ref[...].astype(f32), ((0, 5), (0, MODEL_WIDTH - BUCKETS)))
    first_ref[576:624, :] = jnp.concatenate([ups, table], 0).astype(bf16)


def second_pack_kernel(half, first_ref, wo_ref, up_ref, win_ref, second_ref, both_ref):
    second_ref[0:192, :] = wo_ref[...]
    second_ref[192:240, :] = jnp.pad(up_ref[...].astype(f32), ((0, 8), (0, 0))).astype(bf16)
    second_ref[240:, :] = win_ref[...]
    both_ref[:SECOND_ROWS, :] = second_ref[:SECOND_ROWS, :]
    both_ref[SECOND_ROWS:, :] = first_ref[...]


def pad_to(rows, count):
    if rows.shape[0] == count:
        return rows
    return jnp.concatenate([rows, jnp.zeros((count - rows.shape[0], rows.shape[1]), rows.dtype)], 0)


def repeated_router(router, copies):
    rows = lax.broadcasted_iota(jnp.int32, (LANES, EXPERTS), 0)
    first = ADAPTER_RANK * lax.broadcasted_iota(jnp.int32, (LANES, EXPERTS), 1)
    hot = jnp.zeros((LANES, EXPERTS), jnp.bool_)
    for c in range(copies):
        hot = hot | ((rows >= LORA * c + first) & (rows < LORA * c + first + ADAPTER_RANK))
    return nn(hot.astype(bf16), router).astype(bf16)


def down_rows(downs, router_rows):
    downs = pad_to(jnp.concatenate([part.astype(f32) for part in downs], 0), LANES)
    return jnp.concatenate([downs, pad_to(router_rows.astype(f32), LANES)], 0).astype(bf16)


def join_packs(one_ref, two_ref, ups_one, ups_two, joined_scr, ups_scr):
    for part in range(3):
        at = LANES * part
        joined_scr[0, at : at + LANES, :] = one_ref[192 * part : 192 * part + LANES, :]
        joined_scr[1, at : at + 64, :] = one_ref[192 * part + LANES : 192 * part + 192, :]
        joined_scr[1, at + 64 : at + LANES, :] = two_ref[192 * part : 192 * part + 64, :]
        joined_scr[2, at : at + LANES, :] = two_ref[192 * part + 64 : 192 * part + 192, :]
    pieces = []
    for part in range(3):
        cols = slice(192 * part, 192 * part + 192)
        pieces.append(jnp.concatenate([ups_one[:LORA, cols], ups_two[:LORA, cols]], 1).astype(f32))
    zero = jnp.zeros((LORA, LANES), f32)
    for pair in range(3):
        rows = []
        for part in range(3):
            piece = pieces[part][:, LANES * pair : LANES * pair + LANES]
            rows.append(jnp.concatenate([piece if p == part else zero for p in range(3)], 1))
        ups_scr[pair] = pad_to(jnp.concatenate(rows, 0), LANES).astype(bf16)


def project_pair(normed_ref, mixed_ref, joined_scr, ups_scr, q_ref, k_ref, v_ref, joined_ref, ups_ref):
    pair = pl.program_id(0)
    joined, ups = joined_scr[pair], ups_scr[pair]
    joined_ref[0] = joined
    ups_ref[0] = ups
    for first in (0, HALF_ROWS):
        rows = slice(first, first + HALF_ROWS)
        result = (nt(normed_ref[rows, :], joined) + nn(mixed_ref[rows, :], ups)).astype(bf16)
        q_ref[rows, :] = result[:, :LANES]
        k_ref[rows, :] = result[:, LANES : 2 * LANES]
        v_ref[rows, :] = result[:, 2 * LANES :]


def first_kernel(
    place, lengths, xs_ref, xl_ref, gain_ref, downs_in, router_ref, one_ref, ups_one, two_ref, ups_two, map_ref,
    q_ref, k_ref, v_ref, o_ref, lse_ref, tile_ref, joined_ref, ups_ref, normed_ref, mixed_ref, spread_ref, downs_ref,
    joined_scr, ups_scr, down_scr,
):
    @pl.when(pl.program_id(0) == 0)
    def _():
        join_packs(one_ref, two_ref, ups_one, ups_two, joined_scr, ups_scr)
        down_scr[...] = down_rows([downs_in[0], downs_in[1], downs_in[2]], repeated_router(router_ref[...], 3))
        for x_ref, first in ((xs_ref, 0), (xl_ref, HALF_ROWS)):
            rows = slice(first, first + HALF_ROWS)
            x = x_ref[...].astype(f32)
            scale = lax.rsqrt(jnp.mean(x * x, -1, keepdims=True) + EPS)
            normed = (x * scale * gain_ref[...].astype(f32)).astype(bf16)
            normed_ref[rows, :] = normed
            both = nt(normed, down_scr[...])
            downs = both[:, :LANES]
            spread = softmax_repeated(both[:, LANES:], 3 * LORA, 3.0 * ADAPTER_RANK)
            mixed_ref[rows, :] = (spread * downs).astype(bf16)
            spread_ref[rows, :] = spread
            downs_ref[rows, :] = downs

    project_pair(normed_ref, mixed_ref, joined_scr, ups_scr, q_ref, k_ref, v_ref, joined_ref, ups_ref)
    forward_attention(place, lengths, q_ref, k_ref, v_ref, ups_one, ups_two, map_ref, o_ref, lse_ref, tile_ref)


def second_kernel(
    place, lengths, normed_ref, mixed_ref, one_ref, ups_one, two_ref, ups_two, map_ref,
    q_in, k_in, v_in, o_in, lse_in, tile_in, joined_in, ups_in,
    q_ref, k_ref, v_ref, o_ref, lse_ref, tile_ref, joined_ref, ups_ref, joined_scr, ups_scr,
):
    @pl.when(pl.program_id(0) == 0)
    def _():
        join_packs(one_ref, two_ref, ups_one, ups_two, joined_scr, ups_scr)

    project_pair(normed_ref, mixed_ref, joined_scr, ups_scr, q_ref, k_ref, v_ref, joined_ref, ups_ref)
    forward_attention(place, lengths, q_ref, k_ref, v_ref, ups_one, ups_two, map_ref, o_ref, lse_ref, tile_ref)


def split_pair(rows):
    lanes = lane_index(rows.shape)
    zero = jnp.zeros_like(rows)
    return jnp.concatenate([jnp.where(lanes < HEAD_WIDTH, rows, zero), jnp.where(lanes < HEAD_WIDTH, zero, rows)], 0)


def merge_pair(turned):
    return jnp.concatenate([turned[:HEAD_WIDTH, :LANES], turned[HEAD_WIDTH:, LANES:]], 0).T


def bucket_hot(map_ref):
    rows = lax.broadcasted_iota(jnp.int32, (BUCKETS, 2 * LONG_LEN), 0)
    return rows == map_ref[...]


def build_tiles(one_ref, two_ref, map_ref, tile_ref):
    pair = pl.program_id(0)
    hot = bucket_hot(map_ref).astype(bf16)
    table = jnp.concatenate(
        [one_ref[LORA : LORA + 8, :BUCKETS].astype(f32), two_ref[LORA : LORA + 8, :BUCKETS].astype(f32)], 0
    )
    by_offset = nn(table.astype(bf16), hot)
    heads = lax.broadcasted_iota(jnp.int32, (16, 1), 0)
    heads = jnp.where(heads < 8, heads, heads - 5)
    used = lax.broadcasted_iota(jnp.int32, (16, 1), 0)
    heads = jnp.where((used < 3) | ((used >= 8) & (used < 11)), heads, -1)
    rows_in = lax.broadcasted_iota(jnp.int32, (LANES, LANES), 0)
    lanes = lane_index((LANES, LANES))
    for t in range(2):
        row = jnp.sum(jnp.where(heads == 2 * pair + t, by_offset, 0.0), 0, keepdims=True)
        for d in range(7):
            block = 6 - d
            low = jnp.broadcast_to(row[:, LANES * block : LANES * block + LANES], (LANES, LANES))
            high = jnp.broadcast_to(row[:, LANES * block + LANES : LANES * block + 2 * LANES], (LANES, LANES))
            low = pltpu.roll(low, 1, 1, stride=1, stride_axis=0)
            high = pltpu.roll(high, 1, 1, stride=1, stride_axis=0)
            tile_ref[d, :, LANES * t : LANES * t + LANES] = jnp.where(lanes <= rows_in, low, high).astype(bf16)


def chunk_scores(keys, pair_queries, tiles, length):
    scores = nt(keys, pair_queries) + tiles
    positions = lax.broadcasted_iota(jnp.int32, scores.shape, 0)
    return jnp.where(positions < length, scores, NEG)


def chunk_layout():
    chunks = []
    for c in range(LONG_LEN // LANES):
        chunks.append((HALF_ROWS, LONG_LEN, HALF_ROWS + LANES * c, 3 - c, 4))
    for s in range(HALF_ROWS // SHORT_LEN):
        chunks.append((LANES * s, SHORT_LEN, LANES * s, 3, s))
    return chunks


def length_of(place, lengths, which):
    m = place[0]
    if which == 4:
        return lengths[SHORT_SEQS + m]
    return lengths[4 * m + which]


def tiles_of(tile_ref, first, span):
    return jnp.concatenate([tile_ref[first + b].astype(f32) for b in range(span // LANES)], 0)


def forward_attention(place, lengths, q_ref, k_ref, v_ref, one_ref, two_ref, map_ref, o_ref, lse_ref, tile_ref):
    tiles = tile_ref.at[0]
    build_tiles(one_ref, two_ref, map_ref, tiles)
    for number, (key_row, span, query_row, first, which) in enumerate(chunk_layout()):
        keys = k_ref[key_row : key_row + span, :]
        values_turned = v_ref[key_row : key_row + span, :].T
        queries = split_pair(q_ref[query_row : query_row + LANES, :])
        scores = chunk_scores(keys, queries, tiles_of(tiles, first, span), length_of(place, lengths, which))
        peak = jnp.max(scores, 0, keepdims=True)
        raised = jnp.exp(scores - peak)
        total = jnp.sum(raised, 0, keepdims=True)
        lse_ref[0, number : number + 1, :] = peak + jnp.log(total)
        weights = (raised * (1.0 / total)).astype(bf16)
        o_ref[query_row : query_row + LANES, :] = merge_pair(nn(values_turned, weights)).astype(bf16)


def backward_attention(
    place, lengths, q_ref, k_ref, v_ref, do_ref, lse_ref, tile_ref, map_ref, turn_ref,
    dq_ref, dk_ref, dv_ref, table_ref, weights_all, grads_all, queries_all, douts_all, diagonal,
):
    diagonal[...] = jnp.zeros_like(diagonal)
    turn = turn_ref[...]
    for number, (key_row, span, query_row, first, which) in enumerate(chunk_layout()):
        long = which == 4
        keys = k_ref[key_row : key_row + span, :]
        values = v_ref[key_row : key_row + span, :]
        queries = split_pair(q_ref[query_row : query_row + LANES, :])
        douts = split_pair(do_ref[query_row : query_row + LANES, :])
        scores = chunk_scores(keys, queries, tiles_of(tile_ref.at[0], first, span), length_of(place, lengths, which))
        probs = jnp.exp(scores - lse_ref[0, number : number + 1, :])
        weights = probs.astype(bf16)
        grad_probs = nt(values, douts)
        inner = jnp.sum(probs * grad_probs, 0, keepdims=True)
        grads = (probs * (grad_probs - inner)).astype(bf16)
        dq_ref[query_row : query_row + LANES, :] = merge_pair(nn(keys.T, grads)).astype(bf16)
        for b in range(span // LANES):
            diagonal[first + b] += nn(turn, grads[LANES * b : LANES * b + LANES, :])
        if long:
            at = 2 * LANES * number
            weights_all[:, at : at + 2 * LANES] = weights
            grads_all[:, at : at + 2 * LANES] = grads
            queries_all[at : at + 2 * LANES, :] = queries
            douts_all[at : at + 2 * LANES, :] = douts
        else:
            dv_ref[key_row : key_row + span, :] = nn(weights, douts).astype(bf16)
            dk_ref[key_row : key_row + span, :] = nn(grads, queries).astype(bf16)
    dv_ref[HALF_ROWS:, :] = nn(weights_all[...], douts_all[...]).astype(bf16)
    dk_ref[HALF_ROWS:, :] = nn(grads_all[...], queries_all[...]).astype(bf16)
    rows_in = lax.broadcasted_iota(jnp.int32, (LANES, LANES), 0)
    lanes = lane_index((LANES, LANES))
    hot = bucket_hot(map_ref).astype(f32)
    sums = []
    for t in range(2):
        pieces = [jnp.zeros((1, LANES), f32) for _ in range(8)]
        for d in range(7):
            block = 6 - d
            rolled = pltpu.roll(diagonal[d, :, LANES * t : LANES * t + LANES], 0, 1, stride=1, stride_axis=0)
            low = jnp.where(lanes >= rows_in, rolled, 0.0)
            pieces[block] = pieces[block] + jnp.sum(low, 0, keepdims=True)
            pieces[block + 1] = pieces[block + 1] + jnp.sum(rolled - low, 0, keepdims=True)
        sums.append(jnp.concatenate(pieces, 1))
    sums = jnp.concatenate(sums + [jnp.zeros((6, 2 * LONG_LEN), f32)], 0)
    table = lax.dot_general(
        sums, hot, (((1,), (1,)), ((), ())), precision=lax.Precision.HIGHEST, preferred_element_type=f32
    )
    table_ref[...] = jnp.concatenate([table, jnp.zeros((8, LANES - BUCKETS), f32)], 1)


WIDER = MODEL_WIDTH + LANES


def feedforward_shard(inputs, douts, win_scr, wout_scr):
    before = nn(inputs, win_scr[...])
    sig = 0.5 * jnp.tanh(0.5 * before) + 0.5
    active = (before * sig).astype(bf16)
    out = nn(active, wout_scr[...])
    grad_active = nt(douts, wout_scr[...]).astype(bf16).astype(f32)
    grad_before = (sig * (1.0 + before * (1.0 - sig)) * grad_active).astype(bf16)
    back = nt(grad_before, win_scr[...])
    grad_up = tn(inputs[:, MODEL_WIDTH:], grad_before)[:LORA]
    grad_low = tn(douts[:, MODEL_WIDTH:], active)[:LORA]
    return out, back, grad_up, grad_low


def fill_adapters(win_scr, wout_scr, up, low):
    win_scr[MODEL_WIDTH:, :] = pad_to(up[:LORA, :].astype(f32), LANES).astype(bf16)
    wout_scr[:, MODEL_WIDTH:] = pad_to(low[...].astype(f32), LANES).T.astype(bf16)


def shard_copies(wins, wouts, half, win_scr, wout_scr, sems, first):
    pieces = []
    if len(wins) == 1:
        pieces.append((wins[0], win_scr.at[pl.ds(0, MODEL_WIDTH)]))
    else:
        rows = MODEL_WIDTH // 2
        for k in range(2):
            there = pl.ds(pl.multiple_of(rows * jnp.bitwise_xor(half, k), rows), rows)
            pieces.append((wins[k].at[pl.ds(SECOND_ROWS, rows)], win_scr.at[there]))
    pieces.append((wouts[0], wout_scr.at[:, pl.ds(0, MODEL_WIDTH)]))
    return [pltpu.make_async_copy(source, goal, sems.at[first + i]) for i, (source, goal) in enumerate(pieces)]


def fill_output_maps(place, ao_in, bo_in, ao_scr, bo_scr):
    bo_scr[...] = pad_to(bo_in[...].astype(f32), LANES).astype(bf16)
    for at in range(4):

        @pl.when(place[0] == at)
        def _():
            pieces = [ao_in[:, 192 * (at ^ j) : 192 * (at ^ j) + 192] for j in range(4)]
            ao_scr[...] = pad_to(jnp.concatenate(pieces, 1).astype(f32), LANES).astype(bf16)


def start(copies):
    for copy in copies:
        copy.start()


def wait(copies):
    for copy in copies:
        copy.wait()


def both_blocks():
    return [slice(HALF_ROWS * i, HALF_ROWS * i + HALF_ROWS) for i in range(2)]


def middle_kernel(
    place, x_ref, cot_ref, att_ref, wo0, wo1, wo2, wo3, spread1_ref, win0, wout0, win1, wout1,
    ao_in, bo_in, gain_ref, down_in, router_ref, bf_in, up0, low0, up1, low1,
    hidden, inputs_ref, douts_ref, narrow, out_ref, back_ref, shard_ref,
    ao_scr, bo_scr, wo_scr, down_scr, bf_scr, win_scr, wout_scr,
):
    @pl.when(pl.program_id(0) == 0)
    def _():
        fill_output_maps(place, ao_in, bo_in, ao_scr, bo_scr)
        for j, wo in enumerate((wo0, wo1, wo2, wo3)):
            wo_scr[192 * j : 192 * j + 192, :] = wo[...]
        down_scr[...] = down_rows([down_in[...]], repeated_router(router_ref[...], 1))
        bf_scr[...] = pad_to(bf_in[...].astype(f32), LANES).astype(bf16)
        for j, (win, wout, up, low) in enumerate(((win0, wout0, up0, low0), (win1, wout1, up1, low1))):
            win_scr[j, :MODEL_WIDTH, :] = win[...]
            wout_scr[j, :, :MODEL_WIDTH] = wout[...]
            fill_adapters(win_scr.at[j], wout_scr.at[j], up, low)
        shard_ref[...] = jnp.zeros_like(shard_ref)

    attended = att_ref[...]
    downo = nt(attended, ao_scr[...])
    mixo = (spread1_ref[...] * downo).astype(bf16)
    held = x_ref[...].astype(f32) + (nn(attended, wo_scr[...]) + nn(mixo, bo_scr[...]))
    hidden[...] = held
    scale = lax.rsqrt(jnp.mean(held * held, -1, keepdims=True) + EPS)
    normed = (held * scale * gain_ref[...].astype(f32)).astype(bf16)
    both = nt(normed, down_scr[...])
    downi = both[:, :LANES]
    spread = softmax_repeated(both[:, LANES:], LORA, 1.0 * ADAPTER_RANK)
    cot = cot_ref[...]
    sidef = nt(cot, bf_scr[...])
    inputs = jnp.concatenate([normed, (spread * downi).astype(bf16)], 1)
    douts = jnp.concatenate([cot, (spread * sidef).astype(bf16)], 1)
    inputs_ref[...] = inputs
    douts_ref[...] = douts
    narrow[:, :LANES] = spread
    narrow[:, LANES : 2 * LANES] = downi
    narrow[:, 2 * LANES : 3 * LANES] = sidef
    narrow[:, 3 * LANES :] = downo
    for j in range(2):
        out, back, grad_up, grad_low = feedforward_shard(inputs, douts, win_scr.at[j], wout_scr.at[j])
        if j == 0:
            out_ref[...] = out
            back_ref[...] = back
        else:
            out_ref[...] += out
            back_ref[...] += back
        shard_ref[j, 0] += grad_up
        shard_ref[j, 1] += grad_low


def send_pieces(pieces, own_ref, sent_refs):
    own_ref[...] = pieces[0]
    for j, sent in enumerate(sent_refs):
        sent[...] = pieces[j + 1].astype(bf16)


def post_kernel(
    place, half, att, wo0, wo1, wo2, wo3, spread1, win0, win1, wout0, win2, win3, wout1,
    hidden_in, inputs_in, douts_in, narrow_in, out_in, back_in,
    ao_in, bo_in, gain_ref, down_in, router_ref, bf_in, up0, low0, up1, low1, group_ref, pick_ref, shard_ref,
    result_out, ghidden_out, gatt_out, prod_out, ao_grad, own_ref, sent1, sent2, sent3,
    att_scr, spread1_scr, hidden, inputs, douts, narrow, out, back, result, gatt, prod,
    ao_scr, bo_scr, wo_scr, down_scr, bf_scr, win_scr, wout_scr,
    shard_acc, pair_acc, bff_acc, bo_acc, ao_acc, gain_acc, pieces, arrived, left,
):
    def copies(pairs, at):
        return [pltpu.make_async_copy(source, goal, arrived.at[at + i]) for i, (source, goal) in enumerate(pairs)]

    early = copies([(inputs_in, inputs), (douts_in, douts)], 0)
    first = shard_copies((win0, win1), (wout0,), half[0], win_scr.at[0], wout_scr.at[0], arrived, 2)
    second = shard_copies((win2, win3), (wout1,), half[0], win_scr.at[1], wout_scr.at[1], arrived, 5)
    sums = copies([(out_in, out), (back_in, back)], 8)
    rest = [(hidden_in, hidden), (narrow_in, narrow), (att, att_scr), (spread1, spread1_scr)]
    rest += [(wo.at[pl.ds(0, 192)], wo_scr.at[pl.ds(192 * j, 192)]) for j, wo in enumerate((wo0, wo1, wo2, wo3))]
    rest = copies(rest, 10)
    start(early + first + sums + second + rest)
    fill_output_maps(place, ao_in, bo_in, ao_scr, bo_scr)
    down_scr[...] = down_rows([down_in[...]], router_ref[...])
    bf_scr[...] = pad_to(bf_in[...].astype(f32), LANES).astype(bf16)
    fill_adapters(win_scr.at[0], wout_scr.at[0], up0, low0)
    fill_adapters(win_scr.at[1], wout_scr.at[1], up1, low1)
    for j, weights in enumerate((first, second)):
        wait(weights)
        if j == 0:
            wait(early)
        more_out, more_back, grad_up, grad_low = feedforward_shard(
            inputs[...], douts[...], win_scr.at[j], wout_scr.at[j]
        )
        if j == 0:
            wait(sums)
        out[...] += more_out
        back[...] += more_back
        shard_acc[j, 0] = grad_up
        shard_acc[j, 1] = grad_low
    wait(rest)
    leaving = []

    def send(scr, goal, where):
        leaving.append(pltpu.make_async_copy(scr.at[where], goal.at[where], left.at[len(leaving)]))
        leaving[-1].start()

    def gather(scr, value, fresh):
        if fresh:
            scr[...] = value
        else:
            scr[...] += value

    for i, rows in enumerate(both_blocks()):
        normed, cot = inputs[rows, :MODEL_WIDTH], douts[rows, :MODEL_WIDTH]
        downf, sidei = out[rows, MODEL_WIDTH:], back[rows, MODEL_WIDTH:]
        spread, downi = narrow[rows, :LANES], narrow[rows, LANES : 2 * LANES]
        sidef, downo = narrow[rows, 2 * LANES : 3 * LANES], narrow[rows, 3 * LANES :]
        held = hidden[rows, :]
        mixf = (spread * downf).astype(bf16)
        result[rows, :] = (held + (out[rows, :MODEL_WIDTH] + nn(mixf, bf_scr[...]))).astype(bf16)
        gdowni = (spread * sidei).astype(bf16)
        logit = logit_gradient(downf * sidef + downi * sidei, spread, group_ref[...], pick_ref[...])
        pair = jnp.concatenate([gdowni, logit], 1)
        grad_normed = back[rows, :MODEL_WIDTH] + nn(pair, down_scr[...])
        scale = lax.rsqrt(jnp.mean(held * held, -1, keepdims=True) + EPS)
        weighted = grad_normed * gain_ref[...].astype(f32)
        inner = jnp.mean(weighted * held, -1, keepdims=True)
        ghidden = cot.astype(f32) + scale * weighted - held * (scale * scale * scale * inner)
        branch = ghidden.astype(bf16)
        sideo = nt(branch, bo_scr[...])
        gates = spread1_scr[rows, :]
        gdowno = (gates * sideo).astype(bf16)
        prod[rows, :] = downo * sideo
        gatt[rows, :] = (nt(branch, wo_scr[...]) + nn(gdowno, ao_scr[...])).astype(bf16)
        gather(pair_acc, tn(pair, normed), i == 0)
        gather(bff_acc, tn(mixf, cot), i == 0)
        gather(bo_acc, tn((gates * downo).astype(bf16), branch), i == 0)
        gather(ao_acc, tn(gdowno, att_scr[rows, :]), i == 0)
        gather(gain_acc, jnp.sum(grad_normed * held * scale, 0, keepdims=True), i == 0)
        hidden[rows, :] = ghidden
        where = pl.ds(HALF_ROWS * i, HALF_ROWS)
        send(result, result_out, where)
        send(hidden, ghidden_out, where)
        send(gatt, gatt_out, where)
        send(prod, prod_out, where)
    ao_grad[...] = ao_acc[:LORA]
    quarters = (pair_acc[:LORA], bff_acc[:LORA], bo_acc[:LORA], router_quarter(pair_acc, gain_acc))
    for j in range(4):
        source, at = (shard_ref, j) if j < 2 else (shard_acc, j - 2)
        pieces[j, 0:LORA] = source[at, 0]
        pieces[j, LORA : 2 * LORA] = source[at, 1]
        pieces[jnp.bitwise_xor(place[0], j), 2 * LORA : 3 * LORA] = quarters[j]
    send_pieces(pieces, own_ref, (sent1, sent2, sent3))
    wait(leaving)


def router_quarter(pair_acc, gain_acc):
    gain = jnp.broadcast_to(gain_acc[...], (8, MODEL_WIDTH))
    return jnp.concatenate([pair_acc[LANES : LANES + 16, :], gain, jnp.zeros((16, MODEL_WIDTH), f32)], 0)


def back_kernel(
    place, lengths, q_ref, k_ref, v_ref, do_ref, lse_ref, tile_ref, map_ref, turn_ref, joined_ref, ups_ref,
    normed_ref, mixed_ref, spread_ref, downs_ref, prod_ref, downs_in, router_ref, group_ref, pick_ref, ao_grad,
    gnormed_ref, own_ref, sent1, sent2, sent3,
    weights_all, grads_all, queries_all, douts_all, diagonal, dq_scr, dk_scr, dv_scr, table_scr,
    side_scr, up_scr, down_scr, pair_acc, pieces,
):
    pair = pl.program_id(0)
    backward_attention(
        place, lengths, q_ref, k_ref, v_ref, do_ref, lse_ref, tile_ref, map_ref, turn_ref,
        dq_scr, dk_scr, dv_scr, table_scr.at[pair], weights_all, grads_all, queries_all, douts_all, diagonal,
    )
    sides = jnp.concatenate([dq_scr[...], dk_scr[...], dv_scr[...]], 1)
    up_scr[pair] = tn(mixed_ref[...], sides)

    @pl.when(pair == 0)
    def _():
        gnormed_ref[...] = nn(sides, joined_ref[0])
        side_scr[...] = nt(sides, ups_ref[0])

    @pl.when(pair > 0)
    def _():
        gnormed_ref[...] += nn(sides, joined_ref[0])
        side_scr[...] += nt(sides, ups_ref[0])

    @pl.when(pair == pl.num_programs(0) - 1)
    def _():
        down_scr[...] = down_rows([downs_in[0], downs_in[1], downs_in[2]], router_ref[...])
        side = side_scr[...]
        spread = spread_ref[...]
        gdown = (spread * side).astype(bf16)
        gates = jnp.where(lane_index(spread.shape) < LORA, spread, 0.0)
        logit = logit_gradient(downs_ref[...] * side + prod_ref[...], gates, group_ref[...], pick_ref[...])
        both = jnp.concatenate([gdown, logit], 1)
        gnormed_ref[...] += nn(both, down_scr[...])
        pair_acc[...] = tn(both, normed_ref[...])
        quarters = (
            pair_acc[0:LORA],
            pair_acc[LORA : 2 * LORA],
            pair_acc[2 * LORA : 3 * LORA],
            jnp.concatenate([pair_acc[LANES : LANES + 16, :], jnp.zeros((24, MODEL_WIDTH), f32)], 0),
        )
        ups = [
            [
                jnp.concatenate(
                    [up_scr[3 * half + p, LORA * part : LORA * part + LORA, LANES * part : LANES * part + LANES] for p in range(3)], 1
                )
                for part in range(3)
            ]
            for half in range(2)
        ]
        for j in range(4):
            half, odd = j // 2, j % 2
            parts = [ao_grad[:, 192 * j : 192 * j + 192]]
            parts += [ups[half][part][:, 192 * odd : 192 * odd + 192] for part in range(3)]
            pieces[j, 0:LORA] = jnp.concatenate(parts, 1)
            pieces[jnp.bitwise_xor(place[0], j), LORA : 2 * LORA] = quarters[j]
            heads = [3 * j + i for i in range(3)]
            rows = [table_scr[head // 2, head % 2 : head % 2 + 1, :] for head in heads]
            rows = jnp.concatenate(rows + [jnp.zeros((5, LANES), f32)], 0)
            pieces[j, 2 * LORA : 2 * LORA + 8] = jnp.concatenate([rows, jnp.zeros((8, MODEL_WIDTH - LANES), f32)], 1)
        send_pieces(pieces, own_ref, (sent1, sent2, sent3))


def last_kernel(place, x_ref, gain_ref, gnormed_ref, ghidden_ref, gtokens_ref, ggain_ref):
    grad_normed = gnormed_ref[...]
    x = x_ref[...].astype(f32)
    scale = lax.rsqrt(jnp.mean(x * x, -1, keepdims=True) + EPS)
    weighted = grad_normed * gain_ref[...].astype(f32)
    inner = jnp.mean(weighted * x, -1, keepdims=True)
    gtokens_ref[...] = (ghidden_ref[...] + scale * weighted - x * (scale * scale * scale * inner)).astype(bf16)

    @pl.when(pl.program_id(0) == 0)
    def _():
        ggain_ref[...] = jnp.zeros_like(ggain_ref)

    ggain_ref[...] += jnp.sum(grad_normed * x * scale, 0, keepdims=True)


FF_ROWS, AT_ROWS, FLAT_ROWS = 120, 88, 1280


def spread_kernel(place, own, one, two, three, out_ref, held, arrived, left):
    inward, outward = [], []
    for j, source in enumerate((own, one, two, three)):
        there = jnp.bitwise_xor(place[0], j)
        for part in range(2):
            rows = pl.ds(HALF_ROWS * part, HALF_ROWS)
            goal = pl.ds(pl.multiple_of(HALF_ROWS * (4 * part + there), HALF_ROWS), HALF_ROWS)
            inward.append(pltpu.make_async_copy(source.at[rows], held.at[j, rows], arrived.at[j, part]))
            outward.append(pltpu.make_async_copy(held.at[j, rows], out_ref.at[goal], left.at[j, part]))
    for copy in inward:
        copy.start()
    for copy, onward in zip(inward, outward):
        copy.wait()
        onward.start()
    for copy in outward:
        copy.wait()


def scatter_kernel(spot, ff0, ff1, ff2, ff3, at0, at1, at2, at3, ggain, keep_ref, send_ref, flat):
    ff = ff0[...] + ff1[...].astype(f32) + ff2[...].astype(f32) + ff3[...].astype(f32)
    at = at0[...] + at1[...].astype(f32) + at2[...].astype(f32) + at3[...].astype(f32)
    rows = FF_ROWS + AT_ROWS
    for t in range(6):
        flat[rows * t : rows * t + FF_ROWS, :] = ff[:, LANES * t : LANES * t + LANES]
        flat[rows * t + FF_ROWS : rows * t + rows, :] = at[:, LANES * t : LANES * t + LANES]
    flat[6 * rows :, :] = jnp.zeros((FLAT_ROWS - 6 * rows, LANES), f32)
    for t in range(6):
        flat[6 * rows + t : 6 * rows + t + 1, :] = ggain[:, LANES * t : LANES * t + LANES]
    half = FLAT_ROWS // 2
    keep_ref[...] = flat[pl.ds(pl.multiple_of(half * spot[0], half), half), :]
    send_ref[...] = flat[pl.ds(pl.multiple_of(half * (1 - spot[0]), half), half), :].astype(bf16)


def unpack_kernel(
    place, own, one, two, three, gain1_ref, gain2_ref, qkv_ref, bq_ref, bkv_ref, ao_ref, bo_ref, ai_ref, bi_ref,
    aff_ref, bff_ref, r1_ref, r2_ref, table_ref, quarters2, quarters1,
):
    rows = FF_ROWS + AT_ROWS

    def piece(ref, first, count):
        return jnp.concatenate([ref[rows * t + first : rows * t + first + count, :] for t in range(6)], 1).astype(f32)

    m = place[0]
    bi_ref[...] = piece(own, 0, LORA)
    mine = piece(own, FF_ROWS, LORA)
    bq_ref[...] = mine[:, 192:384]
    bkv_ref[0] = mine[:, 384:576]
    bkv_ref[1] = mine[:, 576:768]
    table_ref[...] = own[FF_ROWS + 2 * LORA : FF_ROWS + 2 * LORA + 8, :].astype(f32)[:3, :BUCKETS]
    for j, ref in enumerate((own, one, two, three)):
        there = jnp.bitwise_xor(m, j)
        quarters2[there] = piece(ref, 2 * LORA, LORA)
        quarters1[there] = piece(ref, FF_ROWS + LORA, LORA)
        low = piece(ref, LORA, LORA)
        out = piece(ref, FF_ROWS, LORA)[:, :192]
        for at in range(4):

            @pl.when(there == at)
            def _():
                aff_ref[:, MODEL_WIDTH * at : MODEL_WIDTH * at + MODEL_WIDTH] = low
                ao_ref[:, 192 * at : 192 * at + 192] = out

    for part in range(3):
        qkv_ref[part] = quarters1[part]
    ai_ref[...] = quarters2[0]
    bff_ref[...] = quarters2[1]
    bo_ref[...] = quarters2[2]
    r1_ref[...] = quarters1[3, :EXPERTS]
    r2_ref[...] = quarters2[3, :EXPERTS]
    total = jnp.zeros((8, LANES), f32)
    for ref in (own, one, two, three):
        total = total + ref[6 * rows : 6 * rows + 16, :].astype(f32)[:8]
    gain1_ref[...] = total[:6]
    gain2_ref[...] = jnp.concatenate([quarters2[3, 16:17, LANES * t : LANES * t + LANES] for t in range(6)], 0)


def whole(array):
    return pl.BlockSpec(array.shape, lambda *_: (0,) * array.ndim)


def rows_block(array):
    return pl.BlockSpec((HALF_ROWS, array.shape[1]), lambda i, *_: (i, 0))


def token_block():
    return pl.BlockSpec((HALF_ROWS, MODEL_WIDTH), lambda i, place, *_: (place[0] + 4 * i, 0))


def shape(dims, dtype):
    return jax.ShapeDtypeStruct(dims, dtype)


def call(kernel, grid, scalars, inputs, in_specs, outs, out_specs, scratch=(), aliases=None, flops=0):
    return pl.pallas_call(
        kernel,
        grid_spec=pltpu.PrefetchScalarGridSpec(
            num_scalar_prefetch=len(scalars),
            grid=grid,
            in_specs=in_specs,
            out_specs=out_specs,
            scratch_shapes=list(scratch),
        ),
        out_shape=outs,
        input_output_aliases=aliases or {},
        compiler_params=pltpu.CompilerParams(vmem_limit_bytes=VMEM_LIMIT),
        cost_estimate=pl.CostEstimate(flops=flops, bytes_accessed=0, transcendentals=0),
    )(*scalars, *inputs)


def exchange(value, axis, size, mask):
    return lax.ppermute(value, axis, [(i, i ^ mask) for i in range(size)])


def sum_over(keep, send, axis, size, index):
    bits = size.bit_length() - 1
    for bit in range(bits):
        if bit > 0:
            mine = (index >> bit) & 1
            halves = keep.reshape(2, -1, keep.shape[-1])
            send = lax.dynamic_index_in_dim(halves, 1 - mine, 0, False).astype(bf16)
            keep = lax.dynamic_index_in_dim(halves, mine, 0, False)
        keep = keep + exchange(send, axis, size, 1 << bit).astype(f32)
    total = keep.astype(bf16)
    for bit in reversed(range(bits)):
        other = exchange(total, axis, size, 1 << bit)
        mine = (index >> bit) & 1
        total = jnp.where(mine == 0, jnp.concatenate([total, other], 0), jnp.concatenate([other, total], 0))
    return total


def constants():
    group1 = np.zeros((LANES, LANES), np.float32)
    for i in range(3 * LORA):
        for j in range(LORA):
            group1[i, j] = float((i % LORA) // ADAPTER_RANK == j // ADAPTER_RANK)
    pick = np.zeros((LANES, LANES), np.float32)
    for e in range(EXPERTS):
        pick[ADAPTER_RANK * e, e] = 1.0
    turn = np.eye(LANES, dtype=np.float32)[::-1].copy()
    return tuple(jnp.asarray(c, bf16) for c in (group1, pick, turn))


def local(
    dp_size,
    mp_size,
    tokens,
    cotangent,
    attention_norm_gain,
    feedforward_norm_gain,
    query_projection_weight,
    key_value_weight,
    attention_output_weight,
    ffn_input_weight,
    ffn_output_weight,
    projection_down_weight,
    query_up_weight,
    key_value_up_weight,
    attention_output_down_weight,
    attention_output_up_weight,
    ffn_input_down_weight,
    ffn_input_up_weight,
    ffn_output_down_weight,
    ffn_output_up_weight,
    attention_router_weight,
    feedforward_router_weight,
    bucket_bias_table,
    offset_bucket_map,
    sequence_length_list,
):
    m = lax.axis_index("mp").astype(jnp.int32)
    d = lax.axis_index("dp").astype(jnp.int32)
    place = m.reshape(1)
    spot = (d & 1).reshape(1)
    group, pick, turn = constants()

    def mp_swap(value, mask):
        return exchange(value, "mp", mp_size, mask)

    def pack_part(rows, index):
        return pl.BlockSpec((rows, MODEL_WIDTH), lambda *_: (index, 0))

    def element_part(rows, first):
        return pl.BlockSpec((pl.Element(rows), pl.Element(MODEL_WIDTH)), lambda *_: (first, 0))

    inputs = [
        query_projection_weight.T,
        jnp.transpose(key_value_weight, (0, 2, 1)),
        query_up_weight,
        key_value_up_weight,
        bucket_bias_table.T,
    ]
    pack_shape = shape((FIRST_ROWS, MODEL_WIDTH), bf16)
    pack0 = call(first_pack_kernel, (1,), [], inputs, [whole(a) for a in inputs], pack_shape, whole(pack_shape))
    pack2 = mp_swap(pack0, 2)
    win0, wout0 = ffn_input_weight, ffn_output_weight
    half = (d & 1).reshape(1)
    inputs = [pack0, attention_output_weight, ffn_input_up_weight, win0]
    outs = [shape((SECOND_ROWS + HALF_SHARD, MODEL_WIDTH), bf16), shape((SECOND_ROWS + FIRST_ROWS, MODEL_WIDTH), bf16)]
    more0, both0 = call(
        second_pack_kernel,
        (1,),
        [half],
        inputs,
        [whole(a) for a in inputs[:3]] + [pl.BlockSpec((HALF_SHARD, MODEL_WIDTH), lambda i, half: (half[0], 0))],
        outs,
        [whole(o) for o in outs],
    )
    both1 = mp_swap(both0, 1)
    more2 = mp_swap(more0, 2)
    wout2 = mp_swap(wout0, 2)

    gain1 = attention_norm_gain.reshape(1, -1)
    gain2 = feedforward_norm_gain.reshape(1, -1)
    downs_in = jnp.transpose(projection_down_weight, (0, 2, 1))
    router1, router2 = attention_router_weight.T, feedforward_router_weight.T
    rev_map = jnp.concatenate([offset_bucket_map[::-1], jnp.full((1,), -1, jnp.int32)]).reshape(1, -1)

    wide, narrow = shape((ROWS, MODEL_WIDTH), bf16), shape((ROWS, LANES), f32)
    narrow16 = shape((ROWS, LANES), bf16)

    joined_shape, ups_shape = shape((6, 384, MODEL_WIDTH), bf16), shape((6, LANES, 384), bf16)
    pair_outs = [wide, wide, wide, wide, shape((6, 8, 256), f32), shape((6, 7, LANES, 256), bf16), joined_shape, ups_shape]

    def pair_specs(first):
        specs = [pl.BlockSpec((ROWS, LANES), lambda p, *_: (0, first + p))] * 4
        for o in pair_outs[4:]:
            specs.append(pl.BlockSpec((1,) + o.shape[1:], lambda p, *_, n=len(o.shape): (first + p,) + (0,) * (n - 1)))
        return specs

    def half_of_rows(part):
        return pl.BlockSpec((HALF_ROWS, MODEL_WIDTH), lambda p, place, *_: (place[0] + 4 * part, 0))

    joined_scratch = [pltpu.VMEM((3, 384, MODEL_WIDTH), bf16), pltpu.VMEM((3, LANES, 384), bf16)]
    fixed = [wide, narrow16, narrow, narrow]
    *pair_state, normed1, mixed1, spread1, downs1 = call(
        first_kernel,
        (3,),
        [place, sequence_length_list],
        [tokens, tokens, gain1, downs_in, router1, pack0, pack0, both1, both1, rev_map],
        [half_of_rows(0), half_of_rows(1), whole(gain1), whole(downs_in), whole(router1)]
        + [pack_part(576, 0), pack_part(48, 12), element_part(576, 240), pack_part(48, 17)]
        + [whole(rev_map)],
        pair_outs + fixed,
        pair_specs(0) + [whole(o) for o in fixed],
        scratch=joined_scratch + [pltpu.VMEM((256, MODEL_WIDTH), bf16)],
        flops=20_000_000_000,
    )
    pack2, normed1, win0, wout0 = lax.optimization_barrier((pack2, normed1, win0, wout0))
    pack3 = mp_swap(pack2, 1)
    win1, wout1 = mp_swap(win0, 1), mp_swap(wout0, 1)
    inputs = [normed1, mixed1, pack2, pack2, pack3, pack3, rev_map]
    queries, keys, all_values, attended, lse, tiles, joined, ups = call(
        second_kernel,
        (3,),
        [place, sequence_length_list],
        inputs + pair_state,
        [whole(normed1), whole(mixed1)]
        + [pack_part(576, 0), pack_part(48, 12)] * 2
        + [whole(rev_map)]
        + [pl.BlockSpec(memory_space=pl.ANY)] * 8,
        pair_outs,
        pair_specs(3),
        scratch=joined_scratch,
        aliases={2 + len(inputs) + i: i for i in range(8)},
    )

    attended, more2 = lax.optimization_barrier((attended, more2))
    more3 = mp_swap(more2, 1)
    other2 = exchange(more2, "dp", dp_size, 1)
    mores = [more0, both1, more2, more3]
    ao_in, bo_in, bf_in = attention_output_down_weight.T, attention_output_up_weight, ffn_output_up_weight
    down_in, low_in = ffn_input_down_weight.T, ffn_output_down_weight.T

    def low_block(j):
        return pl.BlockSpec((LORA, MODEL_WIDTH), lambda i, place, *_: (0, jnp.bitwise_xor(place[0], j)))

    def small_inputs(first):
        values = [ao_in, bo_in, gain2, down_in, router2, bf_in]
        specs = [whole(a) for a in values]
        for j in (first, first + 1):
            values += [mores[j], low_in]
            specs += [pack_part(48, 4), low_block(j)]
        return values, specs

    hbm = pl.BlockSpec(memory_space=pltpu.HBM)
    shard_shape = shape((2, 2, LORA, MODEL_WIDTH), f32)
    wide_f32, wider, wider_f32 = shape((ROWS, MODEL_WIDTH), f32), shape((ROWS, WIDER), bf16), shape((ROWS, WIDER), f32)
    state_shapes = [wide_f32, wider, wider, shape((ROWS, 4 * LANES), f32), wider_f32, wider_f32]

    def held(array):
        return pltpu.VMEM(array.shape, array.dtype)

    map_scratch = [
        pltpu.VMEM((LANES, MODEL_WIDTH), bf16),
        pltpu.VMEM((LANES, MODEL_WIDTH), bf16),
        pltpu.VMEM((MODEL_WIDTH, MODEL_WIDTH), bf16),
        pltpu.VMEM((256, MODEL_WIDTH), bf16),
        pltpu.VMEM((LANES, MODEL_WIDTH), bf16),
        pltpu.VMEM((2, WIDER, MODEL_WIDTH), bf16),
        pltpu.VMEM((2, MODEL_WIDTH, WIDER), bf16),
    ]
    values, specs = small_inputs(0)
    inputs = [tokens, cotangent, attended] + mores + [spread1, win0, wout0, win1, wout1]
    *state, shard_grads = call(
        middle_kernel,
        (2,),
        [place],
        inputs + values,
        [token_block(), token_block(), rows_block(attended)]
        + [pack_part(192, 0)] * 4
        + [rows_block(spread1)]
        + [whole(a) for a in inputs[-4:]]
        + specs,
        state_shapes + [shard_shape],
        [rows_block(a) for a in state_shapes] + [whole(shard_shape)],
        scratch=map_scratch,
    )
    state[0], other2, wout2 = lax.optimization_barrier((state[0], other2, wout2))
    other3 = mp_swap(other2, 1)
    wout3 = mp_swap(wout2, 1)
    values, specs = small_inputs(2)
    ao_shape = shape((LORA, MODEL_WIDTH), f32)
    ff_shapes = [shape((FF_ROWS, MODEL_WIDTH), f32)] + [shape((FF_ROWS, MODEL_WIDTH), bf16)] * 3
    inputs = [attended] + mores + [spread1, more2, other2, wout2, more3, other3, wout3] + state
    values += [group, pick, shard_grads]
    specs += [whole(a) for a in (group, pick, shard_grads)]
    outs = [wide, wide_f32, wide, narrow, ao_shape] + ff_shapes
    result, ghidden, gatt, prod, ao_grad, *ff_pieces = call(
        post_kernel,
        (1,),
        [place, half],
        inputs + values,
        [hbm] * len(inputs) + specs,
        outs,
        [hbm] * 4 + [whole(o) for o in outs[4:]],
        scratch=[held(wide), held(narrow)]
        + [held(a) for a in state_shapes]
        + [held(wide), held(wide), held(narrow)]
        + map_scratch
        + [
            pltpu.VMEM((2, 2, LORA, MODEL_WIDTH), f32),
            pltpu.VMEM((256, MODEL_WIDTH), f32),
            pltpu.VMEM((LANES, MODEL_WIDTH), f32),
            pltpu.VMEM((LANES, MODEL_WIDTH), f32),
            pltpu.VMEM((LANES, MODEL_WIDTH), f32),
            pltpu.VMEM((1, MODEL_WIDTH), f32),
            pltpu.VMEM((4, FF_ROWS, MODEL_WIDTH), f32),
            pltpu.SemaphoreType.DMA((18,)),
            pltpu.SemaphoreType.DMA((8,)),
        ],
    )
    result2 = mp_swap(result, 2)
    ff_parts = [ff_pieces[0]] + [mp_swap(ff_pieces[j], j) for j in (1, 2, 3)]

    at_shapes = [shape((AT_ROWS, MODEL_WIDTH), f32)] + [shape((AT_ROWS, MODEL_WIDTH), bf16)] * 3
    fixed = [normed1, mixed1, spread1, downs1, prod, downs_in, router1, group, pick, ao_grad]
    specs = pair_specs(0)
    gnormed, *at_pieces = call(
        back_kernel,
        (6,),
        [place, sequence_length_list],
        [queries, keys, all_values, gatt, lse, tiles, rev_map, turn, joined, ups] + fixed,
        specs[:6] + [whole(rev_map), whole(turn)] + specs[6:] + [whole(a) for a in fixed],
        [wide_f32] + at_shapes,
        [whole(wide_f32)] + [whole(o) for o in at_shapes],
        scratch=[
            pltpu.VMEM((LONG_LEN, 1024), bf16),
            pltpu.VMEM((LONG_LEN, 1024), bf16),
            pltpu.VMEM((1024, LANES), bf16),
            pltpu.VMEM((1024, LANES), bf16),
            pltpu.VMEM((7, LANES, 256), f32),
            pltpu.VMEM((ROWS, LANES), bf16),
            pltpu.VMEM((ROWS, LANES), bf16),
            pltpu.VMEM((ROWS, LANES), bf16),
            pltpu.VMEM((6, 8, LANES), f32),
            pltpu.VMEM((ROWS, LANES), f32),
            pltpu.VMEM((6, LANES, 384), f32),
            pltpu.VMEM((256, MODEL_WIDTH), bf16),
            pltpu.VMEM((256, MODEL_WIDTH), f32),
            pltpu.VMEM((4, AT_ROWS, MODEL_WIDTH), f32),
        ],
    )
    gain_shape = shape((1, MODEL_WIDTH), f32)
    gtokens, ggain = call(
        last_kernel,
        (2,),
        [place],
        [tokens, gain1, gnormed, ghidden],
        [token_block(), whole(gain1), rows_block(gnormed), rows_block(ghidden)],
        [wide, gain_shape],
        [rows_block(wide), whole(gain_shape)],
    )
    result2, ff_parts, at_pieces = lax.optimization_barrier((result2, ff_parts, at_pieces))
    at_parts = [at_pieces[0]] + [mp_swap(at_pieces[j], j) for j in (1, 2, 3)]
    gtokens2 = mp_swap(gtokens, 2)

    def spread_rows(own, one, two, three):
        return call(
            spread_kernel,
            (1,),
            [place],
            [own, one, two, three],
            [pl.BlockSpec(memory_space=pltpu.HBM)] * 4,
            shape((4 * ROWS, MODEL_WIDTH), bf16),
            pl.BlockSpec(memory_space=pltpu.HBM),
            scratch=[
                pltpu.VMEM((4, ROWS, MODEL_WIDTH), bf16),
                pltpu.SemaphoreType.DMA((4, 2)),
                pltpu.SemaphoreType.DMA((4, 2)),
            ],
        )

    halves = [shape((FLAT_ROWS // 2, LANES), f32), shape((FLAT_ROWS // 2, LANES), bf16)]
    parts = ff_parts + at_parts + [ggain]
    keep, send = call(
        scatter_kernel,
        (1,),
        [spot],
        parts,
        [whole(a) for a in parts],
        halves,
        [whole(a) for a in halves],
        scratch=[pltpu.VMEM((FLAT_ROWS, LANES), f32)],
    )
    send, result2 = lax.optimization_barrier((send, result2))
    result1, result3 = mp_swap(result, 1), mp_swap(result2, 1)
    own = sum_over(keep, send, "dp", dp_size, d)
    own, result1, result3, gtokens2 = lax.optimization_barrier((own, result1, result3, gtokens2))
    two = mp_swap(own, 2)
    one = mp_swap(own, 1)
    gtokens1, gtokens3 = mp_swap(gtokens, 1), mp_swap(gtokens2, 1)
    output = spread_rows(result, result1, result2, result3)
    two, output = lax.optimization_barrier((two, output))
    three = mp_swap(two, 1)
    grad_tokens = spread_rows(gtokens, gtokens1, gtokens2, gtokens3)
    three, grad_tokens = lax.optimization_barrier((three, grad_tokens))
    outs = [
        shape((6, LANES), f32),
        shape((6, LANES), f32),
        shape((3, LORA, MODEL_WIDTH), f32),
        shape((LORA, 192), f32),
        shape((2, LORA, 192), f32),
        shape((LORA, MODEL_WIDTH), f32),
        shape((LORA, MODEL_WIDTH), f32),
        shape((LORA, MODEL_WIDTH), f32),
        shape((LORA, MODEL_WIDTH), f32),
        shape((LORA, 4 * MODEL_WIDTH), f32),
        shape((LORA, MODEL_WIDTH), f32),
        shape((EXPERTS, MODEL_WIDTH), f32),
        shape((EXPERTS, MODEL_WIDTH), f32),
        shape((3, BUCKETS), f32),
    ]
    flats = [own, one, two, three]
    grads = call(
        unpack_kernel,
        (1,),
        [place],
        flats,
        [whole(a) for a in flats],
        outs,
        [whole(o) for o in outs],
        scratch=[pltpu.VMEM((4, LORA, MODEL_WIDTH), f32)] * 2,
    )
    g1, g2, g_qkv, g_bq, g_bkv, g_ao, g_bo, g_ai, g_bi, g_aff, g_bff, g_r1, g_r2, g_table = grads
    return (
        output,
        grad_tokens,
        g1.reshape(-1),
        g2.reshape(-1),
        jnp.transpose(g_qkv, (0, 2, 1)),
        g_bq,
        g_bkv,
        g_ao.T,
        g_bo,
        g_ai.T,
        g_bi,
        g_aff.T,
        g_bff,
        g_r1.T,
        g_r2.T,
        g_table.T,
    )


def solution(mesh):
    in_specs = (
        P("dp", None),
        P("dp", None),
        P(),
        P(),
        P(None, "mp"),
        P(None, None, "mp"),
        P("mp", None),
        P(None, "mp"),
        P("mp", None),
        P(),
        P(None, "mp"),
        P(None, None, "mp"),
        P(),
        P(),
        P(),
        P(None, "mp"),
        P(),
        P(),
        P(),
        P(),
        P(None, "mp"),
        P(),
        P("dp"),
    )
    out_specs = (
        P("dp", None),
        P("dp", None),
        P(),
        P(),
        P(),
        P(None, "mp"),
        P(None, None, "mp"),
        P(),
        P(),
        P(),
        P(None, "mp"),
        P(),
        P(),
        P(),
        P(),
        P(None, "mp"),
    )
    step = functools.partial(local, mesh.shape["dp"], mesh.shape["mp"])
    return jax.shard_map(step, mesh=mesh, in_specs=in_specs, out_specs=out_specs, check_vma=False)
```

```python
import functools

import jax
import jax.numpy as jnp
import numpy as np
from jax import lax
from jax.experimental import pallas as pl
from jax.experimental.pallas import tpu as pltpu
from jax.sharding import PartitionSpec as P

HEAD_WIDTH = 64
BUCKETS = 32
ADAPTER_RANK = 4
SHORT_LEN = 128
LONG_LEN = 512
LONG_SEQS = 4
SHORT_SEQS = 16
MODEL_WIDTH = 768
LORA = 40
EXPERTS = 10
LANES = 128
HALF_ROWS = 512
ROWS = 1024
EPS = 1e-06
NEG = -1e9

bf16 = jnp.bfloat16
f32 = jnp.float32
VMEM_LIMIT = 56 * 1024 * 1024


def nn(a, b):
    return jnp.dot(a, b, preferred_element_type=f32)


def nt(a, b):
    return lax.dot_general(a, b, (((1,), (1,)), ((), ())), preferred_element_type=f32)


def tn(a, b):
    return lax.dot_general(a, b, (((0,), (0,)), ((), ())), preferred_element_type=f32)


def lane_index(shape):
    return lax.broadcasted_iota(jnp.int32, shape, 1)


def softmax_repeated(logits, valid, repeats):
    logits = jnp.where(lane_index(logits.shape) < valid, logits, -1e30)
    raised = jnp.exp(logits - jnp.max(logits, -1, keepdims=True))
    return raised * (repeats / jnp.sum(raised, -1, keepdims=True))


def logit_gradient(products, gates, group, pick):
    high = products.astype(bf16)
    low = (products - high.astype(f32)).astype(bf16)
    gate_grad = nn(high, group) + nn(low, group)
    inner = jnp.sum(gates * gate_grad, -1, keepdims=True) * (1.0 / ADAPTER_RANK)
    logit_grad = (gates * (gate_grad - inner)).astype(bf16)
    return nn(logit_grad, pick).astype(bf16)


QK_ROWS, V_ROWS, SECOND_ROWS, HALF_SHARD = 384, 240, 240, 384


def pack_kernel(half, q_ref, kv_ref, qup_ref, kvup_ref, table_ref, wo_ref, up_ref, win_ref, qk_ref, v_ref, second_ref, both_ref):
    qk_ref[0:192, :] = q_ref[...]
    qk_ref[192:384, :] = kv_ref[0]
    v_ref[0:192, :] = kv_ref[1]
    ups = jnp.concatenate([qup_ref[...], kvup_ref[0], kvup_ref[1], jnp.zeros((LORA, 192), bf16)], 1).astype(f32)
    table = jnp.pad(table_ref[...].astype(f32), ((0, 5), (0, MODEL_WIDTH - BUCKETS)))
    v_ref[192:240, :] = jnp.concatenate([ups, table], 0).astype(bf16)
    second_ref[0:192, :] = wo_ref[...]
    second_ref[192:240, :] = jnp.pad(up_ref[...].astype(f32), ((0, 8), (0, 0))).astype(bf16)
    second_ref[240:, :] = win_ref[...]
    both_ref[:SECOND_ROWS, :] = second_ref[:SECOND_ROWS, :]
    both_ref[SECOND_ROWS : SECOND_ROWS + QK_ROWS, :] = qk_ref[...]
    both_ref[SECOND_ROWS + QK_ROWS :, :] = v_ref[...]


def pad_to(rows, count):
    if rows.shape[0] == count:
        return rows
    return jnp.concatenate([rows, jnp.zeros((count - rows.shape[0], rows.shape[1]), rows.dtype)], 0)


def repeated_router(router, copies):
    rows = lax.broadcasted_iota(jnp.int32, (LANES, EXPERTS), 0)
    first = ADAPTER_RANK * lax.broadcasted_iota(jnp.int32, (LANES, EXPERTS), 1)
    hot = jnp.zeros((LANES, EXPERTS), jnp.bool_)
    for c in range(copies):
        hot = hot | ((rows >= LORA * c + first) & (rows < LORA * c + first + ADAPTER_RANK))
    return nn(hot.astype(bf16), router).astype(bf16)


def down_rows(downs, router_rows):
    downs = pad_to(jnp.concatenate([part.astype(f32) for part in downs], 0), LANES)
    return jnp.concatenate([downs, pad_to(router_rows.astype(f32), LANES)], 0).astype(bf16)


def weight_rows(refs, part):
    if len(refs) == 1:
        return refs[0].at[192 * part : 192 * part + 192]
    return refs[1].at[0:192] if part == 2 else refs[0].at[192 * part : 192 * part + 192]


def join_packs(one, two, ups_one, ups_two, joined_scr, ups_scr):
    for part in range(3):
        at = LANES * part
        one_ref, two_ref = weight_rows(one, part), weight_rows(two, part)
        joined_scr[0, at : at + LANES, :] = one_ref[0:LANES, :]
        joined_scr[1, at : at + 64, :] = one_ref[LANES:192, :]
        joined_scr[1, at + 64 : at + LANES, :] = two_ref[0:64, :]
        joined_scr[2, at : at + LANES, :] = two_ref[64:192, :]
    pieces = []
    for part in range(3):
        cols = slice(192 * part, 192 * part + 192)
        pieces.append(jnp.concatenate([ups_one[:LORA, cols], ups_two[:LORA, cols]], 1).astype(f32))
    zero = jnp.zeros((LORA, LANES), f32)
    for pair in range(3):
        rows = []
        for part in range(3):
            piece = pieces[part][:, LANES * pair : LANES * pair + LANES]
            rows.append(jnp.concatenate([piece if p == part else zero for p in range(3)], 1))
        ups_scr[pair] = pad_to(jnp.concatenate(rows, 0), LANES).astype(bf16)


def project_pair(normed_ref, mixed_ref, joined_scr, ups_scr, q_ref, k_ref, v_ref, joined_ref, ups_ref):
    pair = pl.program_id(0)
    joined, ups = joined_scr[pair], ups_scr[pair]
    joined_ref[0] = joined
    ups_ref[0] = ups
    for first in (0, HALF_ROWS):
        rows = slice(first, first + HALF_ROWS)
        result = (nt(normed_ref[rows, :], joined) + nn(mixed_ref[rows, :], ups)).astype(bf16)
        q_ref[rows, :] = result[:, :LANES]
        k_ref[rows, :] = result[:, LANES : 2 * LANES]
        v_ref[rows, :] = result[:, 2 * LANES :]


def first_kernel(
    place, lengths, xs_ref, xl_ref, gain_ref, downs_in, router_ref, one_qk, one_v, ups_one, two_ref, ups_two, map_ref,
    q_ref, k_ref, v_ref, o_ref, lse_ref, tile_ref, joined_ref, ups_ref, normed_ref, mixed_ref, spread_ref, downs_ref,
    joined_scr, ups_scr, down_scr,
):
    @pl.when(pl.program_id(0) == 0)
    def _():
        join_packs((one_qk, one_v), (two_ref,), ups_one, ups_two, joined_scr, ups_scr)
        down_scr[...] = down_rows([downs_in[0], downs_in[1], downs_in[2]], repeated_router(router_ref[...], 3))
        for x_ref, first in ((xs_ref, 0), (xl_ref, HALF_ROWS)):
            rows = slice(first, first + HALF_ROWS)
            x = x_ref[...].astype(f32)
            scale = lax.rsqrt(jnp.mean(x * x, -1, keepdims=True) + EPS)
            normed = (x * scale * gain_ref[...].astype(f32)).astype(bf16)
            normed_ref[rows, :] = normed
            both = nt(normed, down_scr[...])
            downs = both[:, :LANES]
            spread = softmax_repeated(both[:, LANES:], 3 * LORA, 3.0 * ADAPTER_RANK)
            mixed_ref[rows, :] = (spread * downs).astype(bf16)
            spread_ref[rows, :] = spread
            downs_ref[rows, :] = downs

    project_pair(normed_ref, mixed_ref, joined_scr, ups_scr, q_ref, k_ref, v_ref, joined_ref, ups_ref)
    forward_attention(place, lengths, q_ref, k_ref, v_ref, ups_one, ups_two, map_ref, o_ref, lse_ref, tile_ref)


def second_kernel(
    place, lengths, normed_ref, mixed_ref, one_qk, one_v, ups_one, two_qk, two_v, ups_two, map_ref,
    q_in, k_in, v_in, o_in, lse_in, tile_in, joined_in, ups_in,
    q_ref, k_ref, v_ref, o_ref, lse_ref, tile_ref, joined_ref, ups_ref, joined_scr, ups_scr,
):
    @pl.when(pl.program_id(0) == 0)
    def _():
        join_packs((one_qk, one_v), (two_qk, two_v), ups_one, ups_two, joined_scr, ups_scr)

    project_pair(normed_ref, mixed_ref, joined_scr, ups_scr, q_ref, k_ref, v_ref, joined_ref, ups_ref)
    forward_attention(place, lengths, q_ref, k_ref, v_ref, ups_one, ups_two, map_ref, o_ref, lse_ref, tile_ref)


def split_pair(rows):
    lanes = lane_index(rows.shape)
    zero = jnp.zeros_like(rows)
    return jnp.concatenate([jnp.where(lanes < HEAD_WIDTH, rows, zero), jnp.where(lanes < HEAD_WIDTH, zero, rows)], 0)


def merge_pair(turned):
    return jnp.concatenate([turned[:HEAD_WIDTH, :LANES], turned[HEAD_WIDTH:, LANES:]], 0).T


def bucket_hot(map_ref):
    rows = lax.broadcasted_iota(jnp.int32, (BUCKETS, 2 * LONG_LEN), 0)
    return rows == map_ref[...]


def build_tiles(one_ref, two_ref, map_ref, tile_ref):
    pair = pl.program_id(0)
    hot = bucket_hot(map_ref).astype(bf16)
    table = jnp.concatenate(
        [one_ref[LORA : LORA + 8, :BUCKETS].astype(f32), two_ref[LORA : LORA + 8, :BUCKETS].astype(f32)], 0
    )
    by_offset = nn(table.astype(bf16), hot)
    heads = lax.broadcasted_iota(jnp.int32, (16, 1), 0)
    heads = jnp.where(heads < 8, heads, heads - 5)
    used = lax.broadcasted_iota(jnp.int32, (16, 1), 0)
    heads = jnp.where((used < 3) | ((used >= 8) & (used < 11)), heads, -1)
    rows_in = lax.broadcasted_iota(jnp.int32, (LANES, LANES), 0)
    lanes = lane_index((LANES, LANES))
    for t in range(2):
        row = jnp.sum(jnp.where(heads == 2 * pair + t, by_offset, 0.0), 0, keepdims=True)
        for d in range(7):
            block = 6 - d
            low = jnp.broadcast_to(row[:, LANES * block : LANES * block + LANES], (LANES, LANES))
            high = jnp.broadcast_to(row[:, LANES * block + LANES : LANES * block + 2 * LANES], (LANES, LANES))
            low = pltpu.roll(low, 1, 1, stride=1, stride_axis=0)
            high = pltpu.roll(high, 1, 1, stride=1, stride_axis=0)
            tile_ref[d, :, LANES * t : LANES * t + LANES] = jnp.where(lanes <= rows_in, low, high).astype(bf16)


def chunk_layout():
    chunks = []
    for c in range(LONG_LEN // LANES):
        chunks.append((HALF_ROWS, LONG_LEN, HALF_ROWS + LANES * c, 3 - c, 4))
    for s in range(HALF_ROWS // SHORT_LEN):
        chunks.append((LANES * s, SHORT_LEN, LANES * s, 3, s))
    return chunks


def length_of(place, lengths, which):
    m = place[0]
    if which == 4:
        return lengths[SHORT_SEQS + m]
    return lengths[4 * m + which]


def tiles_of(tile_ref, first, span):
    return jnp.concatenate([tile_ref[first + b].astype(f32) for b in range(span // LANES)], 0)


def biased(scores, tiles, length):
    scores = scores + tiles
    positions = lax.broadcasted_iota(jnp.int32, scores.shape, 0)
    return jnp.where(positions < length, scores, NEG)


def forward_attention(place, lengths, q_ref, k_ref, v_ref, one_ref, two_ref, map_ref, o_ref, lse_ref, tile_ref):
    tiles = tile_ref.at[0]
    build_tiles(one_ref, two_ref, map_ref, tiles)
    chunks = chunk_layout()
    raw = []
    for key_row, span, query_row, first, which in chunks:
        queries = split_pair(q_ref[query_row : query_row + LANES, :])
        raw.append(nt(k_ref[key_row : key_row + span, :], queries))
    weights = []
    for number, (key_row, span, query_row, first, which) in enumerate(chunks):
        scores = biased(raw[number], tiles_of(tiles, first, span), length_of(place, lengths, which))
        peak = jnp.max(scores, 0, keepdims=True)
        raised = jnp.exp(scores - peak)
        total = jnp.sum(raised, 0, keepdims=True)
        lse_ref[0, number : number + 1, :] = peak + jnp.log(total)
        weights.append((raised * (1.0 / total)).astype(bf16))
    turned = v_ref[HALF_ROWS:, :].T
    for number, (key_row, span, query_row, first, which) in enumerate(chunks):
        if which != 4:
            turned = v_ref[key_row : key_row + span, :].T
        o_ref[query_row : query_row + LANES, :] = merge_pair(nn(turned, weights[number])).astype(bf16)


def part_chunks(part):
    if part == 1:
        return [(c, 0, LONG_LEN, LANES * c, 3 - c, 4) for c in range(LONG_LEN // LANES)]
    return [(4 + s, LANES * s, SHORT_LEN, LANES * s, 0, s) for s in range(HALF_ROWS // SHORT_LEN)]


PAIRS = 2


def backward_attention(
    part, place, lengths, q_ref, k_ref, v_ref, do_ref, lse_ref, tile_ref, map_ref, turn_ref, table_scr, gathered
):
    turn = turn_ref[...]
    chunks = part_chunks(part)
    work = [(pair, c) + chunk for pair in range(PAIRS) for c, chunk in enumerate(chunks)]
    raw, grad_probs, kept = [], [], []
    for pair, c, number, key_row, span, query_row, first, which in work:
        cols = slice(LANES * pair, LANES * pair + LANES)
        queries = split_pair(q_ref[query_row : query_row + LANES, cols])
        douts = split_pair(do_ref[query_row : query_row + LANES, cols])
        raw.append(nt(k_ref[key_row : key_row + span, cols], queries))
        grad_probs.append(nt(v_ref[key_row : key_row + span, cols], douts))
        kept.append((queries, douts))
    grads, weights = [], []
    for i, (pair, c, number, key_row, span, query_row, first, which) in enumerate(work):
        scores = biased(raw[i], tiles_of(tile_ref.at[pair], first, span), length_of(place, lengths, which))
        probs = jnp.exp(scores - lse_ref[pair, number : number + 1, :])
        weights.append(probs.astype(bf16))
        weighted = probs * grad_probs[i]
        inner = jnp.sum(weighted, 0, keepdims=True)
        grads.append((weighted - probs * inner).astype(bf16))
        if part == 1:
            weights_all, grads_all, queries_all, douts_all = gathered
            at = slice(2 * LANES * c, 2 * LANES * c + 2 * LANES)
            weights_all[pair, :, at] = weights[i]
            grads_all[pair, :, at] = grads[i]
            queries_all[pair, at, :] = kept[i][0]
            douts_all[pair, at, :] = kept[i][1]
    result = []
    for pair in range(PAIRS):
        cols = slice(LANES * pair, LANES * pair + LANES)
        turned = k_ref[:, cols].T if part == 1 else None
        dq, dk, dv = [], [], []
        for i, (of, c, number, key_row, span, query_row, first, which) in enumerate(work):
            if of != pair:
                continue
            if part == 0:
                turned = k_ref[key_row : key_row + span, cols].T
                dv.append(nn(weights[i], kept[i][1]).astype(bf16))
                dk.append(nn(grads[i], kept[i][0]).astype(bf16))
            dq.append(merge_pair(nn(turned, grads[i])).astype(bf16))
        if part == 1:
            dv.append(nn(weights_all[pair], douts_all[pair]).astype(bf16))
            dk.append(nn(grads_all[pair], queries_all[pair]).astype(bf16))
        result.append((dq, dk, dv))
    rows_in = lax.broadcasted_iota(jnp.int32, (LANES, LANES), 0)
    lanes = lane_index((LANES, LANES))
    sums = []
    for pair in range(PAIRS):
        mine = grads[len(chunks) * pair : len(chunks) * pair + len(chunks)]
        pieces = [[jnp.zeros((1, LANES), f32) for _ in range(8)] for _ in range(2)]
        for d in range(7):
            if part == 0:
                stack = mine if d == 3 else []
            else:
                stack = [mine[c][LANES * (d - 3 + c) : LANES * (d - 2 + c), :] for c in range(4) if 0 <= d - 3 + c < 4]
            if len(stack) == 0:
                continue
            diagonal = nn(jnp.concatenate([turn] * len(stack), 1), jnp.concatenate(stack, 0))
            block = 6 - d
            for t in range(2):
                rolled = pltpu.roll(diagonal[:, LANES * t : LANES * t + LANES], 0, 1, stride=1, stride_axis=0)
                low = jnp.where(lanes >= rows_in, rolled, 0.0)
                pieces[t][block] = pieces[t][block] + jnp.sum(low, 0, keepdims=True)
                pieces[t][block + 1] = pieces[t][block + 1] + jnp.sum(rolled - low, 0, keepdims=True)
        sums += [jnp.concatenate(p, 1) for p in pieces]
    sums = jnp.concatenate(sums + [jnp.zeros((8 - 2 * PAIRS, 2 * LONG_LEN), f32)], 0)
    hot = bucket_hot(map_ref).astype(f32)
    table = lax.dot_general(
        sums, hot, (((1,), (1,)), ((), ())), precision=lax.Precision.HIGHEST, preferred_element_type=f32
    )
    table_scr[pl.program_id(0)] = jnp.concatenate([table, jnp.zeros((8, LANES - BUCKETS), f32)], 1)
    return result


WIDER = MODEL_WIDTH + LANES


def feedforward_shard(inputs, douts, win_scr, wout_scr, ready=lambda: None):
    before = nn(inputs[...], win_scr[...])
    ready()
    inputs, douts = inputs[...], douts[...]
    sig = 0.5 * jnp.tanh(0.5 * before) + 0.5
    active = (before * sig).astype(bf16)
    out = nn(active, wout_scr[...])
    grad_active = nt(douts, wout_scr[...]).astype(bf16).astype(f32)
    grad_before = (sig * (1.0 + before * (1.0 - sig)) * grad_active).astype(bf16)
    back = nt(grad_before, win_scr[...])
    grad_up = tn(inputs[:, MODEL_WIDTH:], grad_before)[:LORA]
    grad_low = tn(douts[:, MODEL_WIDTH:], active)[:LORA]
    return out, back, grad_up, grad_low


def fill_adapters(win_scr, wout_scr, up, low):
    win_scr[MODEL_WIDTH:, :] = pad_to(up[:LORA, :].astype(f32), LANES).astype(bf16)
    wout_scr[:, MODEL_WIDTH:] = pad_to(low[...].astype(f32), LANES).T.astype(bf16)


def shard_copies(wins, wouts, half, win_scr, wout_scr, sems, first):
    pieces = []
    if len(wins) == 1:
        pieces.append((wins[0], win_scr.at[pl.ds(0, MODEL_WIDTH)]))
    else:
        rows = MODEL_WIDTH // 2
        for k in range(2):
            there = pl.ds(pl.multiple_of(rows * jnp.bitwise_xor(half, k), rows), rows)
            pieces.append((wins[k].at[pl.ds(SECOND_ROWS, rows)], win_scr.at[there]))
    pieces.append((wouts[0], wout_scr.at[:, pl.ds(0, MODEL_WIDTH)]))
    return [pltpu.make_async_copy(source, goal, sems.at[first + i]) for i, (source, goal) in enumerate(pieces)]


def fill_output_maps(place, ao_in, bo_in, ao_scr, bo_scr):
    bo_scr[...] = pad_to(bo_in[...].astype(f32), LANES).astype(bf16)
    for at in range(4):

        @pl.when(place[0] == at)
        def _():
            pieces = [ao_in[:, 192 * (at ^ j) : 192 * (at ^ j) + 192] for j in range(4)]
            ao_scr[...] = pad_to(jnp.concatenate(pieces, 1).astype(f32), LANES).astype(bf16)


def start(copies):
    for copy in copies:
        copy.start()


def wait(copies):
    for copy in copies:
        copy.wait()


def both_blocks():
    return [slice(HALF_ROWS * i, HALF_ROWS * i + HALF_ROWS) for i in range(2)]


def middle_kernel(
    place, x_ref, cot_ref, att_ref, wo0, wo1, wo2, wo3, spread1_ref, win0, wout0, win1, wout1,
    ao_in, bo_in, gain_ref, down_in, router_ref, bf_in, up0, low0, up1, low1,
    hidden, inputs_ref, douts_ref, narrow, out_ref, back_ref, shard_ref,
    ao_scr, bo_scr, wo_scr, down_scr, bf_scr, win_scr, wout_scr,
):
    @pl.when(pl.program_id(0) == 0)
    def _():
        fill_output_maps(place, ao_in, bo_in, ao_scr, bo_scr)
        for j, wo in enumerate((wo0, wo1, wo2, wo3)):
            wo_scr[192 * j : 192 * j + 192, :] = wo[...]
        down_scr[...] = down_rows([down_in[...]], repeated_router(router_ref[...], 1))
        bf_scr[...] = pad_to(bf_in[...].astype(f32), LANES).astype(bf16)
        for j, (win, wout, up, low) in enumerate(((win0, wout0, up0, low0), (win1, wout1, up1, low1))):
            win_scr[j, :MODEL_WIDTH, :] = win[...]
            wout_scr[j, :, :MODEL_WIDTH] = wout[...]
            fill_adapters(win_scr.at[j], wout_scr.at[j], up, low)
        shard_ref[...] = jnp.zeros_like(shard_ref)

    attended = att_ref[...]
    downo = nt(attended, ao_scr[...])
    mixo = (spread1_ref[...] * downo).astype(bf16)
    held = x_ref[...].astype(f32) + (nn(attended, wo_scr[...]) + nn(mixo, bo_scr[...]))
    hidden[...] = held
    scale = lax.rsqrt(jnp.mean(held * held, -1, keepdims=True) + EPS)
    normed = (held * scale * gain_ref[...].astype(f32)).astype(bf16)
    both = nt(normed, down_scr[...])
    downi = both[:, :LANES]
    spread = softmax_repeated(both[:, LANES:], LORA, 1.0 * ADAPTER_RANK)
    cot = cot_ref[...]
    sidef = nt(cot, bf_scr[...])
    inputs = jnp.concatenate([normed, (spread * downi).astype(bf16)], 1)
    douts = jnp.concatenate([cot, (spread * sidef).astype(bf16)], 1)
    inputs_ref[...] = inputs
    douts_ref[...] = douts
    narrow[:, :LANES] = spread
    narrow[:, LANES : 2 * LANES] = downi
    narrow[:, 2 * LANES : 3 * LANES] = sidef
    narrow[:, 3 * LANES :] = downo
    for j in range(2):
        out, back, grad_up, grad_low = feedforward_shard(inputs, douts, win_scr.at[j], wout_scr.at[j])
        if j == 0:
            out_ref[...] = out
            back_ref[...] = back
        else:
            out_ref[...] += out
            back_ref[...] += back
        shard_ref[j, 0] += grad_up
        shard_ref[j, 1] += grad_low


FF_ROWS, AT_ROWS, FF_FLAT, AT_FLAT = 120, 88, 768, 640
FIRST_ROWS = 256


def send_pieces(pieces, own_ref, sent_refs):
    own_ref[...] = pieces[0]
    for j, sent in enumerate(sent_refs):
        sent[...] = pieces[j + 1].astype(bf16)


def post_kernel(
    place, half, att, wo0, wo1, wo2, wo3, spread1, win0, win1, wout0, win2, win3, wout1,
    hidden_in, inputs_in, douts_in, narrow_in, out_in, back_in,
    ao_in, bo_in, gain_ref, down_in, router_ref, bf_in, up0, low0, up1, low1, group_ref, pick_ref, shard_ref,
    result_out, ghidden_out, gatt_out, prod_out, ao_grad, ff_ref,
    att_scr, spread1_scr, hidden, inputs, douts, narrow, out, back, result, ghidden_scr, gatt, prod,
    ao_scr, bo_scr, wo_scr, down_scr, bf_scr, win_scr, wout_scr,
    shard_acc, pair_acc, bff_acc, bo_acc, ao_acc, gain_acc, pieces, flat, arrived, left,
):
    def copies(pairs, at):
        return [pltpu.make_async_copy(source, goal, arrived.at[at + i]) for i, (source, goal) in enumerate(pairs)]

    early = copies([(inputs_in, inputs), (douts_in, douts)], 0)
    first = shard_copies((win0, win1), (wout0,), half[0], win_scr.at[0], wout_scr.at[0], arrived, 2)
    second = shard_copies((win2, win3), (wout1,), half[0], win_scr.at[1], wout_scr.at[1], arrived, 5)
    sums = copies([(out_in, out), (back_in, back)], 8)
    rest = [(hidden_in, hidden), (narrow_in, narrow), (att, att_scr), (spread1, spread1_scr)]
    rest += [(wo.at[pl.ds(0, 192)], wo_scr.at[pl.ds(192 * j, 192)]) for j, wo in enumerate((wo0, wo1, wo2, wo3))]
    rest = copies(rest, 10)
    start(early[:1] + first + early[1:] + sums + second + rest)
    fill_output_maps(place, ao_in, bo_in, ao_scr, bo_scr)
    down_scr[...] = down_rows([down_in[...]], router_ref[...])
    bf_scr[...] = pad_to(bf_in[...].astype(f32), LANES).astype(bf16)
    fill_adapters(win_scr.at[0], wout_scr.at[0], up0, low0)
    fill_adapters(win_scr.at[1], wout_scr.at[1], up1, low1)
    for j, weights in enumerate((first, second)):
        wait(weights[:2])
        if j == 0:
            wait(early[:1])

        def ready():
            wait(weights[2:])
            if j == 0:
                wait(early[1:])

        more_out, more_back, grad_up, grad_low = feedforward_shard(inputs, douts, win_scr.at[j], wout_scr.at[j], ready)
        if j == 0:
            wait(sums)
        out[...] += more_out
        back[...] += more_back
        shard_acc[j, 0] = grad_up
        shard_acc[j, 1] = grad_low
    wait(rest)
    leaving = []

    def send(scr, goal, where):
        leaving.append(pltpu.make_async_copy(scr.at[where], goal.at[where], left.at[len(leaving)]))
        leaving[-1].start()

    def gather(scr, value, fresh):
        if fresh:
            scr[...] = value
        else:
            scr[...] += value

    def block(i, rows):
        where = pl.ds(HALF_ROWS * i, HALF_ROWS)
        normed, cot = inputs[rows, :MODEL_WIDTH], douts[rows, :MODEL_WIDTH]
        downf, sidei = out[rows, MODEL_WIDTH:], back[rows, MODEL_WIDTH:]
        spread, downi = narrow[rows, :LANES], narrow[rows, LANES : 2 * LANES]
        sidef, downo = narrow[rows, 2 * LANES : 3 * LANES], narrow[rows, 3 * LANES :]
        gates = spread1_scr[rows, :]
        held = hidden[rows, :]
        mixf = (spread * downf).astype(bf16)
        gdowni = (spread * sidei).astype(bf16)
        logit = logit_gradient(downf * sidef + downi * sidei, spread, group_ref[...], pick_ref[...])
        pair = jnp.concatenate([gdowni, logit], 1)
        yield
        grad_normed = back[rows, :MODEL_WIDTH] + nn(pair, down_scr[...])
        result[rows, :] = (held + (out[rows, :MODEL_WIDTH] + nn(mixf, bf_scr[...]))).astype(bf16)
        send(result, result_out, where)
        yield
        scale = lax.rsqrt(jnp.mean(held * held, -1, keepdims=True) + EPS)
        weighted = grad_normed * gain_ref[...].astype(f32)
        inner = jnp.mean(weighted * held, -1, keepdims=True)
        ghidden = cot.astype(f32) + scale * weighted - held * (scale * scale * scale * inner)
        branch = ghidden.astype(bf16)
        ghidden_scr[rows, :] = ghidden
        send(ghidden_scr, ghidden_out, where)
        gather(gain_acc, jnp.sum(grad_normed * held * scale, 0, keepdims=True), i == 0)
        yield
        sideo = nt(branch, bo_scr[...])
        through = nt(branch, wo_scr[...])
        gather(pair_acc, tn(pair, normed), i == 0)
        gather(bff_acc, tn(mixf, cot), i == 0)
        yield
        gdowno = (gates * sideo).astype(bf16)
        prod[rows, :] = downo * sideo
        send(prod, prod_out, where)
        gatt[rows, :] = (through + nn(gdowno, ao_scr[...])).astype(bf16)
        send(gatt, gatt_out, where)
        gather(bo_acc, tn((gates * downo).astype(bf16), branch), i == 0)
        gather(ao_acc, tn(gdowno, att_scr[rows, :]), i == 0)
        yield

    for _ in zip(*[block(i, rows) for i, rows in enumerate(both_blocks())]):
        pass
    ao_grad[...] = ao_acc[:LORA]
    quarters = (pair_acc[:LORA], bff_acc[:LORA], bo_acc[:LORA], router_quarter(pair_acc, gain_acc))
    for j in range(4):
        source, at = (shard_ref, j) if j < 2 else (shard_acc, j - 2)
        pieces[j, 0:LORA] = source[at, 0]
        pieces[j, LORA : 2 * LORA] = source[at, 1]
        pieces[jnp.bitwise_xor(place[0], j), 2 * LORA : 3 * LORA] = quarters[j]
    devices = ff_ref.shape[0]
    rows = FF_FLAT // devices
    flat[6 * FF_ROWS :, :] = jnp.zeros((FF_FLAT - 6 * FF_ROWS, LANES), f32)
    for j in range(4):
        for t in range(6):
            flat[FF_ROWS * t : FF_ROWS * t + FF_ROWS, :] = pieces[j, :, LANES * t : LANES * t + LANES]
        for k in range(devices):
            ff_ref[k, rows * j : rows * j + rows, :] = flat[rows * k : rows * k + rows, :].astype(bf16)
    wait(leaving)


def router_quarter(pair_acc, gain_acc):
    gain = jnp.broadcast_to(gain_acc[...], (8, MODEL_WIDTH))
    return jnp.concatenate([pair_acc[LANES : LANES + 16, :], gain, jnp.zeros((16, MODEL_WIDTH), f32)], 0)


def back_part(
    part, place, lengths, q_ref, k_ref, v_ref, do_ref, lse_ref, tile_ref, map_ref, turn_ref, joined_ref, ups_ref,
    normed_ref, mixed_ref, spread_ref, downs_ref, prod_ref, ghidden_ref, x_ref, gain_ref, downs_in, router_ref,
    group_ref, pick_ref, up_scr, table_scr, sides_scr, side_scr, gnormed, down_scr, gathered, finish,
):
    pair = pl.program_id(0)
    grads = backward_attention(
        part, place, lengths, q_ref, k_ref, v_ref, do_ref, lse_ref, tile_ref, map_ref, turn_ref, table_scr, gathered
    )
    for i, blocks in enumerate(grads):
        for kind in range(3):
            at = LANES * (3 * i + kind)
            sides_scr[:, at : at + LANES] = jnp.concatenate(blocks[kind], 0)
    sides = sides_scr[...]
    joined = joined_ref[...].reshape(-1, MODEL_WIDTH)
    ups = jnp.concatenate([ups_ref[i] for i in range(PAIRS)], 1)
    up_scr[pair] = tn(mixed_ref[...], sides)

    @pl.when(pair == 0)
    def _():
        gnormed[...] = nn(sides, joined)
        side_scr[...] = nt(sides, ups)

    @pl.when(pair > 0)
    def _():
        gnormed[...] += nn(sides, joined)
        side_scr[...] += nt(sides, ups)

    @pl.when(pair == pl.num_programs(0) - 1)
    def _():
        down_scr[...] = down_rows([downs_in[0], downs_in[1], downs_in[2]], router_ref[...])
        side = side_scr[...]
        spread = spread_ref[...]
        gdown = (spread * side).astype(bf16)
        gates = jnp.where(lane_index(spread.shape) < LORA, spread, 0.0)
        logit = logit_gradient(downs_ref[...] * side + prod_ref[...], gates, group_ref[...], pick_ref[...])
        both = jnp.concatenate([gdown, logit], 1)
        grad_normed = gnormed[...] + nn(both, down_scr[...])
        x = x_ref[...].astype(f32)
        scale = lax.rsqrt(jnp.mean(x * x, -1, keepdims=True) + EPS)
        weighted = grad_normed * gain_ref[...].astype(f32)
        inner = jnp.mean(weighted * x, -1, keepdims=True)
        gtokens = (ghidden_ref[...] + scale * weighted - x * (scale * scale * scale * inner)).astype(bf16)
        finish(gtokens, tn(both, normed_ref[...]), jnp.sum(grad_normed * x * scale, 0, keepdims=True))


def short_kernel(*refs):
    ins, outs, scratch = refs[:24], refs[24:30], refs[30:]
    ga_ref, gb_ref, up_ref, pair_ref, ggain_ref, table_ref = outs

    def finish(gtokens, pair_grad, ggain):
        ga_ref[...] = gtokens[:FIRST_ROWS]
        gb_ref[...] = gtokens[FIRST_ROWS:]
        pair_ref[...] = pair_grad
        ggain_ref[...] = ggain

    back_part(0, *ins, up_ref, table_ref, *scratch, None, finish)


def long_kernel(*refs):
    place, ins, more, outs, scratch = refs[0], refs[:24], refs[24:30], refs[30:36], refs[36:]
    ao_grad, up_in, pair_in, ggain_in, table_in, gb_in = more
    gtokens_ref, ggain_ref, own_ref, sent1, sent2, sent3 = outs
    up_scr, table_scr, pair_acc, pieces = scratch[:4]

    def finish(gtokens, pair_grad, ggain):
        gtokens_ref[: HALF_ROWS - FIRST_ROWS, :] = gb_in[...]
        gtokens_ref[HALF_ROWS - FIRST_ROWS :, :] = gtokens
        ggain_ref[...] = ggain + ggain_in[...]
        pair_acc[...] = pair_grad + pair_in[...]
        quarters = (
            pair_acc[0:LORA],
            pair_acc[LORA : 2 * LORA],
            pair_acc[2 * LORA : 3 * LORA],
            jnp.concatenate([pair_acc[LANES : LANES + 16, :], jnp.zeros((24, MODEL_WIDTH), f32)], 0),
        )
        ups = []
        for half in range(2):
            for part in range(3):
                rows, pairs = slice(LORA * part, LORA * part + LORA), []
                for p in range(3 * half, 3 * half + 3):
                    cols = slice(384 * (p % PAIRS) + LANES * part, 384 * (p % PAIRS) + LANES * part + LANES)
                    pairs.append(up_scr[p // PAIRS, rows, cols] + up_in[p // PAIRS, rows, cols])
                ups.append(jnp.concatenate(pairs, 1))
        for j in range(4):
            half, odd = j // 2, j % 2
            parts = [ao_grad[:, 192 * j : 192 * j + 192]]
            parts += [ups[3 * half + part][:, 192 * odd : 192 * odd + 192] for part in range(3)]
            pieces[j, 0:LORA] = jnp.concatenate(parts, 1)
            pieces[jnp.bitwise_xor(place[0], j), LORA : 2 * LORA] = quarters[j]
            heads = [3 * j + i for i in range(3)]
            rows = []
            for head in heads:
                step, row = head // (2 * PAIRS), head % (2 * PAIRS)
                rows.append(table_scr[step, row : row + 1, :] + table_in[step, row : row + 1, :])
            rows = jnp.concatenate(rows + [jnp.zeros((5, LANES), f32)], 0)
            pieces[j, 2 * LORA : 2 * LORA + 8] = jnp.concatenate([rows, jnp.zeros((8, MODEL_WIDTH - LANES), f32)], 1)
        send_pieces(pieces, own_ref, (sent1, sent2, sent3))

    back_part(1, *ins, up_scr, table_scr, *scratch[4:8], scratch[8:], finish)


def spread_kernel(place, *refs):
    out_ref, held, arrived, left = refs[-4:]
    count = (len(refs) - 4) // 4
    inward, outward = [], []
    for j in range(4):
        there = jnp.bitwise_xor(place[0], j)
        first = 0
        for source in refs[count * j : count * j + count]:
            rows = pl.ds(first, source.shape[0])
            inward.append(pltpu.make_async_copy(source, held.at[j, rows], arrived.at[len(inward)]))
            first += source.shape[0]
        for part in range(2):
            rows = pl.ds(HALF_ROWS * part, HALF_ROWS)
            goal = pl.ds(pl.multiple_of(HALF_ROWS * (4 * part + there), HALF_ROWS), HALF_ROWS)
            outward.append(pltpu.make_async_copy(held.at[j, rows], out_ref.at[goal], left.at[2 * j + part]))
    for copy in inward:
        copy.start()
    for j in range(4):
        for copy in inward[count * j : count * j + count]:
            copy.wait()
        for copy in outward[2 * j : 2 * j + 2]:
            copy.start()
    for copy in outward:
        copy.wait()


def sum_kernel(at0, at1, at2, at3, ggain, flat):
    at = at0[...] + at1[...].astype(f32) + at2[...].astype(f32) + at3[...].astype(f32)
    at = at.astype(bf16)
    for t in range(6):
        flat[AT_ROWS * t : AT_ROWS * t + AT_ROWS, :] = at[:, LANES * t : LANES * t + LANES]
    gain = jnp.concatenate([ggain[:, LANES * t : LANES * t + LANES] for t in range(6)], 0)
    flat[6 * AT_ROWS :, :] = pad_to(gain, AT_FLAT - 6 * AT_ROWS).astype(bf16)


def unpack_kernel(
    place, own, one, two, three, gain1_ref, gain2_ref, qkv_ref, bq_ref, bkv_ref, ao_ref, bo_ref, ai_ref, bi_ref,
    aff_ref, bff_ref, r1_ref, r2_ref, table_ref, quarters2, quarters1, ffs, ats,
):
    devices = own.shape[0]
    ff_rows, at_rows = FF_FLAT // devices, AT_FLAT // devices
    for j, ref in enumerate((own, one, two, three)):
        for k in range(devices):
            both = ref[k].astype(f32)
            ffs[j, ff_rows * k : ff_rows * k + ff_rows, :] = both[:ff_rows]
            ats[j, at_rows * k : at_rows * k + at_rows, :] = both[ff_rows:]

    def piece(scr, j, height, first, count):
        return jnp.concatenate([scr[j, height * t + first : height * t + first + count, :] for t in range(6)], 1)

    m = place[0]
    bi_ref[...] = piece(ffs, 0, FF_ROWS, 0, LORA)
    mine = piece(ats, 0, AT_ROWS, 0, LORA)
    bq_ref[...] = mine[:, 192:384]
    bkv_ref[0] = mine[:, 384:576]
    bkv_ref[1] = mine[:, 576:768]
    table_ref[...] = ats[0, 2 * LORA : 2 * LORA + 3, :BUCKETS]
    for j in range(4):
        there = jnp.bitwise_xor(m, j)
        quarters2[there] = piece(ffs, j, FF_ROWS, 2 * LORA, LORA)
        quarters1[there] = piece(ats, j, AT_ROWS, LORA, LORA)
        low = piece(ffs, j, FF_ROWS, LORA, LORA)
        out = piece(ats, j, AT_ROWS, 0, LORA)[:, :192]
        for at in range(4):

            @pl.when(there == at)
            def _():
                aff_ref[:, MODEL_WIDTH * at : MODEL_WIDTH * at + MODEL_WIDTH] = low
                ao_ref[:, 192 * at : 192 * at + 192] = out

    for part in range(3):
        qkv_ref[part] = quarters1[part]
    ai_ref[...] = quarters2[0]
    bff_ref[...] = quarters2[1]
    bo_ref[...] = quarters2[2]
    r1_ref[...] = quarters1[3, :EXPERTS]
    r2_ref[...] = quarters2[3, :EXPERTS]
    total = jnp.zeros((8, LANES), f32)
    for j in range(4):
        total = total + ats[j, 6 * AT_ROWS : 6 * AT_ROWS + 8, :]
    gain1_ref[...] = total[:6]
    gain2_ref[...] = jnp.concatenate([quarters2[3, 16:17, LANES * t : LANES * t + LANES] for t in range(6)], 0)


def whole(array):
    return pl.BlockSpec(array.shape, lambda *_: (0,) * array.ndim)


def rows_block(array):
    return pl.BlockSpec((HALF_ROWS, array.shape[1]), lambda i, *_: (i, 0))


def token_block():
    return pl.BlockSpec((HALF_ROWS, MODEL_WIDTH), lambda i, place, *_: (place[0] + 4 * i, 0))


def shape(dims, dtype):
    return jax.ShapeDtypeStruct(dims, dtype)


def call(kernel, grid, scalars, inputs, in_specs, outs, out_specs, scratch=(), aliases=None, flops=0):
    return pl.pallas_call(
        kernel,
        grid_spec=pltpu.PrefetchScalarGridSpec(
            num_scalar_prefetch=len(scalars),
            grid=grid,
            in_specs=in_specs,
            out_specs=out_specs,
            scratch_shapes=list(scratch),
        ),
        out_shape=outs,
        input_output_aliases=aliases or {},
        compiler_params=pltpu.CompilerParams(vmem_limit_bytes=VMEM_LIMIT),
        cost_estimate=pl.CostEstimate(flops=flops, bytes_accessed=0, transcendentals=0),
    )(*scalars, *inputs)


def exchange(value, axis, size, mask):
    return lax.ppermute(value, axis, [(i, i ^ mask) for i in range(size)])


def scatter_over(flat, axis, size):
    pieces = lax.all_to_all(flat.reshape(size, -1, flat.shape[-1]), axis, 0, 0)
    return jnp.sum(pieces.astype(f32), 0)


def gather_over(mine, axis, size):
    return lax.all_to_all(jnp.broadcast_to(mine[None], (size,) + mine.shape), axis, 0, 0)


def constants():
    group1 = np.zeros((LANES, LANES), np.float32)
    for i in range(3 * LORA):
        for j in range(LORA):
            group1[i, j] = float((i % LORA) // ADAPTER_RANK == j // ADAPTER_RANK)
    pick = np.zeros((LANES, LANES), np.float32)
    for e in range(EXPERTS):
        pick[ADAPTER_RANK * e, e] = 1.0
    turn = np.eye(LANES, dtype=np.float32)[::-1].copy()
    return tuple(jnp.asarray(c, bf16) for c in (group1, pick, turn))


def local(
    dp_size,
    mp_size,
    tokens,
    cotangent,
    attention_norm_gain,
    feedforward_norm_gain,
    query_projection_weight,
    key_value_weight,
    attention_output_weight,
    ffn_input_weight,
    ffn_output_weight,
    projection_down_weight,
    query_up_weight,
    key_value_up_weight,
    attention_output_down_weight,
    attention_output_up_weight,
    ffn_input_down_weight,
    ffn_input_up_weight,
    ffn_output_down_weight,
    ffn_output_up_weight,
    attention_router_weight,
    feedforward_router_weight,
    bucket_bias_table,
    offset_bucket_map,
    sequence_length_list,
):
    m = lax.axis_index("mp").astype(jnp.int32)
    d = lax.axis_index("dp").astype(jnp.int32)
    place = m.reshape(1)
    group, pick, turn = constants()

    def mp_swap(value, mask):
        return exchange(value, "mp", mp_size, mask)

    def pack_part(rows, index):
        return pl.BlockSpec((rows, MODEL_WIDTH), lambda *_: (index, 0))

    def element_part(rows, first):
        return pl.BlockSpec((pl.Element(rows), pl.Element(MODEL_WIDTH)), lambda *_: (first, 0))

    win0, wout0 = ffn_input_weight, ffn_output_weight
    half = (d & 1).reshape(1)
    inputs = [
        query_projection_weight.T,
        jnp.transpose(key_value_weight, (0, 2, 1)),
        query_up_weight,
        key_value_up_weight,
        bucket_bias_table.T,
        attention_output_weight,
        ffn_input_up_weight,
        win0,
    ]
    outs = [
        shape((rows, MODEL_WIDTH), bf16)
        for rows in (QK_ROWS, V_ROWS, SECOND_ROWS + HALF_SHARD, SECOND_ROWS + QK_ROWS + V_ROWS)
    ]
    *pack0, more0, both0 = call(
        pack_kernel,
        (1,),
        [half],
        inputs,
        [whole(a) for a in inputs[:-1]] + [pl.BlockSpec((HALF_SHARD, MODEL_WIDTH), lambda i, half: (half[0], 0))],
        outs,
        [whole(o) for o in outs],
    )
    pack2 = [mp_swap(p, 2) for p in pack0]
    both1 = mp_swap(both0, 1)
    more2 = mp_swap(more0, 2)
    wout2 = mp_swap(wout0, 2)

    gain1 = attention_norm_gain.reshape(1, -1)
    gain2 = feedforward_norm_gain.reshape(1, -1)
    downs_in = jnp.transpose(projection_down_weight, (0, 2, 1))
    router1, router2 = attention_router_weight.T, feedforward_router_weight.T
    rev_map = jnp.concatenate([offset_bucket_map[::-1], jnp.full((1,), -1, jnp.int32)]).reshape(1, -1)

    wide, narrow = shape((ROWS, MODEL_WIDTH), bf16), shape((ROWS, LANES), f32)
    narrow16 = shape((ROWS, LANES), bf16)

    joined_shape, ups_shape = shape((6, 384, MODEL_WIDTH), bf16), shape((6, LANES, 384), bf16)
    pair_outs = [wide, wide, wide, wide, shape((6, 8, 256), f32), shape((6, 7, LANES, 256), bf16), joined_shape, ups_shape]

    def pair_specs(first):
        specs = [pl.BlockSpec((ROWS, LANES), lambda p, *_: (0, first + p))] * 4
        for o in pair_outs[4:]:
            specs.append(pl.BlockSpec((1,) + o.shape[1:], lambda p, *_, n=len(o.shape): (first + p,) + (0,) * (n - 1)))
        return specs

    def half_of_rows(part):
        return pl.BlockSpec((HALF_ROWS, MODEL_WIDTH), lambda p, place, *_: (place[0] + 4 * part, 0))

    joined_scratch = [pltpu.VMEM((3, 384, MODEL_WIDTH), bf16), pltpu.VMEM((3, LANES, 384), bf16)]
    fixed = [wide, narrow16, narrow, narrow]
    *pair_state, normed1, mixed1, spread1, downs1 = call(
        first_kernel,
        (3,),
        [place, sequence_length_list],
        [tokens, tokens, gain1, downs_in, router1, *pack0, pack0[1], both1, both1, rev_map],
        [half_of_rows(0), half_of_rows(1), whole(gain1), whole(downs_in), whole(router1)]
        + [pack_part(384, 0), pack_part(192, 0), pack_part(48, 4), element_part(576, 240), pack_part(48, 17)]
        + [whole(rev_map)],
        pair_outs + fixed,
        pair_specs(0) + [whole(o) for o in fixed],
        scratch=joined_scratch + [pltpu.VMEM((256, MODEL_WIDTH), bf16)],
    )
    win1, wout1 = mp_swap(win0, 1), mp_swap(wout0, 1)
    pack2, normed1, win1, wout1 = lax.optimization_barrier((pack2, normed1, win1, wout1))
    pack3 = [mp_swap(p, 1) for p in pack2]
    inputs = [normed1, mixed1, *pack2, pack2[1], *pack3, pack3[1], rev_map]
    queries, keys, all_values, attended, lse, tiles, joined, ups = call(
        second_kernel,
        (3,),
        [place, sequence_length_list],
        inputs + pair_state,
        [whole(normed1), whole(mixed1)]
        + [pack_part(384, 0), pack_part(192, 0), pack_part(48, 4)] * 2
        + [whole(rev_map)]
        + [pl.BlockSpec(memory_space=pl.ANY)] * 8,
        pair_outs,
        pair_specs(3),
        scratch=joined_scratch,
        aliases={2 + len(inputs) + i: i for i in range(8)},
    )

    attended, more2 = lax.optimization_barrier((attended, more2))
    more3 = mp_swap(more2, 1)
    other2 = exchange(more2, "dp", dp_size, 1)
    mores = [more0, both1, more2, more3]
    ao_in, bo_in, bf_in = attention_output_down_weight.T, attention_output_up_weight, ffn_output_up_weight
    down_in, low_in = ffn_input_down_weight.T, ffn_output_down_weight.T

    def low_block(j):
        return pl.BlockSpec((LORA, MODEL_WIDTH), lambda i, place, *_: (0, jnp.bitwise_xor(place[0], j)))

    def small_inputs(first):
        values = [ao_in, bo_in, gain2, down_in, router2, bf_in]
        specs = [whole(a) for a in values]
        for j in (first, first + 1):
            values += [mores[j], low_in]
            specs += [pack_part(48, 4), low_block(j)]
        return values, specs

    hbm = pl.BlockSpec(memory_space=pltpu.HBM)
    shard_shape = shape((2, 2, LORA, MODEL_WIDTH), f32)
    wide_f32, wider, wider_f32 = shape((ROWS, MODEL_WIDTH), f32), shape((ROWS, WIDER), bf16), shape((ROWS, WIDER), f32)
    state_shapes = [wide_f32, wider, wider, shape((ROWS, 4 * LANES), f32), wider_f32, wider_f32]

    def held(array):
        return pltpu.VMEM(array.shape, array.dtype)

    map_scratch = [
        pltpu.VMEM((LANES, MODEL_WIDTH), bf16),
        pltpu.VMEM((LANES, MODEL_WIDTH), bf16),
        pltpu.VMEM((MODEL_WIDTH, MODEL_WIDTH), bf16),
        pltpu.VMEM((256, MODEL_WIDTH), bf16),
        pltpu.VMEM((LANES, MODEL_WIDTH), bf16),
        pltpu.VMEM((2, WIDER, MODEL_WIDTH), bf16),
        pltpu.VMEM((2, MODEL_WIDTH, WIDER), bf16),
    ]
    values, specs = small_inputs(0)
    inputs = [tokens, cotangent, attended] + mores + [spread1, win0, wout0, win1, wout1]
    *state, shard_grads = call(
        middle_kernel,
        (2,),
        [place],
        inputs + values,
        [token_block(), token_block(), rows_block(attended)]
        + [pack_part(192, 0)] * 4
        + [rows_block(spread1)]
        + [whole(a) for a in inputs[-4:]]
        + specs,
        state_shapes + [shard_shape],
        [rows_block(a) for a in state_shapes] + [whole(shard_shape)],
        scratch=map_scratch,
    )
    state[0], other2, wout2 = lax.optimization_barrier((state[0], other2, wout2))
    other3 = mp_swap(other2, 1)
    wout3 = mp_swap(wout2, 1)
    values, specs = small_inputs(2)
    ao_shape = shape((LORA, MODEL_WIDTH), f32)
    ff_shape = shape((dp_size, 4 * FF_FLAT // dp_size, LANES), bf16)
    inputs = [attended] + mores + [spread1, more2, other2, wout2, more3, other3, wout3] + state
    values += [group, pick, shard_grads]
    specs += [whole(a) for a in (group, pick, shard_grads)]
    outs = [wide, wide_f32, wide, narrow, ao_shape, ff_shape]
    result, ghidden, gatt, prod, ao_grad, ff_flat = call(
        post_kernel,
        (1,),
        [place, half],
        inputs + values,
        [hbm] * len(inputs) + specs,
        outs,
        [hbm] * 4 + [whole(o) for o in outs[4:]],
        scratch=[held(wide), held(narrow)]
        + [held(a) for a in state_shapes]
        + [held(wide), held(wide_f32), held(wide), held(narrow)]
        + map_scratch
        + [
            pltpu.VMEM((2, 2, LORA, MODEL_WIDTH), f32),
            pltpu.VMEM((256, MODEL_WIDTH), f32),
            pltpu.VMEM((LANES, MODEL_WIDTH), f32),
            pltpu.VMEM((LANES, MODEL_WIDTH), f32),
            pltpu.VMEM((LANES, MODEL_WIDTH), f32),
            pltpu.VMEM((1, MODEL_WIDTH), f32),
            pltpu.VMEM((4, FF_ROWS, MODEL_WIDTH), f32),
            pltpu.VMEM((FF_FLAT, LANES), f32),
            pltpu.SemaphoreType.DMA((18,)),
            pltpu.SemaphoreType.DMA((8,)),
        ],
    )
    result2 = mp_swap(result, 2)
    ff_pieces = lax.all_to_all(ff_flat, "dp", 0, 0)

    at_shapes = [shape((AT_ROWS, MODEL_WIDTH), f32)] + [shape((AT_ROWS, MODEL_WIDTH), bf16)] * 3
    gain_shape, up_shape = shape((1, MODEL_WIDTH), f32), shape((6 // PAIRS, LANES, 384 * PAIRS), f32)
    pair_shape, table_shape = shape((256, MODEL_WIDTH), f32), shape((6 // PAIRS, 8, LANES), f32)

    def part_call(kernel, part, more, outs, scratch):
        def block(array):
            return pl.BlockSpec((HALF_ROWS, array.shape[1]), lambda p, *_: (part, 0))

        pair = [pl.BlockSpec((HALF_ROWS, PAIRS * LANES), lambda p, *_: (part, p))] * 4
        if part == 0:
            tile = pl.BlockSpec((PAIRS, 1, LANES, 256), lambda p, *_: (p, 3, 0, 0))
        else:
            tile = pl.BlockSpec((PAIRS, 7, LANES, 256), lambda p, *_: (p, 0, 0, 0))
        three = [pl.BlockSpec((PAIRS,) + a.shape[1:], lambda p, *_: (p, 0, 0)) for a in (lse, joined, ups)]
        by_rows = [normed1, mixed1, spread1, downs1, prod, ghidden]
        fixed = [gain1, downs_in, router1, group, pick] + more
        return call(
            kernel,
            (6 // PAIRS,),
            [place, sequence_length_list],
            [queries, keys, all_values, gatt, lse, tiles, rev_map, turn, joined, ups] + by_rows + [tokens] + fixed,
            pair
            + [three[0], tile, whole(rev_map), whole(turn)]
            + three[1:]
            + [block(a) for a in by_rows]
            + [half_of_rows(part)]
            + [whole(a) for a in fixed],
            outs,
            [whole(o) for o in outs],
            scratch=scratch
            + [
                pltpu.VMEM((HALF_ROWS, 384 * PAIRS), bf16),
                pltpu.VMEM((HALF_ROWS, LANES), f32),
                pltpu.VMEM((HALF_ROWS, MODEL_WIDTH), f32),
                pltpu.VMEM((256, MODEL_WIDTH), bf16),
            ]
            + (
                [pltpu.VMEM((PAIRS, LONG_LEN, 1024), bf16)] * 2 + [pltpu.VMEM((PAIRS, 1024, LANES), bf16)] * 2
                if part == 1
                else []
            ),
        )

    early_shape = shape((FIRST_ROWS, MODEL_WIDTH), bf16)
    rest_shape = shape((ROWS - FIRST_ROWS, MODEL_WIDTH), bf16)
    gearly, *short_grads = part_call(
        short_kernel,
        0,
        [],
        [early_shape, shape((HALF_ROWS - FIRST_ROWS, MODEL_WIDTH), bf16), up_shape, pair_shape, gain_shape, table_shape],
        [],
    )
    gearly2 = mp_swap(gearly, 2)
    grest, ggain, *at_pieces = part_call(
        long_kernel,
        1,
        [ao_grad] + short_grads[1:] + short_grads[:1],
        [rest_shape, gain_shape] + at_shapes,
        [held(up_shape), held(table_shape), held(pair_shape), pltpu.VMEM((4, AT_ROWS, MODEL_WIDTH), f32)],
    )
    result2, gearly2, at_pieces, ff_pieces, ggain = lax.optimization_barrier(
        (result2, gearly2, at_pieces, ff_pieces, ggain)
    )
    at_parts = [at_pieces[0]] + [mp_swap(at_pieces[j], j) for j in (1, 2, 3)]
    ff_sums = jnp.sum(ff_pieces.astype(f32), 0).reshape(4, -1, LANES)
    ff_sum = ff_sums[0]
    for j in (1, 2, 3):
        ff_sum = ff_sum + mp_swap(ff_sums[j].astype(bf16), j).astype(f32)
    grest, at_parts, ff_sum = lax.optimization_barrier((grest, at_parts, ff_sum))
    grest2 = mp_swap(grest, 2)

    def spread_rows(*parts):
        return call(
            spread_kernel,
            (1,),
            [place],
            list(parts),
            [hbm] * len(parts),
            shape((4 * ROWS, MODEL_WIDTH), bf16),
            hbm,
            scratch=[
                pltpu.VMEM((4, ROWS, MODEL_WIDTH), bf16),
                pltpu.SemaphoreType.DMA((len(parts),)),
                pltpu.SemaphoreType.DMA((8,)),
            ],
        )

    parts = at_parts + [ggain]
    flat_shape = shape((AT_FLAT, LANES), bf16)
    flat = call(sum_kernel, (1,), [], parts, [whole(a) for a in parts], flat_shape, whole(flat_shape))
    flat, result2 = lax.optimization_barrier((flat, result2))
    result1, result3 = mp_swap(result, 1), mp_swap(result2, 1)
    at_sum = scatter_over(flat, "dp", dp_size)
    own = gather_over(jnp.concatenate([ff_sum, at_sum], 0).astype(bf16), "dp", dp_size)
    output = spread_rows(result, result1, result2, result3)
    own, output, grest2 = lax.optimization_barrier((own, output, grest2))
    two = mp_swap(own, 2)
    one = mp_swap(own, 1)
    gearly1, gearly3, grest1, grest3 = mp_swap(gearly, 1), mp_swap(gearly2, 1), mp_swap(grest, 1), mp_swap(grest2, 1)
    grad_tokens = spread_rows(gearly, grest, gearly1, grest1, gearly2, grest2, gearly3, grest3)
    two, grad_tokens = lax.optimization_barrier((two, grad_tokens))
    three = mp_swap(two, 1)
    outs = [
        shape((6, LANES), f32),
        shape((6, LANES), f32),
        shape((3, LORA, MODEL_WIDTH), f32),
        shape((LORA, 192), f32),
        shape((2, LORA, 192), f32),
        shape((LORA, MODEL_WIDTH), f32),
        shape((LORA, MODEL_WIDTH), f32),
        shape((LORA, MODEL_WIDTH), f32),
        shape((LORA, MODEL_WIDTH), f32),
        shape((LORA, 4 * MODEL_WIDTH), f32),
        shape((LORA, MODEL_WIDTH), f32),
        shape((EXPERTS, MODEL_WIDTH), f32),
        shape((EXPERTS, MODEL_WIDTH), f32),
        shape((3, BUCKETS), f32),
    ]
    flats = [own, one, two, three]
    grads = call(
        unpack_kernel,
        (1,),
        [place],
        flats,
        [whole(a) for a in flats],
        outs,
        [whole(o) for o in outs],
        scratch=[pltpu.VMEM((4, LORA, MODEL_WIDTH), f32)] * 2
        + [pltpu.VMEM((4, FF_FLAT, LANES), f32), pltpu.VMEM((4, AT_FLAT, LANES), f32)],
    )
    g1, g2, g_qkv, g_bq, g_bkv, g_ao, g_bo, g_ai, g_bi, g_aff, g_bff, g_r1, g_r2, g_table = grads
    return (
        output,
        grad_tokens,
        g1.reshape(-1),
        g2.reshape(-1),
        jnp.transpose(g_qkv, (0, 2, 1)),
        g_bq,
        g_bkv,
        g_ao.T,
        g_bo,
        g_ai.T,
        g_bi,
        g_aff.T,
        g_bff,
        g_r1.T,
        g_r2.T,
        g_table.T,
    )


def solution(mesh):
    in_specs = (
        P("dp", None),
        P("dp", None),
        P(),
        P(),
        P(None, "mp"),
        P(None, None, "mp"),
        P("mp", None),
        P(None, "mp"),
        P("mp", None),
        P(),
        P(None, "mp"),
        P(None, None, "mp"),
        P(),
        P(),
        P(),
        P(None, "mp"),
        P(),
        P(),
        P(),
        P(),
        P(None, "mp"),
        P(),
        P("dp"),
    )
    out_specs = (
        P("dp", None),
        P("dp", None),
        P(),
        P(),
        P(),
        P(None, "mp"),
        P(None, None, "mp"),
        P(),
        P(),
        P(),
        P(None, "mp"),
        P(),
        P(),
        P(),
        P(),
        P(None, "mp"),
    )
    step = functools.partial(local, mesh.shape["dp"], mesh.shape["mp"])
    return jax.shard_map(step, mesh=mesh, in_specs=in_specs, out_specs=out_specs, check_vma=False)
```

```python
import functools

import jax
import jax.numpy as jnp
import numpy as np
from jax import lax
from jax.experimental import pallas as pl
from jax.experimental.pallas import tpu as pltpu
from jax.sharding import PartitionSpec as P

HEAD_WIDTH = 64
BUCKETS = 32
ADAPTER_RANK = 4
SHORT_LEN = 128
LONG_LEN = 512
LONG_SEQS = 4
SHORT_SEQS = 16
MODEL_WIDTH = 768
LORA = 40
EXPERTS = 10
LANES = 128
HALF_ROWS = 512
ROWS = 1024
EPS = 1e-06
NEG = -1e9

bf16 = jnp.bfloat16
f32 = jnp.float32
VMEM_LIMIT = 56 * 1024 * 1024


def nn(a, b):
    return jnp.dot(a, b, preferred_element_type=f32)


def nt(a, b):
    return lax.dot_general(a, b, (((1,), (1,)), ((), ())), preferred_element_type=f32)


def tn(a, b):
    return lax.dot_general(a, b, (((0,), (0,)), ((), ())), preferred_element_type=f32)


def lane_index(shape):
    return lax.broadcasted_iota(jnp.int32, shape, 1)


def softmax_repeated(logits, valid, repeats):
    logits = jnp.where(lane_index(logits.shape) < valid, logits, -1e30)
    raised = jnp.exp(logits - jnp.max(logits, -1, keepdims=True))
    return raised * (repeats / jnp.sum(raised, -1, keepdims=True))


def logit_gradient(products, gates, group, pick):
    high = products.astype(bf16)
    low = (products - high.astype(f32)).astype(bf16)
    gate_grad = nn(high, group) + nn(low, group)
    inner = jnp.sum(gates * gate_grad, -1, keepdims=True) * (1.0 / ADAPTER_RANK)
    logit_grad = (gates * (gate_grad - inner)).astype(bf16)
    return nn(logit_grad, pick).astype(bf16)


QK_ROWS, V_ROWS, SECOND_ROWS, HALF_SHARD = 384, 240, 240, 384


def pack_kernel(half, q_ref, kv_ref, qup_ref, kvup_ref, table_ref, wo_ref, up_ref, win_ref, qk_ref, v_ref, second_ref, both_ref):
    qk_ref[0:192, :] = q_ref[...]
    qk_ref[192:384, :] = kv_ref[0]
    v_ref[0:192, :] = kv_ref[1]
    ups = jnp.concatenate([qup_ref[...], kvup_ref[0], kvup_ref[1], jnp.zeros((LORA, 192), bf16)], 1).astype(f32)
    table = jnp.pad(table_ref[...].astype(f32), ((0, 5), (0, MODEL_WIDTH - BUCKETS)))
    v_ref[192:240, :] = jnp.concatenate([ups, table], 0).astype(bf16)
    second_ref[0:192, :] = wo_ref[...]
    second_ref[192:240, :] = jnp.pad(up_ref[...].astype(f32), ((0, 8), (0, 0))).astype(bf16)
    second_ref[240:, :] = win_ref[...]
    both_ref[:SECOND_ROWS, :] = second_ref[:SECOND_ROWS, :]
    both_ref[SECOND_ROWS : SECOND_ROWS + QK_ROWS, :] = qk_ref[...]
    both_ref[SECOND_ROWS + QK_ROWS :, :] = v_ref[...]


def pad_to(rows, count):
    if rows.shape[0] == count:
        return rows
    return jnp.concatenate([rows, jnp.zeros((count - rows.shape[0], rows.shape[1]), rows.dtype)], 0)


def repeated_router(router, copies):
    rows = lax.broadcasted_iota(jnp.int32, (LANES, EXPERTS), 0)
    first = ADAPTER_RANK * lax.broadcasted_iota(jnp.int32, (LANES, EXPERTS), 1)
    hot = jnp.zeros((LANES, EXPERTS), jnp.bool_)
    for c in range(copies):
        hot = hot | ((rows >= LORA * c + first) & (rows < LORA * c + first + ADAPTER_RANK))
    return nn(hot.astype(bf16), router).astype(bf16)


def down_rows(downs, router_rows):
    downs = pad_to(jnp.concatenate([part.astype(f32) for part in downs], 0), LANES)
    return jnp.concatenate([downs, pad_to(router_rows.astype(f32), LANES)], 0).astype(bf16)


def weight_rows(refs, part):
    if len(refs) == 1:
        return refs[0].at[192 * part : 192 * part + 192]
    return refs[1].at[0:192] if part == 2 else refs[0].at[192 * part : 192 * part + 192]


def join_packs(one, two, ups_one, ups_two, joined_scr, ups_scr):
    for part in range(3):
        at = LANES * part
        one_ref, two_ref = weight_rows(one, part), weight_rows(two, part)
        joined_scr[0, at : at + LANES, :] = one_ref[0:LANES, :]
        joined_scr[1, at : at + 64, :] = one_ref[LANES:192, :]
        joined_scr[1, at + 64 : at + LANES, :] = two_ref[0:64, :]
        joined_scr[2, at : at + LANES, :] = two_ref[64:192, :]
    pieces = []
    for part in range(3):
        cols = slice(192 * part, 192 * part + 192)
        pieces.append(jnp.concatenate([ups_one[:LORA, cols], ups_two[:LORA, cols]], 1).astype(f32))
    zero = jnp.zeros((LORA, LANES), f32)
    for pair in range(3):
        rows = []
        for part in range(3):
            piece = pieces[part][:, LANES * pair : LANES * pair + LANES]
            rows.append(jnp.concatenate([piece if p == part else zero for p in range(3)], 1))
        ups_scr[pair] = pad_to(jnp.concatenate(rows, 0), LANES).astype(bf16)


def project_pair(normed_ref, mixed_ref, joined_scr, ups_scr, q_ref, k_ref, v_ref, joined_ref, ups_ref):
    pair = pl.program_id(0)
    joined, ups = joined_scr[pair], ups_scr[pair]
    joined_ref[0] = joined
    ups_ref[0] = ups
    for first in (0, HALF_ROWS):
        rows = slice(first, first + HALF_ROWS)
        result = (nt(normed_ref[rows, :], joined) + nn(mixed_ref[rows, :], ups)).astype(bf16)
        q_ref[rows, :] = result[:, :LANES]
        k_ref[rows, :] = result[:, LANES : 2 * LANES]
        v_ref[rows, :] = result[:, 2 * LANES :]


def first_kernel(
    place, lengths, xs_ref, xl_ref, gain_ref, downs_in, router_ref, one_qk, one_v, ups_one, two_ref, ups_two, map_ref,
    q_ref, k_ref, v_ref, o_ref, lse_ref, tile_ref, joined_ref, ups_ref, normed_ref, mixed_ref, spread_ref, downs_ref,
    joined_scr, ups_scr, down_scr,
):
    @pl.when(pl.program_id(0) == 0)
    def _():
        join_packs((one_qk, one_v), (two_ref,), ups_one, ups_two, joined_scr, ups_scr)
        down_scr[...] = down_rows([downs_in[0], downs_in[1], downs_in[2]], repeated_router(router_ref[...], 3))
        for x_ref, first in ((xs_ref, 0), (xl_ref, HALF_ROWS)):
            rows = slice(first, first + HALF_ROWS)
            x = x_ref[...].astype(f32)
            scale = lax.rsqrt(jnp.mean(x * x, -1, keepdims=True) + EPS)
            normed = (x * scale * gain_ref[...].astype(f32)).astype(bf16)
            normed_ref[rows, :] = normed
            both = nt(normed, down_scr[...])
            downs = both[:, :LANES]
            spread = softmax_repeated(both[:, LANES:], 3 * LORA, 3.0 * ADAPTER_RANK)
            mixed_ref[rows, :] = (spread * downs).astype(bf16)
            spread_ref[rows, :] = spread
            downs_ref[rows, :] = downs

    project_pair(normed_ref, mixed_ref, joined_scr, ups_scr, q_ref, k_ref, v_ref, joined_ref, ups_ref)
    forward_attention(place, lengths, q_ref, k_ref, v_ref, ups_one, ups_two, map_ref, o_ref, lse_ref, tile_ref)


def second_kernel(
    place, lengths, normed_ref, mixed_ref, one_qk, one_v, ups_one, two_qk, two_v, ups_two, map_ref,
    q_in, k_in, v_in, o_in, lse_in, tile_in, joined_in, ups_in,
    q_ref, k_ref, v_ref, o_ref, lse_ref, tile_ref, joined_ref, ups_ref, joined_scr, ups_scr,
):
    @pl.when(pl.program_id(0) == 0)
    def _():
        join_packs((one_qk, one_v), (two_qk, two_v), ups_one, ups_two, joined_scr, ups_scr)

    project_pair(normed_ref, mixed_ref, joined_scr, ups_scr, q_ref, k_ref, v_ref, joined_ref, ups_ref)
    forward_attention(place, lengths, q_ref, k_ref, v_ref, ups_one, ups_two, map_ref, o_ref, lse_ref, tile_ref)


def split_pair(rows):
    lanes = lane_index(rows.shape)
    zero = jnp.zeros_like(rows)
    return jnp.concatenate([jnp.where(lanes < HEAD_WIDTH, rows, zero), jnp.where(lanes < HEAD_WIDTH, zero, rows)], 0)


def merge_pair(turned):
    return jnp.concatenate([turned[:HEAD_WIDTH, :LANES], turned[HEAD_WIDTH:, LANES:]], 0).T


def bucket_hot(map_ref):
    rows = lax.broadcasted_iota(jnp.int32, (BUCKETS, 2 * LONG_LEN), 0)
    return rows == map_ref[...]


def build_tiles(one_ref, two_ref, map_ref, tile_ref):
    pair = pl.program_id(0)
    hot = bucket_hot(map_ref).astype(bf16)
    table = jnp.concatenate(
        [one_ref[LORA : LORA + 8, :BUCKETS].astype(f32), two_ref[LORA : LORA + 8, :BUCKETS].astype(f32)], 0
    )
    by_offset = nn(table.astype(bf16), hot)
    heads = lax.broadcasted_iota(jnp.int32, (16, 1), 0)
    heads = jnp.where(heads < 8, heads, heads - 5)
    used = lax.broadcasted_iota(jnp.int32, (16, 1), 0)
    heads = jnp.where((used < 3) | ((used >= 8) & (used < 11)), heads, -1)
    rows_in = lax.broadcasted_iota(jnp.int32, (LANES, LANES), 0)
    lanes = lane_index((LANES, LANES))
    for t in range(2):
        row = jnp.sum(jnp.where(heads == 2 * pair + t, by_offset, 0.0), 0, keepdims=True)
        for d in range(7):
            block = 6 - d
            low = jnp.broadcast_to(row[:, LANES * block : LANES * block + LANES], (LANES, LANES))
            high = jnp.broadcast_to(row[:, LANES * block + LANES : LANES * block + 2 * LANES], (LANES, LANES))
            low = pltpu.roll(low, 1, 1, stride=1, stride_axis=0)
            high = pltpu.roll(high, 1, 1, stride=1, stride_axis=0)
            tile_ref[d, :, LANES * t : LANES * t + LANES] = jnp.where(lanes <= rows_in, low, high).astype(bf16)


def chunk_layout():
    chunks = []
    for c in range(LONG_LEN // LANES):
        chunks.append((HALF_ROWS, LONG_LEN, HALF_ROWS + LANES * c, 3 - c, 4))
    for s in range(HALF_ROWS // SHORT_LEN):
        chunks.append((LANES * s, SHORT_LEN, LANES * s, 3, s))
    return chunks


def length_of(place, lengths, which):
    m = place[0]
    if which == 4:
        return lengths[SHORT_SEQS + m]
    return lengths[4 * m + which]


def tiles_of(tile_ref, first, span):
    return jnp.concatenate([tile_ref[first + b].astype(f32) for b in range(span // LANES)], 0)


def biased(scores, tiles, length):
    scores = scores + tiles
    positions = lax.broadcasted_iota(jnp.int32, scores.shape, 0)
    return jnp.where(positions < length, scores, NEG)


def forward_attention(place, lengths, q_ref, k_ref, v_ref, one_ref, two_ref, map_ref, o_ref, lse_ref, tile_ref):
    tiles = tile_ref.at[0]
    build_tiles(one_ref, two_ref, map_ref, tiles)
    chunks = chunk_layout()
    raw = []
    for key_row, span, query_row, first, which in chunks:
        queries = split_pair(q_ref[query_row : query_row + LANES, :])
        raw.append(nt(k_ref[key_row : key_row + span, :], queries))
    weights = []
    for number, (key_row, span, query_row, first, which) in enumerate(chunks):
        scores = biased(raw[number], tiles_of(tiles, first, span), length_of(place, lengths, which))
        peak = jnp.max(scores, 0, keepdims=True)
        raised = jnp.exp(scores - peak)
        total = jnp.sum(raised, 0, keepdims=True)
        lse_ref[0, number : number + 1, :] = peak + jnp.log(total)
        weights.append((raised * (1.0 / total)).astype(bf16))
    turned = v_ref[HALF_ROWS:, :].T
    for number, (key_row, span, query_row, first, which) in enumerate(chunks):
        if which != 4:
            turned = v_ref[key_row : key_row + span, :].T
        o_ref[query_row : query_row + LANES, :] = merge_pair(nn(turned, weights[number])).astype(bf16)


def part_chunks(part):
    if part == 1:
        return [(c, 0, LONG_LEN, LANES * c, 3 - c, 4) for c in range(LONG_LEN // LANES)]
    return [(4 + s, LANES * s, SHORT_LEN, LANES * s, 0, s) for s in range(HALF_ROWS // SHORT_LEN)]


PAIRS = 2


def backward_attention(
    part, place, lengths, q_ref, k_ref, v_ref, do_ref, lse_ref, tile_ref, map_ref, turn_ref, table_scr, gathered
):
    turn = turn_ref[...]
    chunks = part_chunks(part)
    work = [(pair, c) + chunk for pair in range(PAIRS) for c, chunk in enumerate(chunks)]
    raw, grad_probs, kept = [], [], []
    for pair, c, number, key_row, span, query_row, first, which in work:
        cols = slice(LANES * pair, LANES * pair + LANES)
        queries = split_pair(q_ref[query_row : query_row + LANES, cols])
        douts = split_pair(do_ref[query_row : query_row + LANES, cols])
        raw.append(nt(k_ref[key_row : key_row + span, cols], queries))
        grad_probs.append(nt(v_ref[key_row : key_row + span, cols], douts))
        kept.append((queries, douts))
    grads, weights = [], []
    for i, (pair, c, number, key_row, span, query_row, first, which) in enumerate(work):
        scores = biased(raw[i], tiles_of(tile_ref.at[pair], first, span), length_of(place, lengths, which))
        probs = jnp.exp(scores - lse_ref[pair, number : number + 1, :])
        weights.append(probs.astype(bf16))
        weighted = probs * grad_probs[i]
        inner = jnp.sum(weighted, 0, keepdims=True)
        grads.append((weighted - probs * inner).astype(bf16))
        if part == 1:
            weights_all, grads_all, queries_all, douts_all = gathered
            at = slice(2 * LANES * c, 2 * LANES * c + 2 * LANES)
            weights_all[pair, :, at] = weights[i]
            grads_all[pair, :, at] = grads[i]
            queries_all[pair, at, :] = kept[i][0]
            douts_all[pair, at, :] = kept[i][1]
    result = []
    for pair in range(PAIRS):
        cols = slice(LANES * pair, LANES * pair + LANES)
        turned = k_ref[:, cols].T if part == 1 else None
        dq, dk, dv = [], [], []
        for i, (of, c, number, key_row, span, query_row, first, which) in enumerate(work):
            if of != pair:
                continue
            if part == 0:
                turned = k_ref[key_row : key_row + span, cols].T
                dv.append(nn(weights[i], kept[i][1]).astype(bf16))
                dk.append(nn(grads[i], kept[i][0]).astype(bf16))
            dq.append(merge_pair(nn(turned, grads[i])).astype(bf16))
        if part == 1:
            dv.append(nn(weights_all[pair], douts_all[pair]).astype(bf16))
            dk.append(nn(grads_all[pair], queries_all[pair]).astype(bf16))
        result.append((dq, dk, dv))
    rows_in = lax.broadcasted_iota(jnp.int32, (LANES, LANES), 0)
    lanes = lane_index((LANES, LANES))
    sums = []
    for pair in range(PAIRS):
        mine = grads[len(chunks) * pair : len(chunks) * pair + len(chunks)]
        pieces = [[jnp.zeros((1, LANES), f32) for _ in range(8)] for _ in range(2)]
        for d in range(7):
            if part == 0:
                stack = mine if d == 3 else []
            else:
                stack = [mine[c][LANES * (d - 3 + c) : LANES * (d - 2 + c), :] for c in range(4) if 0 <= d - 3 + c < 4]
            if len(stack) == 0:
                continue
            diagonal = nn(jnp.concatenate([turn] * len(stack), 1), jnp.concatenate(stack, 0))
            block = 6 - d
            for t in range(2):
                rolled = pltpu.roll(diagonal[:, LANES * t : LANES * t + LANES], 0, 1, stride=1, stride_axis=0)
                low = jnp.where(lanes >= rows_in, rolled, 0.0)
                pieces[t][block] = pieces[t][block] + jnp.sum(low, 0, keepdims=True)
                pieces[t][block + 1] = pieces[t][block + 1] + jnp.sum(rolled - low, 0, keepdims=True)
        sums += [jnp.concatenate(p, 1) for p in pieces]
    sums = jnp.concatenate(sums + [jnp.zeros((8 - 2 * PAIRS, 2 * LONG_LEN), f32)], 0)
    hot = bucket_hot(map_ref).astype(f32)
    table = lax.dot_general(
        sums, hot, (((1,), (1,)), ((), ())), precision=lax.Precision.HIGHEST, preferred_element_type=f32
    )
    table_scr[pl.program_id(0)] = jnp.concatenate([table, jnp.zeros((8, LANES - BUCKETS), f32)], 1)
    return result


WIDER = MODEL_WIDTH + LANES


def feedforward_shard(inputs, douts, win_scr, wout_scr, ready=lambda: None):
    before = nn(inputs[...], win_scr[...])
    ready()
    inputs, douts = inputs[...], douts[...]
    sig = 0.5 * jnp.tanh(0.5 * before) + 0.5
    active = (before * sig).astype(bf16)
    out = nn(active, wout_scr[...])
    grad_active = nt(douts, wout_scr[...]).astype(bf16).astype(f32)
    grad_before = (sig * (1.0 + before * (1.0 - sig)) * grad_active).astype(bf16)
    back = nt(grad_before, win_scr[...])
    grad_up = tn(inputs[:, MODEL_WIDTH:], grad_before)[:LORA]
    grad_low = tn(douts[:, MODEL_WIDTH:], active)[:LORA]
    return out, back, grad_up, grad_low


def fill_adapters(win_scr, wout_scr, up, low):
    win_scr[MODEL_WIDTH:, :] = pad_to(up[:LORA, :].astype(f32), LANES).astype(bf16)
    wout_scr[:, MODEL_WIDTH:] = pad_to(low[...].astype(f32), LANES).T.astype(bf16)


def shard_copies(wins, wouts, half, win_scr, wout_scr, sems, first):
    pieces = []
    if len(wins) == 1:
        pieces.append((wins[0], win_scr.at[pl.ds(0, MODEL_WIDTH)]))
    else:
        rows = MODEL_WIDTH // 2
        for k in range(2):
            there = pl.ds(pl.multiple_of(rows * jnp.bitwise_xor(half, k), rows), rows)
            pieces.append((wins[k].at[pl.ds(SECOND_ROWS, rows)], win_scr.at[there]))
    pieces.append((wouts[0], wout_scr.at[:, pl.ds(0, MODEL_WIDTH)]))
    return [pltpu.make_async_copy(source, goal, sems.at[first + i]) for i, (source, goal) in enumerate(pieces)]


def fill_output_maps(place, ao_in, bo_in, ao_scr, bo_scr):
    bo_scr[...] = pad_to(bo_in[...].astype(f32), LANES).astype(bf16)
    for at in range(4):

        @pl.when(place[0] == at)
        def _():
            pieces = [ao_in[:, 192 * (at ^ j) : 192 * (at ^ j) + 192] for j in range(4)]
            ao_scr[...] = pad_to(jnp.concatenate(pieces, 1).astype(f32), LANES).astype(bf16)


def start(copies):
    for copy in copies:
        copy.start()


def wait(copies):
    for copy in copies:
        copy.wait()


def both_blocks():
    return [slice(HALF_ROWS * i, HALF_ROWS * i + HALF_ROWS) for i in range(2)]


def middle_kernel(
    place, x_ref, cot_ref, att_ref, wo0, wo1, wo2, wo3, spread1_ref, win0, wout0, win1, wout1,
    ao_in, bo_in, gain_ref, down_in, router_ref, bf_in, up0, low0, up1, low1,
    hidden, inputs_ref, douts_ref, narrow, out_ref, back_ref, shard_ref,
    ao_scr, bo_scr, wo_scr, down_scr, bf_scr, win_scr, wout_scr,
):
    @pl.when(pl.program_id(0) == 0)
    def _():
        fill_output_maps(place, ao_in, bo_in, ao_scr, bo_scr)
        for j, wo in enumerate((wo0, wo1, wo2, wo3)):
            wo_scr[192 * j : 192 * j + 192, :] = wo[...]
        down_scr[...] = down_rows([down_in[...]], repeated_router(router_ref[...], 1))
        bf_scr[...] = pad_to(bf_in[...].astype(f32), LANES).astype(bf16)
        for j, (win, wout, up, low) in enumerate(((win0, wout0, up0, low0), (win1, wout1, up1, low1))):
            win_scr[j, :MODEL_WIDTH, :] = win[...]
            wout_scr[j, :, :MODEL_WIDTH] = wout[...]
            fill_adapters(win_scr.at[j], wout_scr.at[j], up, low)
        shard_ref[...] = jnp.zeros_like(shard_ref)

    attended = att_ref[...]
    downo = nt(attended, ao_scr[...])
    mixo = (spread1_ref[...] * downo).astype(bf16)
    held = x_ref[...].astype(f32) + (nn(attended, wo_scr[...]) + nn(mixo, bo_scr[...]))
    hidden[...] = held
    scale = lax.rsqrt(jnp.mean(held * held, -1, keepdims=True) + EPS)
    normed = (held * scale * gain_ref[...].astype(f32)).astype(bf16)
    both = nt(normed, down_scr[...])
    downi = both[:, :LANES]
    spread = softmax_repeated(both[:, LANES:], LORA, 1.0 * ADAPTER_RANK)
    cot = cot_ref[...]
    sidef = nt(cot, bf_scr[...])
    inputs = jnp.concatenate([normed, (spread * downi).astype(bf16)], 1)
    douts = jnp.concatenate([cot, (spread * sidef).astype(bf16)], 1)
    inputs_ref[...] = inputs
    douts_ref[...] = douts
    narrow[:, :LANES] = spread
    narrow[:, LANES : 2 * LANES] = downi
    narrow[:, 2 * LANES : 3 * LANES] = sidef
    narrow[:, 3 * LANES :] = downo
    for j in range(2):
        out, back, grad_up, grad_low = feedforward_shard(inputs, douts, win_scr.at[j], wout_scr.at[j])
        if j == 0:
            out_ref[...] = out
            back_ref[...] = back
        else:
            out_ref[...] += out
            back_ref[...] += back
        shard_ref[j, 0] += grad_up
        shard_ref[j, 1] += grad_low


FF_ROWS, AT_ROWS = 120, 88
FF_ALL, FF_OWN, AT_ALL, AT_OWN = 512, 256, 384, 256
FIRST_ROWS = 256


def send_pieces(pieces, own_ref, sent_refs):
    own_ref[...] = pieces[0]
    for j, sent in enumerate(sent_refs):
        sent[...] = pieces[j + 1].astype(bf16)


def post_kernel(
    place, half, att, wo0, wo1, wo2, wo3, spread1, win0, win1, wout0, win2, win3, wout1,
    hidden_in, inputs_in, douts_in, narrow_in, out_in, back_in,
    ao_in, bo_in, gain_ref, down_in, router_ref, bf_in, up0, low0, up1, low1, group_ref, pick_ref, shard_ref,
    result_out, ghidden_out, gatt_out, prod_out, ao_grad, ff_ref,
    att_scr, spread1_scr, hidden, inputs, douts, narrow, out, back, result, ghidden_scr, gatt, prod,
    ao_scr, bo_scr, wo_scr, down_scr, bf_scr, win_scr, wout_scr,
    shard_acc, pair_acc, bff_acc, bo_acc, ao_acc, gain_acc, pieces, flat, arrived, left,
):
    def copies(pairs, at):
        return [pltpu.make_async_copy(source, goal, arrived.at[at + i]) for i, (source, goal) in enumerate(pairs)]

    early = copies([(inputs_in, inputs), (douts_in, douts)], 0)
    first = shard_copies((win0, win1), (wout0,), half[0], win_scr.at[0], wout_scr.at[0], arrived, 2)
    second = shard_copies((win2, win3), (wout1,), half[0], win_scr.at[1], wout_scr.at[1], arrived, 5)
    sums = copies([(out_in, out), (back_in, back)], 8)
    rest = [(hidden_in, hidden), (narrow_in, narrow), (att, att_scr), (spread1, spread1_scr)]
    rest += [(wo.at[pl.ds(0, 192)], wo_scr.at[pl.ds(192 * j, 192)]) for j, wo in enumerate((wo0, wo1, wo2, wo3))]
    rest = copies(rest, 10)
    start(early[:1] + first + early[1:] + sums + second + rest)
    fill_output_maps(place, ao_in, bo_in, ao_scr, bo_scr)
    down_scr[...] = down_rows([down_in[...]], router_ref[...])
    bf_scr[...] = pad_to(bf_in[...].astype(f32), LANES).astype(bf16)
    fill_adapters(win_scr.at[0], wout_scr.at[0], up0, low0)
    fill_adapters(win_scr.at[1], wout_scr.at[1], up1, low1)
    for j, weights in enumerate((first, second)):
        wait(weights[:2])
        if j == 0:
            wait(early[:1])

        def ready():
            wait(weights[2:])
            if j == 0:
                wait(early[1:])

        more_out, more_back, grad_up, grad_low = feedforward_shard(inputs, douts, win_scr.at[j], wout_scr.at[j], ready)
        if j == 0:
            wait(sums)
        out[...] += more_out
        back[...] += more_back
        shard_acc[j, 0] = grad_up
        shard_acc[j, 1] = grad_low
    wait(rest)
    leaving = []

    def send(scr, goal, where):
        leaving.append(pltpu.make_async_copy(scr.at[where], goal.at[where], left.at[len(leaving)]))
        leaving[-1].start()

    def gather(scr, value, fresh):
        if fresh:
            scr[...] = value
        else:
            scr[...] += value

    def block(i, rows):
        where = pl.ds(HALF_ROWS * i, HALF_ROWS)
        normed, cot = inputs[rows, :MODEL_WIDTH], douts[rows, :MODEL_WIDTH]
        downf, sidei = out[rows, MODEL_WIDTH:], back[rows, MODEL_WIDTH:]
        spread, downi = narrow[rows, :LANES], narrow[rows, LANES : 2 * LANES]
        sidef, downo = narrow[rows, 2 * LANES : 3 * LANES], narrow[rows, 3 * LANES :]
        gates = spread1_scr[rows, :]
        held = hidden[rows, :]
        mixf = (spread * downf).astype(bf16)
        gdowni = (spread * sidei).astype(bf16)
        logit = logit_gradient(downf * sidef + downi * sidei, spread, group_ref[...], pick_ref[...])
        pair = jnp.concatenate([gdowni, logit], 1)
        yield
        grad_normed = back[rows, :MODEL_WIDTH] + nn(pair, down_scr[...])
        result[rows, :] = (held + (out[rows, :MODEL_WIDTH] + nn(mixf, bf_scr[...]))).astype(bf16)
        send(result, result_out, where)
        yield
        scale = lax.rsqrt(jnp.mean(held * held, -1, keepdims=True) + EPS)
        weighted = grad_normed * gain_ref[...].astype(f32)
        inner = jnp.mean(weighted * held, -1, keepdims=True)
        ghidden = cot.astype(f32) + scale * weighted - held * (scale * scale * scale * inner)
        branch = ghidden.astype(bf16)
        ghidden_scr[rows, :] = ghidden
        send(ghidden_scr, ghidden_out, where)
        gather(gain_acc, jnp.sum(grad_normed * held * scale, 0, keepdims=True), i == 0)
        yield
        sideo = nt(branch, bo_scr[...])
        through = nt(branch, wo_scr[...])
        gather(pair_acc, tn(pair, normed), i == 0)
        gather(bff_acc, tn(mixf, cot), i == 0)
        yield
        gdowno = (gates * sideo).astype(bf16)
        prod[rows, :] = downo * sideo
        send(prod, prod_out, where)
        gatt[rows, :] = (through + nn(gdowno, ao_scr[...])).astype(bf16)
        send(gatt, gatt_out, where)
        gather(bo_acc, tn((gates * downo).astype(bf16), branch), i == 0)
        gather(ao_acc, tn(gdowno, att_scr[rows, :]), i == 0)
        yield

    for _ in zip(*[block(i, rows) for i, rows in enumerate(both_blocks())]):
        pass
    ao_grad[...] = ao_acc[:LORA]
    quarters = (pair_acc[:LORA], bff_acc[:LORA], bo_acc[:LORA], router_quarter(pair_acc, gain_acc))
    for j in range(4):
        source, at = (shard_ref, j) if j < 2 else (shard_acc, j - 2)
        pieces[j, 0:LORA] = source[at, 0]
        pieces[j, LORA : 2 * LORA] = source[at, 1]
        pieces[jnp.bitwise_xor(place[0], j), 2 * LORA : 3 * LORA] = quarters[j]
    devices = ff_ref.shape[0]
    every, mine = FF_ALL // devices, FF_OWN // devices
    flat[...] = jnp.zeros_like(flat)
    for j in range(4):
        for t in range(6):
            cols = slice(LANES * t, LANES * t + LANES)
            flat[2 * LORA * t : 2 * LORA * t + 2 * LORA, :] = pieces[j, LORA:, cols]
            flat[FF_ALL + LORA * t : FF_ALL + LORA * t + LORA, :] = pieces[j, :LORA, cols]
        for k in range(devices):
            chunk = [flat[every * k : every * k + every, :], flat[FF_ALL + mine * k : FF_ALL + mine * k + mine, :]]
            ff_ref[k, (every + mine) * j : (every + mine) * (j + 1), :] = jnp.concatenate(chunk, 0).astype(bf16)
    wait(leaving)


def router_quarter(pair_acc, gain_acc):
    gain = jnp.broadcast_to(gain_acc[...], (8, MODEL_WIDTH))
    return jnp.concatenate([pair_acc[LANES : LANES + 16, :], gain, jnp.zeros((16, MODEL_WIDTH), f32)], 0)


def back_part(
    part, place, lengths, q_ref, k_ref, v_ref, do_ref, lse_ref, tile_ref, map_ref, turn_ref, joined_ref, ups_ref,
    mixed_ref, normed_in, spread_in, downs_in_rows, prod_in, ghidden_in, tokens, gain_ref, downs_in, router_ref,
    group_ref, pick_ref, up_scr, table_scr, sides_scr, side_scr, gnormed, down_scr,
    normed_ref, spread_ref, downs_ref, prod_ref, ghidden_ref, x_ref, sems, gathered, finish,
):
    pair = pl.program_id(0)

    def late_copies():
        rows = pl.ds(HALF_ROWS * part, HALF_ROWS)
        own_rows = pl.ds(pl.multiple_of(HALF_ROWS * (place[0] + 4 * part), HALF_ROWS), HALF_ROWS)
        sources = [normed_in.at[rows], spread_in.at[rows], downs_in_rows.at[rows], prod_in.at[rows], ghidden_in.at[rows]]
        goals = [normed_ref, spread_ref, downs_ref, prod_ref, ghidden_ref, x_ref]
        return [
            pltpu.make_async_copy(source, goal, sems.at[i])
            for i, (source, goal) in enumerate(zip(sources + [tokens.at[own_rows]], goals))
        ]

    @pl.when(pair == 0)
    def _():
        start(late_copies())

    grads = backward_attention(
        part, place, lengths, q_ref, k_ref, v_ref, do_ref, lse_ref, tile_ref, map_ref, turn_ref, table_scr, gathered
    )
    for i, blocks in enumerate(grads):
        for kind in range(3):
            at = LANES * (3 * i + kind)
            sides_scr[:, at : at + LANES] = jnp.concatenate(blocks[kind], 0)
    sides = sides_scr[...]
    joined = joined_ref[...].reshape(-1, MODEL_WIDTH)
    ups = jnp.concatenate([ups_ref[i] for i in range(PAIRS)], 1)
    up = tn(mixed_ref[...], sides)
    pieces = []
    for i in range(3 * PAIRS):
        rows = slice(LORA * (i % 3), LORA * (i % 3) + LORA)
        pieces.append(up[rows, LANES * i : LANES * i + LANES])
    up_scr[pair] = jnp.concatenate(pieces, 1)

    @pl.when(pair == 0)
    def _():
        gnormed[...] = nn(sides, joined)
        side_scr[...] = nt(sides, ups)

    @pl.when(pair > 0)
    def _():
        gnormed[...] += nn(sides, joined)
        side_scr[...] += nt(sides, ups)

    @pl.when(pair == pl.num_programs(0) - 1)
    def _():
        down_scr[...] = down_rows([downs_in[0], downs_in[1], downs_in[2]], router_ref[...])
        wait(late_copies())
        side = side_scr[...]
        spread = spread_ref[...]
        gdown = (spread * side).astype(bf16)
        gates = jnp.where(lane_index(spread.shape) < LORA, spread, 0.0)
        logit = logit_gradient(downs_ref[...] * side + prod_ref[...], gates, group_ref[...], pick_ref[...])
        both = jnp.concatenate([gdown, logit], 1)
        grad_normed = gnormed[...] + nn(both, down_scr[...])
        x = x_ref[...].astype(f32)
        scale = lax.rsqrt(jnp.mean(x * x, -1, keepdims=True) + EPS)
        weighted = grad_normed * gain_ref[...].astype(f32)
        inner = jnp.mean(weighted * x, -1, keepdims=True)
        gtokens = (ghidden_ref[...] + scale * weighted - x * (scale * scale * scale * inner)).astype(bf16)
        finish(gtokens, tn(both, normed_ref[...]), jnp.sum(grad_normed * x * scale, 0, keepdims=True))


def short_kernel(*refs):
    ins, outs, scratch = refs[:24], refs[24:30], refs[30:]
    ga_ref, gb_ref, up_ref, pair_ref, ggain_ref, table_ref = outs

    def finish(gtokens, pair_grad, ggain):
        ga_ref[...] = gtokens[:FIRST_ROWS]
        gb_ref[...] = gtokens[FIRST_ROWS:]
        pair_ref[...] = pair_grad
        ggain_ref[...] = ggain

    back_part(0, *ins, up_ref, table_ref, *scratch, None, finish)


def long_kernel(*refs):
    place, ins, more, outs, scratch = refs[0], refs[:24], refs[24:30], refs[30:36], refs[36:]
    ao_grad, up_in, pair_in, ggain_in, table_in, gb_in = more
    gtokens_ref, ggain_ref, own_ref, sent1, sent2, sent3 = outs
    up_scr, table_scr, pair_acc, pieces = scratch[:4]

    def finish(gtokens, pair_grad, ggain):
        gtokens_ref[: HALF_ROWS - FIRST_ROWS, :] = gb_in[...]
        gtokens_ref[HALF_ROWS - FIRST_ROWS :, :] = gtokens
        ggain_ref[...] = ggain + ggain_in[...]
        pair_acc[...] = pair_grad + pair_in[...]
        quarters = (
            pair_acc[0:LORA],
            pair_acc[LORA : 2 * LORA],
            pair_acc[2 * LORA : 3 * LORA],
            jnp.concatenate([pair_acc[LANES : LANES + 16, :], jnp.zeros((24, MODEL_WIDTH), f32)], 0),
        )
        ups = []
        for half in range(2):
            for part in range(3):
                pairs = []
                for p in range(3 * half, 3 * half + 3):
                    cols = slice(384 * (p % PAIRS) + LANES * part, 384 * (p % PAIRS) + LANES * part + LANES)
                    pairs.append(up_scr[p // PAIRS, :, cols] + up_in[p // PAIRS, :, cols])
                ups.append(jnp.concatenate(pairs, 1))
        for j in range(4):
            half, odd = j // 2, j % 2
            parts = [ao_grad[:, 192 * j : 192 * j + 192]]
            parts += [ups[3 * half + part][:, 192 * odd : 192 * odd + 192] for part in range(3)]
            pieces[j, 0:LORA] = jnp.concatenate(parts, 1)
            pieces[jnp.bitwise_xor(place[0], j), LORA : 2 * LORA] = quarters[j]
            heads = [3 * j + i for i in range(3)]
            rows = []
            for head in heads:
                step, row = head // (2 * PAIRS), head % (2 * PAIRS)
                rows.append(table_scr[step, row : row + 1, :] + table_in[step, row : row + 1, :])
            rows = jnp.concatenate(rows + [jnp.zeros((5, LANES), f32)], 0)
            pieces[j, 2 * LORA : 2 * LORA + 8] = jnp.concatenate([rows, jnp.zeros((8, MODEL_WIDTH - LANES), f32)], 1)
        send_pieces(pieces, own_ref, (sent1, sent2, sent3))

    back_part(1, *ins, up_scr, table_scr, *scratch[4:15], scratch[15:], finish)


def spread_kernel(layout, place, *refs):
    out_ref, held, arrived, left = refs[-4:]
    inward, outward = [], []
    at = 0
    for (j, first), source in zip(layout, refs):
        count = source.shape[0]
        inward.append(pltpu.make_async_copy(source, held.at[pl.ds(at, count)], arrived.at[len(inward)]))
        there = jnp.bitwise_xor(place[0], j)
        onward = []
        row = first
        while row < first + count:
            part, offset = divmod(row, HALF_ROWS)
            rows = min(HALF_ROWS - offset, first + count - row)
            goal = pl.multiple_of(HALF_ROWS * (4 * part + there), HALF_ROWS) + offset
            goal = out_ref.at[pl.ds(pl.multiple_of(goal, FIRST_ROWS), rows)]
            number = sum(len(o) for o in outward) + len(onward)
            onward.append(pltpu.make_async_copy(held.at[pl.ds(at + row - first, rows)], goal, left.at[number]))
            row += rows
        outward.append(onward)
        at += count
    for copy in inward:
        copy.start()
    for copy, onward in zip(inward, outward):
        copy.wait()
        start(onward)
    for onward in outward:
        wait(onward)


def sum_kernel(at0, at1, at2, at3, ggain, out_ref, flat):
    at = at0[...] + at1[...].astype(f32) + at2[...].astype(f32) + at3[...].astype(f32)
    flat[...] = jnp.zeros_like(flat)
    for t in range(6):
        part = at[:, LANES * t : LANES * t + LANES]
        flat[LORA * t : LORA * t + LORA, :] = part[LORA : 2 * LORA]
        first = LORA * (6 + t) if t < 2 else AT_ALL + LORA * (t - 2)
        flat[first : first + LORA, :] = part[:LORA]
    flat[AT_ALL + 4 * LORA : AT_ALL + 4 * LORA + 8, :] = at[2 * LORA :, :LANES]
    gain = jnp.concatenate([ggain[:, LANES * t : LANES * t + LANES] for t in range(6)], 0)
    flat[8 * LORA : 8 * LORA + 8, :] = pad_to(gain, 8)
    devices = out_ref.shape[0]
    every, mine = AT_ALL // devices, AT_OWN // devices
    for k in range(devices):
        chunk = [flat[every * k : every * k + every, :], flat[AT_ALL + mine * k : AT_ALL + mine * k + mine, :]]
        out_ref[k] = jnp.concatenate(chunk, 0).astype(bf16)


def unpack_kernel(
    place, own, one, two, three, gain1_ref, gain2_ref, qkv_ref, bq_ref, bkv_ref, ao_ref, bo_ref, ai_ref, bi_ref,
    aff_ref, bff_ref, r1_ref, r2_ref, table_ref, quarters2, quarters1, ffs, ats, ff_own, at_own,
):
    devices = own.shape[0]
    ff_all, ff_mine, at_all, at_mine = FF_ALL // devices, FF_OWN // devices, AT_ALL // devices, AT_OWN // devices
    for k in range(devices):
        for j, ref in enumerate((own, one, two, three)):
            both = ref[k].astype(f32)
            ffs[j, ff_all * k : ff_all * k + ff_all, :] = both[:ff_all]
            ats[j, at_all * k : at_all * k + at_all, :] = both[ff_all : ff_all + at_all]
            if j == 0:
                rest = both[ff_all + at_all :]
                ff_own[ff_mine * k : ff_mine * k + ff_mine, :] = rest[:ff_mine]
                at_own[at_mine * k : at_mine * k + at_mine, :] = rest[ff_mine:]

    def rows_of(ref, first, step):
        return jnp.concatenate([ref[first + step * t : first + step * t + LORA, :] for t in range(6)], 1)

    m = place[0]
    bi_ref[...] = rows_of(ff_own, 0, LORA)
    blocks = [ats[0, 6 * LORA + LORA * t : 7 * LORA + LORA * t, :] for t in range(2)]
    blocks += [at_own[LORA * t : LORA * t + LORA, :] for t in range(4)]
    mine = jnp.concatenate(blocks, 1)
    bq_ref[...] = mine[:, 192:384]
    bkv_ref[0] = mine[:, 384:576]
    bkv_ref[1] = mine[:, 576:768]
    table_ref[...] = at_own[4 * LORA : 4 * LORA + 3, :BUCKETS]
    for j in range(4):
        there = jnp.bitwise_xor(m, j)
        quarters2[there] = rows_of(ffs.at[j], LORA, 2 * LORA)
        quarters1[there] = rows_of(ats.at[j], 0, LORA)
        low = rows_of(ffs.at[j], 0, 2 * LORA)
        out = [ats[j, 6 * LORA + LORA * t : 7 * LORA + LORA * t, :] for t in range(2)]
        out = jnp.concatenate(out, 1)[:, :192]
        for at in range(4):

            @pl.when(there == at)
            def _():
                aff_ref[:, MODEL_WIDTH * at : MODEL_WIDTH * at + MODEL_WIDTH] = low
                ao_ref[:, 192 * at : 192 * at + 192] = out

    for part in range(3):
        qkv_ref[part] = quarters1[part]
    ai_ref[...] = quarters2[0]
    bff_ref[...] = quarters2[1]
    bo_ref[...] = quarters2[2]
    r1_ref[...] = quarters1[3, :EXPERTS]
    r2_ref[...] = quarters2[3, :EXPERTS]
    total = jnp.zeros((8, LANES), f32)
    for j in range(4):
        total = total + ats[j, 8 * LORA : 8 * LORA + 8, :]
    gain1_ref[...] = total[:6]
    gain2_ref[...] = jnp.concatenate([quarters2[3, 16:17, LANES * t : LANES * t + LANES] for t in range(6)], 0)


def whole(array):
    return pl.BlockSpec(array.shape, lambda *_: (0,) * array.ndim)


def rows_block(array):
    return pl.BlockSpec((HALF_ROWS, array.shape[1]), lambda i, *_: (i, 0))


def token_block():
    return pl.BlockSpec((HALF_ROWS, MODEL_WIDTH), lambda i, place, *_: (place[0] + 4 * i, 0))


def shape(dims, dtype):
    return jax.ShapeDtypeStruct(dims, dtype)


def call(kernel, grid, scalars, inputs, in_specs, outs, out_specs, scratch=(), aliases=None, flops=0):
    return pl.pallas_call(
        kernel,
        grid_spec=pltpu.PrefetchScalarGridSpec(
            num_scalar_prefetch=len(scalars),
            grid=grid,
            in_specs=in_specs,
            out_specs=out_specs,
            scratch_shapes=list(scratch),
        ),
        out_shape=outs,
        input_output_aliases=aliases or {},
        compiler_params=pltpu.CompilerParams(vmem_limit_bytes=VMEM_LIMIT),
        cost_estimate=pl.CostEstimate(flops=flops, bytes_accessed=0, transcendentals=0),
    )(*scalars, *inputs)


def exchange(value, axis, size, mask):
    return lax.ppermute(value, axis, [(i, i ^ mask) for i in range(size)])


def scatter_over(flat, axis, size):
    pieces = lax.all_to_all(flat, axis, 0, 0)
    return jnp.sum(pieces.astype(f32), 0)


def gather_over(mine, axis, size):
    return lax.all_to_all(jnp.broadcast_to(mine[None], (size,) + mine.shape), axis, 0, 0)


def constants():
    group1 = np.zeros((LANES, LANES), np.float32)
    for i in range(3 * LORA):
        for j in range(LORA):
            group1[i, j] = float((i % LORA) // ADAPTER_RANK == j // ADAPTER_RANK)
    pick = np.zeros((LANES, LANES), np.float32)
    for e in range(EXPERTS):
        pick[ADAPTER_RANK * e, e] = 1.0
    turn = np.eye(LANES, dtype=np.float32)[::-1].copy()
    return tuple(jnp.asarray(c, bf16) for c in (group1, pick, turn))


def local(
    dp_size,
    mp_size,
    tokens,
    cotangent,
    attention_norm_gain,
    feedforward_norm_gain,
    query_projection_weight,
    key_value_weight,
    attention_output_weight,
    ffn_input_weight,
    ffn_output_weight,
    projection_down_weight,
    query_up_weight,
    key_value_up_weight,
    attention_output_down_weight,
    attention_output_up_weight,
    ffn_input_down_weight,
    ffn_input_up_weight,
    ffn_output_down_weight,
    ffn_output_up_weight,
    attention_router_weight,
    feedforward_router_weight,
    bucket_bias_table,
    offset_bucket_map,
    sequence_length_list,
):
    m = lax.axis_index("mp").astype(jnp.int32)
    d = lax.axis_index("dp").astype(jnp.int32)
    place = m.reshape(1)
    group, pick, turn = constants()

    def mp_swap(value, mask):
        return exchange(value, "mp", mp_size, mask)

    def pack_part(rows, index):
        return pl.BlockSpec((rows, MODEL_WIDTH), lambda *_: (index, 0))

    def element_part(rows, first):
        return pl.BlockSpec((pl.Element(rows), pl.Element(MODEL_WIDTH)), lambda *_: (first, 0))

    win0, wout0 = ffn_input_weight, ffn_output_weight
    half = (d & 1).reshape(1)
    inputs = [
        query_projection_weight.T,
        jnp.transpose(key_value_weight, (0, 2, 1)),
        query_up_weight,
        key_value_up_weight,
        bucket_bias_table.T,
        attention_output_weight,
        ffn_input_up_weight,
        win0,
    ]
    outs = [
        shape((rows, MODEL_WIDTH), bf16)
        for rows in (QK_ROWS, V_ROWS, SECOND_ROWS + HALF_SHARD, SECOND_ROWS + QK_ROWS + V_ROWS)
    ]
    *pack0, more0, both0 = call(
        pack_kernel,
        (1,),
        [half],
        inputs,
        [whole(a) for a in inputs[:-1]] + [pl.BlockSpec((HALF_SHARD, MODEL_WIDTH), lambda i, half: (half[0], 0))],
        outs,
        [whole(o) for o in outs],
    )
    pack2 = [mp_swap(p, 2) for p in pack0]
    both1 = mp_swap(both0, 1)
    more2 = mp_swap(more0, 2)
    wout2 = mp_swap(wout0, 2)

    gain1 = attention_norm_gain.reshape(1, -1)
    gain2 = feedforward_norm_gain.reshape(1, -1)
    downs_in = jnp.transpose(projection_down_weight, (0, 2, 1))
    router1, router2 = attention_router_weight.T, feedforward_router_weight.T
    rev_map = jnp.concatenate([offset_bucket_map[::-1], jnp.full((1,), -1, jnp.int32)]).reshape(1, -1)

    wide, narrow = shape((ROWS, MODEL_WIDTH), bf16), shape((ROWS, LANES), f32)
    narrow16 = shape((ROWS, LANES), bf16)

    joined_shape, ups_shape = shape((6, 384, MODEL_WIDTH), bf16), shape((6, LANES, 384), bf16)
    pair_outs = [wide, wide, wide, wide, shape((6, 8, 256), f32), shape((6, 7, LANES, 256), bf16), joined_shape, ups_shape]

    def pair_specs(first):
        specs = [pl.BlockSpec((ROWS, LANES), lambda p, *_: (0, first + p))] * 4
        for o in pair_outs[4:]:
            specs.append(pl.BlockSpec((1,) + o.shape[1:], lambda p, *_, n=len(o.shape): (first + p,) + (0,) * (n - 1)))
        return specs

    def half_of_rows(part):
        return pl.BlockSpec((HALF_ROWS, MODEL_WIDTH), lambda p, place, *_: (place[0] + 4 * part, 0))

    joined_scratch = [pltpu.VMEM((3, 384, MODEL_WIDTH), bf16), pltpu.VMEM((3, LANES, 384), bf16)]
    fixed = [wide, narrow16, narrow, narrow]
    *pair_state, normed1, mixed1, spread1, downs1 = call(
        first_kernel,
        (3,),
        [place, sequence_length_list],
        [tokens, tokens, gain1, downs_in, router1, *pack0, pack0[1], both1, both1, rev_map],
        [half_of_rows(0), half_of_rows(1), whole(gain1), whole(downs_in), whole(router1)]
        + [pack_part(384, 0), pack_part(192, 0), pack_part(48, 4), element_part(576, 240), pack_part(48, 17)]
        + [whole(rev_map)],
        pair_outs + fixed,
        pair_specs(0) + [whole(o) for o in fixed],
        scratch=joined_scratch + [pltpu.VMEM((256, MODEL_WIDTH), bf16)],
    )
    win1, wout1 = mp_swap(win0, 1), mp_swap(wout0, 1)
    pack2, normed1, win1, wout1 = lax.optimization_barrier((pack2, normed1, win1, wout1))
    pack3 = [mp_swap(p, 1) for p in pack2]
    inputs = [normed1, mixed1, *pack2, pack2[1], *pack3, pack3[1], rev_map]
    queries, keys, all_values, attended, lse, tiles, joined, ups = call(
        second_kernel,
        (3,),
        [place, sequence_length_list],
        inputs + pair_state,
        [whole(normed1), whole(mixed1)]
        + [pack_part(384, 0), pack_part(192, 0), pack_part(48, 4)] * 2
        + [whole(rev_map)]
        + [pl.BlockSpec(memory_space=pl.ANY)] * 8,
        pair_outs,
        pair_specs(3),
        scratch=joined_scratch,
        aliases={2 + len(inputs) + i: i for i in range(8)},
    )

    attended, more2 = lax.optimization_barrier((attended, more2))
    more3 = mp_swap(more2, 1)
    other2 = exchange(more2, "dp", dp_size, 1)
    mores = [more0, both1, more2, more3]
    ao_in, bo_in, bf_in = attention_output_down_weight.T, attention_output_up_weight, ffn_output_up_weight
    down_in, low_in = ffn_input_down_weight.T, ffn_output_down_weight.T

    def low_block(j):
        return pl.BlockSpec((LORA, MODEL_WIDTH), lambda i, place, *_: (0, jnp.bitwise_xor(place[0], j)))

    def small_inputs(first):
        values = [ao_in, bo_in, gain2, down_in, router2, bf_in]
        specs = [whole(a) for a in values]
        for j in (first, first + 1):
            values += [mores[j], low_in]
            specs += [pack_part(48, 4), low_block(j)]
        return values, specs

    hbm = pl.BlockSpec(memory_space=pltpu.HBM)
    shard_shape = shape((2, 2, LORA, MODEL_WIDTH), f32)
    wide_f32, wider, wider_f32 = shape((ROWS, MODEL_WIDTH), f32), shape((ROWS, WIDER), bf16), shape((ROWS, WIDER), f32)
    state_shapes = [wide_f32, wider, wider, shape((ROWS, 4 * LANES), f32), wider_f32, wider_f32]

    def held(array):
        return pltpu.VMEM(array.shape, array.dtype)

    map_scratch = [
        pltpu.VMEM((LANES, MODEL_WIDTH), bf16),
        pltpu.VMEM((LANES, MODEL_WIDTH), bf16),
        pltpu.VMEM((MODEL_WIDTH, MODEL_WIDTH), bf16),
        pltpu.VMEM((256, MODEL_WIDTH), bf16),
        pltpu.VMEM((LANES, MODEL_WIDTH), bf16),
        pltpu.VMEM((2, WIDER, MODEL_WIDTH), bf16),
        pltpu.VMEM((2, MODEL_WIDTH, WIDER), bf16),
    ]
    values, specs = small_inputs(0)
    inputs = [tokens, cotangent, attended] + mores + [spread1, win0, wout0, win1, wout1]
    *state, shard_grads = call(
        middle_kernel,
        (2,),
        [place],
        inputs + values,
        [token_block(), token_block(), rows_block(attended)]
        + [pack_part(192, 0)] * 4
        + [rows_block(spread1)]
        + [whole(a) for a in inputs[-4:]]
        + specs,
        state_shapes + [shard_shape],
        [rows_block(a) for a in state_shapes] + [whole(shard_shape)],
        scratch=map_scratch,
    )
    state[0], other2, wout2 = lax.optimization_barrier((state[0], other2, wout2))
    other3 = mp_swap(other2, 1)
    wout3 = mp_swap(wout2, 1)
    values, specs = small_inputs(2)
    ao_shape = shape((LORA, MODEL_WIDTH), f32)
    ff_shape = shape((dp_size, 4 * (FF_ALL + FF_OWN) // dp_size, LANES), bf16)
    inputs = [attended] + mores + [spread1, more2, other2, wout2, more3, other3, wout3] + state
    values += [group, pick, shard_grads]
    specs += [whole(a) for a in (group, pick, shard_grads)]
    outs = [wide, wide_f32, wide, narrow, ao_shape, ff_shape]
    result, ghidden, gatt, prod, ao_grad, ff_flat = call(
        post_kernel,
        (1,),
        [place, half],
        inputs + values,
        [hbm] * len(inputs) + specs,
        outs,
        [hbm] * 4 + [whole(o) for o in outs[4:]],
        scratch=[held(wide), held(narrow)]
        + [held(a) for a in state_shapes]
        + [held(wide), held(wide_f32), held(wide), held(narrow)]
        + map_scratch
        + [
            pltpu.VMEM((2, 2, LORA, MODEL_WIDTH), f32),
            pltpu.VMEM((256, MODEL_WIDTH), f32),
            pltpu.VMEM((LANES, MODEL_WIDTH), f32),
            pltpu.VMEM((LANES, MODEL_WIDTH), f32),
            pltpu.VMEM((LANES, MODEL_WIDTH), f32),
            pltpu.VMEM((1, MODEL_WIDTH), f32),
            pltpu.VMEM((4, FF_ROWS, MODEL_WIDTH), f32),
            pltpu.VMEM((FF_ALL + FF_OWN, LANES), f32),
            pltpu.SemaphoreType.DMA((18,)),
            pltpu.SemaphoreType.DMA((8,)),
        ],
    )
    result2 = mp_swap(result, 2)
    ff_pieces = lax.all_to_all(ff_flat, "dp", 0, 0)

    at_shapes = [shape((AT_ROWS, MODEL_WIDTH), f32)] + [shape((AT_ROWS, MODEL_WIDTH), bf16)] * 3
    gain_shape, up_shape = shape((1, MODEL_WIDTH), f32), shape((6 // PAIRS, LORA, 384 * PAIRS), f32)
    pair_shape, table_shape = shape((256, MODEL_WIDTH), f32), shape((6 // PAIRS, 8, LANES), f32)

    def part_call(kernel, part, more, outs, scratch):
        def block(array):
            return pl.BlockSpec((HALF_ROWS, array.shape[1]), lambda p, *_: (part, 0))

        pair = [pl.BlockSpec((HALF_ROWS, PAIRS * LANES), lambda p, *_: (part, p))] * 4
        if part == 0:
            tile = pl.BlockSpec((PAIRS, 1, LANES, 256), lambda p, *_: (p, 3, 0, 0))
        else:
            tile = pl.BlockSpec((PAIRS, 7, LANES, 256), lambda p, *_: (p, 0, 0, 0))
        three = [pl.BlockSpec((PAIRS,) + a.shape[1:], lambda p, *_: (p, 0, 0)) for a in (lse, joined, ups)]
        late = [normed1, spread1, downs1, prod, ghidden, tokens]
        fixed = [gain1, downs_in, router1, group, pick] + more
        return call(
            kernel,
            (6 // PAIRS,),
            [place, sequence_length_list],
            [queries, keys, all_values, gatt, lse, tiles, rev_map, turn, joined, ups, mixed1] + late + fixed,
            pair
            + [three[0], tile, whole(rev_map), whole(turn)]
            + three[1:]
            + [block(mixed1)]
            + [hbm] * len(late)
            + [whole(a) for a in fixed],
            outs,
            [whole(o) for o in outs],
            scratch=scratch
            + [
                pltpu.VMEM((HALF_ROWS, 384 * PAIRS), bf16),
                pltpu.VMEM((HALF_ROWS, LANES), f32),
                pltpu.VMEM((HALF_ROWS, MODEL_WIDTH), f32),
                pltpu.VMEM((256, MODEL_WIDTH), bf16),
            ]
            + [pltpu.VMEM((HALF_ROWS, a.shape[1]), a.dtype) for a in late]
            + [pltpu.SemaphoreType.DMA((len(late),))]
            + (
                [pltpu.VMEM((PAIRS, LONG_LEN, 1024), bf16)] * 2 + [pltpu.VMEM((PAIRS, 1024, LANES), bf16)] * 2
                if part == 1
                else []
            ),
        )

    early_shape = shape((FIRST_ROWS, MODEL_WIDTH), bf16)
    rest_shape = shape((ROWS - FIRST_ROWS, MODEL_WIDTH), bf16)
    gearly, *short_grads = part_call(
        short_kernel,
        0,
        [],
        [early_shape, shape((HALF_ROWS - FIRST_ROWS, MODEL_WIDTH), bf16), up_shape, pair_shape, gain_shape, table_shape],
        [],
    )
    gearly2 = mp_swap(gearly, 2)
    grest, ggain, *at_pieces = part_call(
        long_kernel,
        1,
        [ao_grad] + short_grads[1:] + short_grads[:1],
        [rest_shape, gain_shape] + at_shapes,
        [held(up_shape), held(table_shape), held(pair_shape), pltpu.VMEM((4, AT_ROWS, MODEL_WIDTH), f32)],
    )
    result2, gearly2, at_pieces, ff_pieces, ggain = lax.optimization_barrier(
        (result2, gearly2, at_pieces, ff_pieces, ggain)
    )
    at_parts = [at_pieces[0]] + [mp_swap(at_pieces[j], j) for j in (1, 2, 3)]
    ff_sums = jnp.sum(ff_pieces.astype(f32), 0).reshape(4, -1, LANES)
    ff_sum = ff_sums[0]
    for j in (1, 2, 3):
        ff_sum = ff_sum + mp_swap(ff_sums[j].astype(bf16), j).astype(f32)
    grest, at_parts, ff_sum = lax.optimization_barrier((grest, at_parts, ff_sum))
    grest2 = mp_swap(grest, 2)

    def spread_rows(layout, parts, onto=None):
        rows = sum(p.shape[0] for p in parts)
        inputs = list(parts) + ([] if onto is None else [onto])
        return call(
            functools.partial(spread_kernel, layout),
            (1,),
            [place],
            inputs,
            [hbm] * len(inputs),
            shape((4 * ROWS, MODEL_WIDTH), bf16),
            hbm,
            scratch=[
                pltpu.VMEM((rows, MODEL_WIDTH), bf16),
                pltpu.SemaphoreType.DMA((len(parts),)),
                pltpu.SemaphoreType.DMA((2 * len(parts),)),
            ],
            aliases=None if onto is None else {len(inputs): 0},
        )

    parts = at_parts + [ggain]
    flat_shape = shape((dp_size, (AT_ALL + AT_OWN) // dp_size, LANES), bf16)
    flat = call(
        sum_kernel,
        (1,),
        [],
        parts,
        [whole(a) for a in parts],
        flat_shape,
        whole(flat_shape),
        scratch=[pltpu.VMEM((AT_ALL + AT_OWN, LANES), f32)],
    )
    flat, result2 = lax.optimization_barrier((flat, result2))
    result1, result3 = mp_swap(result, 1), mp_swap(result2, 1)
    at_sum = scatter_over(flat, "dp", dp_size)
    gearly1, gearly3 = mp_swap(gearly, 1), mp_swap(gearly2, 1)
    at_sum, gearly1, gearly3 = lax.optimization_barrier((at_sum, gearly1, gearly3))
    ff_all, at_all = FF_ALL // dp_size, AT_ALL // dp_size
    mine = [ff_sum[:ff_all], at_sum[:at_all], ff_sum[ff_all:], at_sum[at_all:]]
    own = gather_over(jnp.concatenate(mine, 0).astype(bf16), "dp", dp_size)
    output = spread_rows([(0, 0), (1, 0), (2, 0), (3, 0)], [result, result1, result2, result3])
    grest1 = mp_swap(grest, 1)
    some = spread_rows(
        [(0, 0), (0, FIRST_ROWS), (1, 0), (1, FIRST_ROWS), (2, 0), (3, 0)],
        [gearly, grest, gearly1, grest1, gearly2, gearly3],
    )
    own, output, some, grest2 = lax.optimization_barrier((own, output, some, grest2))
    grest3 = mp_swap(grest2, 1)
    shared = own[:, : ff_all + at_all]
    two = mp_swap(shared, 2)
    one = mp_swap(shared, 1)
    grad_tokens = spread_rows([(2, FIRST_ROWS), (3, FIRST_ROWS)], [grest2, grest3], some)
    two, grad_tokens = lax.optimization_barrier((two, grad_tokens))
    three = mp_swap(two, 1)
    outs = [
        shape((6, LANES), f32),
        shape((6, LANES), f32),
        shape((3, LORA, MODEL_WIDTH), f32),
        shape((LORA, 192), f32),
        shape((2, LORA, 192), f32),
        shape((LORA, MODEL_WIDTH), f32),
        shape((LORA, MODEL_WIDTH), f32),
        shape((LORA, MODEL_WIDTH), f32),
        shape((LORA, MODEL_WIDTH), f32),
        shape((LORA, 4 * MODEL_WIDTH), f32),
        shape((LORA, MODEL_WIDTH), f32),
        shape((EXPERTS, MODEL_WIDTH), f32),
        shape((EXPERTS, MODEL_WIDTH), f32),
        shape((3, BUCKETS), f32),
    ]
    flats = [own, one, two, three]
    grads = call(
        unpack_kernel,
        (1,),
        [place],
        flats,
        [whole(a) for a in flats],
        outs,
        [whole(o) for o in outs],
        scratch=[pltpu.VMEM((4, LORA, MODEL_WIDTH), f32)] * 2
        + [pltpu.VMEM((4, FF_ALL, LANES), f32), pltpu.VMEM((4, AT_ALL, LANES), f32)]
        + [pltpu.VMEM((FF_OWN, LANES), f32), pltpu.VMEM((AT_OWN, LANES), f32)],
    )
    g1, g2, g_qkv, g_bq, g_bkv, g_ao, g_bo, g_ai, g_bi, g_aff, g_bff, g_r1, g_r2, g_table = grads
    return (
        output,
        grad_tokens,
        g1.reshape(-1),
        g2.reshape(-1),
        jnp.transpose(g_qkv, (0, 2, 1)),
        g_bq,
        g_bkv,
        g_ao.T,
        g_bo,
        g_ai.T,
        g_bi,
        g_aff.T,
        g_bff,
        g_r1.T,
        g_r2.T,
        g_table.T,
    )


def solution(mesh):
    in_specs = (
        P("dp", None),
        P("dp", None),
        P(),
        P(),
        P(None, "mp"),
        P(None, None, "mp"),
        P("mp", None),
        P(None, "mp"),
        P("mp", None),
        P(),
        P(None, "mp"),
        P(None, None, "mp"),
        P(),
        P(),
        P(),
        P(None, "mp"),
        P(),
        P(),
        P(),
        P(),
        P(None, "mp"),
        P(),
        P("dp"),
    )
    out_specs = (
        P("dp", None),
        P("dp", None),
        P(),
        P(),
        P(),
        P(None, "mp"),
        P(None, None, "mp"),
        P(),
        P(),
        P(),
        P(None, "mp"),
        P(),
        P(),
        P(),
        P(),
        P(None, "mp"),
    )
    step = functools.partial(local, mesh.shape["dp"], mesh.shape["mp"])
    return jax.shard_map(step, mesh=mesh, in_specs=in_specs, out_specs=out_specs, check_vma=False)
```

```python
import functools

import jax
import jax.numpy as jnp
import numpy as np
from jax import lax
from jax.experimental import pallas as pl
from jax.experimental.pallas import tpu as pltpu
from jax.sharding import PartitionSpec as P

HEAD_WIDTH = 64
BUCKETS = 32
ADAPTER_RANK = 4
SHORT_LEN = 128
LONG_LEN = 512
LONG_SEQS = 4
SHORT_SEQS = 16
MODEL_WIDTH = 768
LORA = 40
EXPERTS = 10
LANES = 128
HALF_ROWS = 512
ROWS = 1024
EPS = 1e-06
NEG = -1e9

bf16 = jnp.bfloat16
f32 = jnp.float32
VMEM_LIMIT, SMALL_LIMIT = 56 * 1024 * 1024, 24 * 1024 * 1024


def nn(a, b):
    return jnp.dot(a, b, preferred_element_type=f32)


def nt(a, b):
    return lax.dot_general(a, b, (((1,), (1,)), ((), ())), preferred_element_type=f32)


def tn(a, b):
    return lax.dot_general(a, b, (((0,), (0,)), ((), ())), preferred_element_type=f32)


def lane_index(shape):
    return lax.broadcasted_iota(jnp.int32, shape, 1)


def softmax_repeated(logits, valid, repeats):
    logits = jnp.where(lane_index(logits.shape) < valid, logits, -1e30)
    raised = jnp.exp(logits - jnp.max(logits, -1, keepdims=True))
    return raised * (repeats / jnp.sum(raised, -1, keepdims=True))


def logit_gradient(products, gates, group, pick):
    high = products.astype(bf16)
    low = (products - high.astype(f32)).astype(bf16)
    gate_grad = nn(high, group) + nn(low, group)
    inner = jnp.sum(gates * gate_grad, -1, keepdims=True) * (1.0 / ADAPTER_RANK)
    logit_grad = (gates * (gate_grad - inner)).astype(bf16)
    return nn(logit_grad, pick).astype(bf16)


QK_ROWS, V_ROWS, SECOND_ROWS, HALF_SHARD = 384, 240, 240, 384


def pack_kernel(half, q_ref, kv_ref, qup_ref, kvup_ref, table_ref, wo_ref, up_ref, win_ref, qk_ref, v_ref, second_ref, both_ref):
    qk_ref[0:192, :] = q_ref[...]
    qk_ref[192:384, :] = kv_ref[0]
    v_ref[0:192, :] = kv_ref[1]
    ups = jnp.concatenate([qup_ref[...], kvup_ref[0], kvup_ref[1], jnp.zeros((LORA, 192), bf16)], 1).astype(f32)
    table = jnp.pad(table_ref[...].astype(f32), ((0, 5), (0, MODEL_WIDTH - BUCKETS)))
    v_ref[192:240, :] = jnp.concatenate([ups, table], 0).astype(bf16)
    second_ref[0:192, :] = wo_ref[...]
    second_ref[192:240, :] = jnp.pad(up_ref[...].astype(f32), ((0, 8), (0, 0))).astype(bf16)
    second_ref[240:, :] = win_ref[...]
    both_ref[:SECOND_ROWS, :] = second_ref[:SECOND_ROWS, :]
    both_ref[SECOND_ROWS : SECOND_ROWS + QK_ROWS, :] = qk_ref[...]
    both_ref[SECOND_ROWS + QK_ROWS :, :] = v_ref[...]


def pad_to(rows, count):
    if rows.shape[0] == count:
        return rows
    return jnp.concatenate([rows, jnp.zeros((count - rows.shape[0], rows.shape[1]), rows.dtype)], 0)


def repeated_router(router, copies):
    rows = lax.broadcasted_iota(jnp.int32, (LANES, EXPERTS), 0)
    first = ADAPTER_RANK * lax.broadcasted_iota(jnp.int32, (LANES, EXPERTS), 1)
    hot = jnp.zeros((LANES, EXPERTS), jnp.bool_)
    for c in range(copies):
        hot = hot | ((rows >= LORA * c + first) & (rows < LORA * c + first + ADAPTER_RANK))
    return nn(hot.astype(bf16), router).astype(bf16)


def down_rows(downs, router_rows):
    downs = pad_to(jnp.concatenate([part.astype(f32) for part in downs], 0), LANES)
    return jnp.concatenate([downs, pad_to(router_rows.astype(f32), LANES)], 0).astype(bf16)


def weight_rows(refs, part):
    if len(refs) == 1:
        return refs[0].at[192 * part : 192 * part + 192]
    return refs[1].at[0:192] if part == 2 else refs[0].at[192 * part : 192 * part + 192]


def join_packs(one, two, ups_one, ups_two, joined_scr, ups_scr):
    for part in range(3):
        at = LANES * part
        one_ref, two_ref = weight_rows(one, part), weight_rows(two, part)
        joined_scr[0, at : at + LANES, :] = one_ref[0:LANES, :]
        joined_scr[1, at : at + 64, :] = one_ref[LANES:192, :]
        joined_scr[1, at + 64 : at + LANES, :] = two_ref[0:64, :]
        joined_scr[2, at : at + LANES, :] = two_ref[64:192, :]
    pieces = []
    for part in range(3):
        cols = slice(192 * part, 192 * part + 192)
        pieces.append(jnp.concatenate([ups_one[:LORA, cols], ups_two[:LORA, cols]], 1).astype(f32))
    zero = jnp.zeros((LORA, LANES), f32)
    for pair in range(3):
        rows = []
        for part in range(3):
            piece = pieces[part][:, LANES * pair : LANES * pair + LANES]
            rows.append(jnp.concatenate([piece if p == part else zero for p in range(3)], 1))
        ups_scr[pair] = pad_to(jnp.concatenate(rows, 0), LANES).astype(bf16)


def project_pair(normed_ref, mixed_ref, joined_scr, ups_scr, q_ref, k_ref, v_ref, joined_ref, ups_ref):
    pair = pl.program_id(0)
    joined, ups = joined_scr[pair], ups_scr[pair]
    joined_ref[0] = joined
    ups_ref[0] = ups
    for first in (0, HALF_ROWS):
        rows = slice(first, first + HALF_ROWS)
        result = (nt(normed_ref[rows, :], joined) + nn(mixed_ref[rows, :], ups)).astype(bf16)
        q_ref[rows, :] = result[:, :LANES]
        k_ref[rows, :] = result[:, LANES : 2 * LANES]
        v_ref[rows, :] = result[:, 2 * LANES :]


def first_kernel(
    place, lengths, xs_ref, xl_ref, gain_ref, downs_in, router_ref, one_qk, one_v, ups_one, two_ref, ups_two, map_ref,
    q_ref, k_ref, v_ref, o_ref, lse_ref, tile_ref, joined_ref, ups_ref, normed_ref, mixed_ref, spread_ref, downs_ref,
    joined_scr, ups_scr, down_scr,
):
    @pl.when(pl.program_id(0) == 0)
    def _():
        join_packs((one_qk, one_v), (two_ref,), ups_one, ups_two, joined_scr, ups_scr)
        down_scr[...] = down_rows([downs_in[0], downs_in[1], downs_in[2]], repeated_router(router_ref[...], 3))
        for x_ref, first in ((xs_ref, 0), (xl_ref, HALF_ROWS)):
            rows = slice(first, first + HALF_ROWS)
            x = x_ref[...].astype(f32)
            scale = lax.rsqrt(jnp.mean(x * x, -1, keepdims=True) + EPS)
            normed = (x * scale * gain_ref[...].astype(f32)).astype(bf16)
            normed_ref[rows, :] = normed
            both = nt(normed, down_scr[...])
            downs = both[:, :LANES]
            spread = softmax_repeated(both[:, LANES:], 3 * LORA, 3.0 * ADAPTER_RANK)
            mixed_ref[rows, :] = (spread * downs).astype(bf16)
            spread_ref[rows, :] = spread
            downs_ref[rows, :] = downs

    project_pair(normed_ref, mixed_ref, joined_scr, ups_scr, q_ref, k_ref, v_ref, joined_ref, ups_ref)
    forward_attention(place, lengths, q_ref, k_ref, v_ref, ups_one, ups_two, map_ref, o_ref, lse_ref, tile_ref)


def second_kernel(
    place, lengths, normed_ref, mixed_ref, one_qk, one_v, ups_one, two_qk, two_v, ups_two, map_ref,
    q_in, k_in, v_in, o_in, lse_in, tile_in, joined_in, ups_in,
    q_ref, k_ref, v_ref, o_ref, lse_ref, tile_ref, joined_ref, ups_ref, joined_scr, ups_scr,
):
    @pl.when(pl.program_id(0) == 0)
    def _():
        join_packs((one_qk, one_v), (two_qk, two_v), ups_one, ups_two, joined_scr, ups_scr)

    project_pair(normed_ref, mixed_ref, joined_scr, ups_scr, q_ref, k_ref, v_ref, joined_ref, ups_ref)
    forward_attention(place, lengths, q_ref, k_ref, v_ref, ups_one, ups_two, map_ref, o_ref, lse_ref, tile_ref)


def split_pair(rows):
    lanes = lane_index(rows.shape)
    zero = jnp.zeros_like(rows)
    return jnp.concatenate([jnp.where(lanes < HEAD_WIDTH, rows, zero), jnp.where(lanes < HEAD_WIDTH, zero, rows)], 0)


def merge_pair(turned):
    return jnp.concatenate([turned[:HEAD_WIDTH, :LANES], turned[HEAD_WIDTH:, LANES:]], 0).T


def bucket_hot(map_ref):
    rows = lax.broadcasted_iota(jnp.int32, (BUCKETS, 2 * LONG_LEN), 0)
    return rows == map_ref[...]


def build_tiles(one_ref, two_ref, map_ref, tile_ref):
    pair = pl.program_id(0)
    hot = bucket_hot(map_ref).astype(bf16)
    table = jnp.concatenate(
        [one_ref[LORA : LORA + 8, :BUCKETS].astype(f32), two_ref[LORA : LORA + 8, :BUCKETS].astype(f32)], 0
    )
    by_offset = nn(table.astype(bf16), hot)
    heads = lax.broadcasted_iota(jnp.int32, (16, 1), 0)
    heads = jnp.where(heads < 8, heads, heads - 5)
    used = lax.broadcasted_iota(jnp.int32, (16, 1), 0)
    heads = jnp.where((used < 3) | ((used >= 8) & (used < 11)), heads, -1)
    rows_in = lax.broadcasted_iota(jnp.int32, (LANES, LANES), 0)
    lanes = lane_index((LANES, LANES))
    for t in range(2):
        row = jnp.sum(jnp.where(heads == 2 * pair + t, by_offset, 0.0), 0, keepdims=True)
        for d in range(7):
            block = 6 - d
            low = jnp.broadcast_to(row[:, LANES * block : LANES * block + LANES], (LANES, LANES))
            high = jnp.broadcast_to(row[:, LANES * block + LANES : LANES * block + 2 * LANES], (LANES, LANES))
            low = pltpu.roll(low, 1, 1, stride=1, stride_axis=0)
            high = pltpu.roll(high, 1, 1, stride=1, stride_axis=0)
            tile_ref[d, :, LANES * t : LANES * t + LANES] = jnp.where(lanes <= rows_in, low, high).astype(bf16)


def chunk_layout():
    chunks = []
    for c in range(LONG_LEN // LANES):
        chunks.append((HALF_ROWS, LONG_LEN, HALF_ROWS + LANES * c, 3 - c, 4))
    for s in range(HALF_ROWS // SHORT_LEN):
        chunks.append((LANES * s, SHORT_LEN, LANES * s, 3, s))
    return chunks


def length_of(place, lengths, which):
    m = place[0]
    if which == 4:
        return lengths[SHORT_SEQS + m]
    return lengths[4 * m + which]


def tiles_of(tile_ref, first, span):
    return jnp.concatenate([tile_ref[first + b].astype(f32) for b in range(span // LANES)], 0)


def biased(scores, tiles, length):
    scores = scores + tiles
    positions = lax.broadcasted_iota(jnp.int32, scores.shape, 0)
    return jnp.where(positions < length, scores, NEG)


def forward_attention(place, lengths, q_ref, k_ref, v_ref, one_ref, two_ref, map_ref, o_ref, lse_ref, tile_ref):
    tiles = tile_ref.at[0]
    build_tiles(one_ref, two_ref, map_ref, tiles)
    chunks = chunk_layout()
    raw = []
    for key_row, span, query_row, first, which in chunks:
        queries = split_pair(q_ref[query_row : query_row + LANES, :])
        raw.append(nt(k_ref[key_row : key_row + span, :], queries))
    weights = []
    for number, (key_row, span, query_row, first, which) in enumerate(chunks):
        scores = biased(raw[number], tiles_of(tiles, first, span), length_of(place, lengths, which))
        peak = jnp.max(scores, 0, keepdims=True)
        raised = jnp.exp(scores - peak)
        total = jnp.sum(raised, 0, keepdims=True)
        lse_ref[0, number : number + 1, :] = peak + jnp.log(total)
        weights.append((raised * (1.0 / total)).astype(bf16))
    turned = v_ref[HALF_ROWS:, :].T
    for number, (key_row, span, query_row, first, which) in enumerate(chunks):
        if which != 4:
            turned = v_ref[key_row : key_row + span, :].T
        o_ref[query_row : query_row + LANES, :] = merge_pair(nn(turned, weights[number])).astype(bf16)


def part_chunks(part):
    if part == 1:
        return [(c, 0, LONG_LEN, LANES * c, 3 - c, 4) for c in range(LONG_LEN // LANES)]
    return [(4 + s, LANES * s, SHORT_LEN, LANES * s, 0, s) for s in range(HALF_ROWS // SHORT_LEN)]


PAIRS = 2


def backward_attention(
    part, place, lengths, q_ref, k_ref, v_ref, do_ref, lse_ref, tile_ref, map_ref, turn_ref, table_scr, gathered
):
    turn = turn_ref[...]
    chunks = part_chunks(part)
    work = [(pair, c) + chunk for pair in range(PAIRS) for c, chunk in enumerate(chunks)]
    raw, grad_probs, kept = [], [], []
    for pair, c, number, key_row, span, query_row, first, which in work:
        cols = slice(LANES * pair, LANES * pair + LANES)
        queries = split_pair(q_ref[query_row : query_row + LANES, cols])
        douts = split_pair(do_ref[query_row : query_row + LANES, cols])
        raw.append(nt(k_ref[key_row : key_row + span, cols], queries))
        grad_probs.append(nt(v_ref[key_row : key_row + span, cols], douts))
        kept.append((queries, douts))
    grads, weights = [], []
    for i, (pair, c, number, key_row, span, query_row, first, which) in enumerate(work):
        scores = biased(raw[i], tiles_of(tile_ref.at[pair], first, span), length_of(place, lengths, which))
        probs = jnp.exp(scores - lse_ref[pair, number : number + 1, :])
        weights.append(probs.astype(bf16))
        weighted = probs * grad_probs[i]
        inner = jnp.sum(weighted, 0, keepdims=True)
        grads.append((weighted - probs * inner).astype(bf16))
        if part == 1:
            weights_all, grads_all, queries_all, douts_all = gathered
            at = slice(2 * LANES * c, 2 * LANES * c + 2 * LANES)
            weights_all[pair, :, at] = weights[i]
            grads_all[pair, :, at] = grads[i]
            queries_all[pair, at, :] = kept[i][0]
            douts_all[pair, at, :] = kept[i][1]
    result = []
    for pair in range(PAIRS):
        cols = slice(LANES * pair, LANES * pair + LANES)
        turned = k_ref[:, cols].T if part == 1 else None
        dq, dk, dv = [], [], []
        for i, (of, c, number, key_row, span, query_row, first, which) in enumerate(work):
            if of != pair:
                continue
            if part == 0:
                turned = k_ref[key_row : key_row + span, cols].T
                dv.append(nn(weights[i], kept[i][1]).astype(bf16))
                dk.append(nn(grads[i], kept[i][0]).astype(bf16))
            dq.append(merge_pair(nn(turned, grads[i])).astype(bf16))
        if part == 1:
            dv.append(nn(weights_all[pair], douts_all[pair]).astype(bf16))
            dk.append(nn(grads_all[pair], queries_all[pair]).astype(bf16))
        result.append((dq, dk, dv))
    rows_in = lax.broadcasted_iota(jnp.int32, (LANES, LANES), 0)
    lanes = lane_index((LANES, LANES))
    sums = []
    for pair in range(PAIRS):
        mine = grads[len(chunks) * pair : len(chunks) * pair + len(chunks)]
        pieces = [[jnp.zeros((1, LANES), f32) for _ in range(8)] for _ in range(2)]
        for d in range(7):
            if part == 0:
                stack = mine if d == 3 else []
            else:
                stack = [mine[c][LANES * (d - 3 + c) : LANES * (d - 2 + c), :] for c in range(4) if 0 <= d - 3 + c < 4]
            if len(stack) == 0:
                continue
            diagonal = nn(jnp.concatenate([turn] * len(stack), 1), jnp.concatenate(stack, 0))
            block = 6 - d
            for t in range(2):
                rolled = pltpu.roll(diagonal[:, LANES * t : LANES * t + LANES], 0, 1, stride=1, stride_axis=0)
                low = jnp.where(lanes >= rows_in, rolled, 0.0)
                pieces[t][block] = pieces[t][block] + jnp.sum(low, 0, keepdims=True)
                pieces[t][block + 1] = pieces[t][block + 1] + jnp.sum(rolled - low, 0, keepdims=True)
        sums += [jnp.concatenate(p, 1) for p in pieces]
    sums = jnp.concatenate(sums + [jnp.zeros((8 - 2 * PAIRS, 2 * LONG_LEN), f32)], 0)
    hot = bucket_hot(map_ref).astype(f32)
    table = lax.dot_general(
        sums, hot, (((1,), (1,)), ((), ())), precision=lax.Precision.HIGHEST, preferred_element_type=f32
    )
    table_scr[pl.program_id(0)] = jnp.concatenate([table, jnp.zeros((8, LANES - BUCKETS), f32)], 1)
    return result


WIDER = MODEL_WIDTH + LANES


def feedforward_shard(inputs, douts, win_scr, wout_scr, ready=lambda: None):
    before = nn(inputs[...], win_scr[...])
    ready()
    inputs, douts = inputs[...], douts[...]
    sig = 0.5 * jnp.tanh(0.5 * before) + 0.5
    active = (before * sig).astype(bf16)
    out = nn(active, wout_scr[...])
    grad_active = nt(douts, wout_scr[...]).astype(bf16).astype(f32)
    grad_before = (sig * (1.0 + before * (1.0 - sig)) * grad_active).astype(bf16)
    back = nt(grad_before, win_scr[...])
    grad_up = tn(inputs[:, MODEL_WIDTH:], grad_before)[:LORA]
    grad_low = tn(douts[:, MODEL_WIDTH:], active)[:LORA]
    return out, back, grad_up, grad_low


def fill_adapters(win_scr, wout_scr, up, low):
    win_scr[MODEL_WIDTH:, :] = pad_to(up[:LORA, :].astype(f32), LANES).astype(bf16)
    wout_scr[:, MODEL_WIDTH:] = pad_to(low[...].astype(f32), LANES).T.astype(bf16)


def shard_copies(wins, wouts, half, win_scr, wout_scr, sems, first):
    pieces = []
    if len(wins) == 1:
        pieces.append((wins[0], win_scr.at[pl.ds(0, MODEL_WIDTH)]))
    else:
        rows = MODEL_WIDTH // 2
        for k in range(2):
            there = pl.ds(pl.multiple_of(rows * jnp.bitwise_xor(half, k), rows), rows)
            pieces.append((wins[k].at[pl.ds(SECOND_ROWS, rows)], win_scr.at[there]))
    pieces.append((wouts[0], wout_scr.at[:, pl.ds(0, MODEL_WIDTH)]))
    return [pltpu.make_async_copy(source, goal, sems.at[first + i]) for i, (source, goal) in enumerate(pieces)]


def fill_output_maps(place, ao_in, bo_in, ao_scr, bo_scr):
    bo_scr[...] = pad_to(bo_in[...].astype(f32), LANES).astype(bf16)
    for at in range(4):

        @pl.when(place[0] == at)
        def _():
            pieces = [ao_in[:, 192 * (at ^ j) : 192 * (at ^ j) + 192] for j in range(4)]
            ao_scr[...] = pad_to(jnp.concatenate(pieces, 1).astype(f32), LANES).astype(bf16)


def start(copies):
    for copy in copies:
        copy.start()


def wait(copies):
    for copy in copies:
        copy.wait()


def both_blocks():
    return [slice(HALF_ROWS * i, HALF_ROWS * i + HALF_ROWS) for i in range(2)]


def middle_kernel(
    place, x_ref, cot_ref, att_ref, wo0, wo1, wo2, wo3, spread1_ref, win0, wout0, win1, wout1,
    ao_in, bo_in, gain_ref, down_in, router_ref, bf_in, up0, low0, up1, low1,
    hidden, inputs_ref, douts_ref, narrow, out_ref, back_ref, shard_ref,
    ao_scr, bo_scr, wo_scr, down_scr, bf_scr, win_scr, wout_scr,
):
    @pl.when(pl.program_id(0) == 0)
    def _():
        fill_output_maps(place, ao_in, bo_in, ao_scr, bo_scr)
        for j, wo in enumerate((wo0, wo1, wo2, wo3)):
            wo_scr[192 * j : 192 * j + 192, :] = wo[...]
        down_scr[...] = down_rows([down_in[...]], repeated_router(router_ref[...], 1))
        bf_scr[...] = pad_to(bf_in[...].astype(f32), LANES).astype(bf16)
        for j, (win, wout, up, low) in enumerate(((win0, wout0, up0, low0), (win1, wout1, up1, low1))):
            win_scr[j, :MODEL_WIDTH, :] = win[...]
            wout_scr[j, :, :MODEL_WIDTH] = wout[...]
            fill_adapters(win_scr.at[j], wout_scr.at[j], up, low)
        shard_ref[...] = jnp.zeros_like(shard_ref)

    attended = att_ref[...]
    downo = nt(attended, ao_scr[...])
    mixo = (spread1_ref[...] * downo).astype(bf16)
    held = x_ref[...].astype(f32) + (nn(attended, wo_scr[...]) + nn(mixo, bo_scr[...]))
    hidden[...] = held
    scale = lax.rsqrt(jnp.mean(held * held, -1, keepdims=True) + EPS)
    normed = (held * scale * gain_ref[...].astype(f32)).astype(bf16)
    both = nt(normed, down_scr[...])
    downi = both[:, :LANES]
    spread = softmax_repeated(both[:, LANES:], LORA, 1.0 * ADAPTER_RANK)
    cot = cot_ref[...]
    sidef = nt(cot, bf_scr[...])
    inputs = jnp.concatenate([normed, (spread * downi).astype(bf16)], 1)
    douts = jnp.concatenate([cot, (spread * sidef).astype(bf16)], 1)
    inputs_ref[...] = inputs
    douts_ref[...] = douts
    narrow[:, :LANES] = spread
    narrow[:, LANES : 2 * LANES] = downi
    narrow[:, 2 * LANES : 3 * LANES] = sidef
    narrow[:, 3 * LANES :] = downo
    for j in range(2):
        out, back, grad_up, grad_low = feedforward_shard(inputs, douts, win_scr.at[j], wout_scr.at[j])
        if j == 0:
            out_ref[...] = out
            back_ref[...] = back
        else:
            out_ref[...] += out
            back_ref[...] += back
        shard_ref[j, 0] += grad_up
        shard_ref[j, 1] += grad_low


FF_ROWS, AT_ROWS = 120, 88
FF_ALL, FF_OWN, AT_ALL, AT_OWN = 512, 256, 384, 256
FIRST_ROWS = 256


def send_pieces(pieces, own_ref, sent_refs):
    own_ref[...] = pieces[0]
    for j, sent in enumerate(sent_refs):
        sent[...] = pieces[j + 1].astype(bf16)


def post_kernel(
    place, half, att, wo0, wo1, wo2, wo3, spread1, win0, win1, wout0, win2, win3, wout1,
    hidden_in, inputs_in, douts_in, narrow_in, out_in, back_in,
    ao_in, bo_in, gain_ref, down_in, router_ref, bf_in, up0, low0, up1, low1, group_ref, pick_ref, shard_ref,
    result_out, ghidden_out, gatt_out, prod_out, ao_grad, ff_ref,
    att_scr, spread1_scr, hidden, inputs, douts, narrow, out, back, result, ghidden_scr, gatt, prod,
    ao_scr, bo_scr, wo_scr, down_scr, bf_scr, win_scr, wout_scr,
    shard_acc, pair_acc, bff_acc, bo_acc, ao_acc, gain_acc, pieces, flat, arrived, left,
):
    def copies(pairs, at):
        return [pltpu.make_async_copy(source, goal, arrived.at[at + i]) for i, (source, goal) in enumerate(pairs)]

    early = copies([(inputs_in, inputs), (douts_in, douts)], 0)
    first = shard_copies((win0, win1), (wout0,), half[0], win_scr.at[0], wout_scr.at[0], arrived, 2)
    second = shard_copies((win2, win3), (wout1,), half[0], win_scr.at[1], wout_scr.at[1], arrived, 5)
    sums = copies([(out_in, out), (back_in, back)], 8)
    rest = [(hidden_in, hidden), (narrow_in, narrow), (att, att_scr), (spread1, spread1_scr)]
    rest += [(wo.at[pl.ds(0, 192)], wo_scr.at[pl.ds(192 * j, 192)]) for j, wo in enumerate((wo0, wo1, wo2, wo3))]
    rest = copies(rest, 10)
    start(early[:1] + first + early[1:] + sums + second + rest)
    fill_output_maps(place, ao_in, bo_in, ao_scr, bo_scr)
    down_scr[...] = down_rows([down_in[...]], router_ref[...])
    bf_scr[...] = pad_to(bf_in[...].astype(f32), LANES).astype(bf16)
    fill_adapters(win_scr.at[0], wout_scr.at[0], up0, low0)
    fill_adapters(win_scr.at[1], wout_scr.at[1], up1, low1)
    for j, weights in enumerate((first, second)):
        wait(weights[:2])
        if j == 0:
            wait(early[:1])

        def ready():
            wait(weights[2:])
            if j == 0:
                wait(early[1:])

        more_out, more_back, grad_up, grad_low = feedforward_shard(inputs, douts, win_scr.at[j], wout_scr.at[j], ready)
        if j == 0:
            wait(sums)
        out[...] += more_out
        back[...] += more_back
        shard_acc[j, 0] = grad_up
        shard_acc[j, 1] = grad_low
    wait(rest)
    leaving = []

    def send(scr, goal, where):
        leaving.append(pltpu.make_async_copy(scr.at[where], goal.at[where], left.at[len(leaving)]))
        leaving[-1].start()

    def gather(scr, value, fresh):
        if fresh:
            scr[...] = value
        else:
            scr[...] += value

    def block(i, rows):
        where = pl.ds(HALF_ROWS * i, HALF_ROWS)
        normed, cot = inputs[rows, :MODEL_WIDTH], douts[rows, :MODEL_WIDTH]
        downf, sidei = out[rows, MODEL_WIDTH:], back[rows, MODEL_WIDTH:]
        spread, downi = narrow[rows, :LANES], narrow[rows, LANES : 2 * LANES]
        sidef, downo = narrow[rows, 2 * LANES : 3 * LANES], narrow[rows, 3 * LANES :]
        gates = spread1_scr[rows, :]
        held = hidden[rows, :]
        mixf = (spread * downf).astype(bf16)
        gdowni = (spread * sidei).astype(bf16)
        logit = logit_gradient(downf * sidef + downi * sidei, spread, group_ref[...], pick_ref[...])
        pair = jnp.concatenate([gdowni, logit], 1)
        yield
        grad_normed = back[rows, :MODEL_WIDTH] + nn(pair, down_scr[...])
        result[rows, :] = (held + (out[rows, :MODEL_WIDTH] + nn(mixf, bf_scr[...]))).astype(bf16)
        send(result, result_out, where)
        yield
        scale = lax.rsqrt(jnp.mean(held * held, -1, keepdims=True) + EPS)
        weighted = grad_normed * gain_ref[...].astype(f32)
        inner = jnp.mean(weighted * held, -1, keepdims=True)
        ghidden = cot.astype(f32) + scale * weighted - held * (scale * scale * scale * inner)
        branch = ghidden.astype(bf16)
        ghidden_scr[rows, :] = ghidden
        send(ghidden_scr, ghidden_out, where)
        gather(gain_acc, jnp.sum(grad_normed * held * scale, 0, keepdims=True), i == 0)
        yield
        sideo = nt(branch, bo_scr[...])
        through = nt(branch, wo_scr[...])
        gather(pair_acc, tn(pair, normed), i == 0)
        gather(bff_acc, tn(mixf, cot), i == 0)
        yield
        gdowno = (gates * sideo).astype(bf16)
        prod[rows, :] = downo * sideo
        send(prod, prod_out, where)
        gatt[rows, :] = (through + nn(gdowno, ao_scr[...])).astype(bf16)
        send(gatt, gatt_out, where)
        gather(bo_acc, tn((gates * downo).astype(bf16), branch), i == 0)
        gather(ao_acc, tn(gdowno, att_scr[rows, :]), i == 0)
        yield

    for _ in zip(*[block(i, rows) for i, rows in enumerate(both_blocks())]):
        pass
    ao_grad[...] = ao_acc[:LORA]
    quarters = (pair_acc[:LORA], bff_acc[:LORA], bo_acc[:LORA], router_quarter(pair_acc, gain_acc))
    for j in range(4):
        source, at = (shard_ref, j) if j < 2 else (shard_acc, j - 2)
        pieces[j, 0:LORA] = source[at, 0]
        pieces[j, LORA : 2 * LORA] = source[at, 1]
        pieces[jnp.bitwise_xor(place[0], j), 2 * LORA : 3 * LORA] = quarters[j]
    devices = ff_ref.shape[0]
    every, mine = FF_ALL // devices, FF_OWN // devices
    flat[...] = jnp.zeros_like(flat)
    for j in range(4):
        for t in range(6):
            cols = slice(LANES * t, LANES * t + LANES)
            flat[2 * LORA * t : 2 * LORA * t + 2 * LORA, :] = pieces[j, LORA:, cols]
            flat[FF_ALL + LORA * t : FF_ALL + LORA * t + LORA, :] = pieces[j, :LORA, cols]
        for k in range(devices):
            chunk = [flat[every * k : every * k + every, :], flat[FF_ALL + mine * k : FF_ALL + mine * k + mine, :]]
            ff_ref[k, (every + mine) * j : (every + mine) * (j + 1), :] = jnp.concatenate(chunk, 0).astype(bf16)
    wait(leaving)


def router_quarter(pair_acc, gain_acc):
    gain = jnp.broadcast_to(gain_acc[...], (8, MODEL_WIDTH))
    return jnp.concatenate([pair_acc[LANES : LANES + 16, :], gain, jnp.zeros((16, MODEL_WIDTH), f32)], 0)


def back_part(
    part, place, lengths, q_ref, k_ref, v_ref, do_ref, lse_ref, tile_ref, map_ref, turn_ref, joined_ref, ups_ref,
    mixed_ref, normed_in, spread_in, downs_in_rows, prod_in, ghidden_in, tokens, gain_ref, downs_in, router_ref,
    group_ref, pick_ref, up_scr, table_scr, sides_scr, side_scr, gnormed, down_scr,
    normed_ref, spread_ref, downs_ref, prod_ref, ghidden_ref, x_ref, sems, gathered, finish,
):
    pair = pl.program_id(0)

    def late_copies():
        rows = pl.ds(HALF_ROWS * part, HALF_ROWS)
        own_rows = pl.ds(pl.multiple_of(HALF_ROWS * (place[0] + 4 * part), HALF_ROWS), HALF_ROWS)
        sources = [normed_in.at[rows], spread_in.at[rows], downs_in_rows.at[rows], prod_in.at[rows], ghidden_in.at[rows]]
        goals = [normed_ref, spread_ref, downs_ref, prod_ref, ghidden_ref, x_ref]
        return [
            pltpu.make_async_copy(source, goal, sems.at[i])
            for i, (source, goal) in enumerate(zip(sources + [tokens.at[own_rows]], goals))
        ]

    @pl.when(pair == 0)
    def _():
        start(late_copies())

    grads = backward_attention(
        part, place, lengths, q_ref, k_ref, v_ref, do_ref, lse_ref, tile_ref, map_ref, turn_ref, table_scr, gathered
    )
    for i, blocks in enumerate(grads):
        for kind in range(3):
            at = LANES * (3 * i + kind)
            sides_scr[:, at : at + LANES] = jnp.concatenate(blocks[kind], 0)
    sides = sides_scr[...]
    joined = joined_ref[...].reshape(-1, MODEL_WIDTH)
    ups = jnp.concatenate([ups_ref[i] for i in range(PAIRS)], 1)
    up = tn(mixed_ref[...], sides)
    pieces = []
    for i in range(3 * PAIRS):
        rows = slice(LORA * (i % 3), LORA * (i % 3) + LORA)
        pieces.append(up[rows, LANES * i : LANES * i + LANES])
    up_scr[pair] = jnp.concatenate(pieces, 1)

    @pl.when(pair == 0)
    def _():
        gnormed[...] = nn(sides, joined)
        side_scr[...] = nt(sides, ups)

    @pl.when(pair > 0)
    def _():
        gnormed[...] += nn(sides, joined)
        side_scr[...] += nt(sides, ups)

    @pl.when(pair == pl.num_programs(0) - 1)
    def _():
        down_scr[...] = down_rows([downs_in[0], downs_in[1], downs_in[2]], router_ref[...])
        wait(late_copies())
        side = side_scr[...]
        spread = spread_ref[...]
        gdown = (spread * side).astype(bf16)
        gates = jnp.where(lane_index(spread.shape) < LORA, spread, 0.0)
        logit = logit_gradient(downs_ref[...] * side + prod_ref[...], gates, group_ref[...], pick_ref[...])
        both = jnp.concatenate([gdown, logit], 1)
        grad_normed = gnormed[...] + nn(both, down_scr[...])
        x = x_ref[...].astype(f32)
        scale = lax.rsqrt(jnp.mean(x * x, -1, keepdims=True) + EPS)
        weighted = grad_normed * gain_ref[...].astype(f32)
        inner = jnp.mean(weighted * x, -1, keepdims=True)
        gtokens = (ghidden_ref[...] + scale * weighted - x * (scale * scale * scale * inner)).astype(bf16)
        finish(gtokens, tn(both, normed_ref[...]), jnp.sum(grad_normed * x * scale, 0, keepdims=True))


def short_kernel(*refs):
    ins, outs, scratch = refs[:24], refs[24:30], refs[30:]
    ga_ref, gb_ref, up_ref, pair_ref, ggain_ref, table_ref = outs

    def finish(gtokens, pair_grad, ggain):
        ga_ref[...] = gtokens[:FIRST_ROWS]
        gb_ref[...] = gtokens[FIRST_ROWS:]
        pair_ref[...] = pair_grad
        ggain_ref[...] = ggain

    back_part(0, *ins, up_ref, table_ref, *scratch, None, finish)


def long_kernel(*refs):
    place, ins, more, outs, scratch = refs[0], refs[:24], refs[24:30], refs[30:36], refs[36:]
    ao_grad, up_in, pair_in, ggain_in, table_in, gb_in = more
    gtokens_ref, ggain_ref, own_ref, sent1, sent2, sent3 = outs
    up_scr, table_scr, pair_acc, pieces = scratch[:4]

    def finish(gtokens, pair_grad, ggain):
        gtokens_ref[: HALF_ROWS - FIRST_ROWS, :] = gb_in[...]
        gtokens_ref[HALF_ROWS - FIRST_ROWS :, :] = gtokens
        ggain_ref[...] = ggain + ggain_in[...]
        pair_acc[...] = pair_grad + pair_in[...]
        quarters = (
            pair_acc[0:LORA],
            pair_acc[LORA : 2 * LORA],
            pair_acc[2 * LORA : 3 * LORA],
            jnp.concatenate([pair_acc[LANES : LANES + 16, :], jnp.zeros((24, MODEL_WIDTH), f32)], 0),
        )
        ups = []
        for half in range(2):
            for part in range(3):
                pairs = []
                for p in range(3 * half, 3 * half + 3):
                    cols = slice(384 * (p % PAIRS) + LANES * part, 384 * (p % PAIRS) + LANES * part + LANES)
                    pairs.append(up_scr[p // PAIRS, :, cols] + up_in[p // PAIRS, :, cols])
                ups.append(jnp.concatenate(pairs, 1))
        for j in range(4):
            half, odd = j // 2, j % 2
            parts = [ao_grad[:, 192 * j : 192 * j + 192]]
            parts += [ups[3 * half + part][:, 192 * odd : 192 * odd + 192] for part in range(3)]
            pieces[j, 0:LORA] = jnp.concatenate(parts, 1)
            pieces[jnp.bitwise_xor(place[0], j), LORA : 2 * LORA] = quarters[j]
            heads = [3 * j + i for i in range(3)]
            rows = []
            for head in heads:
                step, row = head // (2 * PAIRS), head % (2 * PAIRS)
                rows.append(table_scr[step, row : row + 1, :] + table_in[step, row : row + 1, :])
            rows = jnp.concatenate(rows + [jnp.zeros((5, LANES), f32)], 0)
            pieces[j, 2 * LORA : 2 * LORA + 8] = jnp.concatenate([rows, jnp.zeros((8, MODEL_WIDTH - LANES), f32)], 1)
        send_pieces(pieces, own_ref, (sent1, sent2, sent3))

    back_part(1, *ins, up_scr, table_scr, *scratch[4:15], scratch[15:], finish)


def spread_kernel(layout, place, *refs):
    out_ref, held, arrived, left = refs[-4:]
    inward, outward = [], []
    at = 0
    for (j, first), source in zip(layout, refs):
        count = source.shape[0]
        inward.append(pltpu.make_async_copy(source, held.at[pl.ds(at, count)], arrived.at[len(inward)]))
        there = jnp.bitwise_xor(place[0], j)
        onward = []
        row = first
        while row < first + count:
            part, offset = divmod(row, HALF_ROWS)
            rows = min(HALF_ROWS - offset, first + count - row)
            goal = pl.multiple_of(HALF_ROWS * (4 * part + there), HALF_ROWS) + offset
            goal = out_ref.at[pl.ds(pl.multiple_of(goal, FIRST_ROWS), rows)]
            number = sum(len(o) for o in outward) + len(onward)
            onward.append(pltpu.make_async_copy(held.at[pl.ds(at + row - first, rows)], goal, left.at[number]))
            row += rows
        outward.append(onward)
        at += count
    for copy in inward:
        copy.start()
    for copy, onward in zip(inward, outward):
        copy.wait()
        start(onward)
    for onward in outward:
        wait(onward)


def sum_kernel(at0, at1, at2, at3, ggain, out_ref, flat):
    at = at0[...] + at1[...].astype(f32) + at2[...].astype(f32) + at3[...].astype(f32)
    flat[...] = jnp.zeros_like(flat)
    for t in range(6):
        part = at[:, LANES * t : LANES * t + LANES]
        flat[LORA * t : LORA * t + LORA, :] = part[LORA : 2 * LORA]
        first = LORA * (6 + t) if t < 2 else AT_ALL + LORA * (t - 2)
        flat[first : first + LORA, :] = part[:LORA]
    flat[AT_ALL + 4 * LORA : AT_ALL + 4 * LORA + 8, :] = at[2 * LORA :, :LANES]
    gain = jnp.concatenate([ggain[:, LANES * t : LANES * t + LANES] for t in range(6)], 0)
    flat[8 * LORA : 8 * LORA + 8, :] = pad_to(gain, 8)
    devices = out_ref.shape[0]
    every, mine = AT_ALL // devices, AT_OWN // devices
    for k in range(devices):
        chunk = [flat[every * k : every * k + every, :], flat[AT_ALL + mine * k : AT_ALL + mine * k + mine, :]]
        out_ref[k] = jnp.concatenate(chunk, 0).astype(bf16)


def unpack_kernel(
    place, own, one, two, three, gain1_ref, gain2_ref, qkv_ref, bq_ref, bkv_ref, ao_ref, bo_ref, ai_ref, bi_ref,
    aff_ref, bff_ref, r1_ref, r2_ref, table_ref, quarters2, quarters1, ffs, ats, ff_own, at_own,
):
    devices = own.shape[0]
    ff_all, ff_mine, at_all, at_mine = FF_ALL // devices, FF_OWN // devices, AT_ALL // devices, AT_OWN // devices
    for k in range(devices):
        for j, ref in enumerate((own, one, two, three)):
            both = ref[k].astype(f32)
            ffs[j, ff_all * k : ff_all * k + ff_all, :] = both[:ff_all]
            ats[j, at_all * k : at_all * k + at_all, :] = both[ff_all : ff_all + at_all]
            if j == 0:
                rest = both[ff_all + at_all :]
                ff_own[ff_mine * k : ff_mine * k + ff_mine, :] = rest[:ff_mine]
                at_own[at_mine * k : at_mine * k + at_mine, :] = rest[ff_mine:]

    def rows_of(ref, first, step):
        return jnp.concatenate([ref[first + step * t : first + step * t + LORA, :] for t in range(6)], 1)

    m = place[0]
    bi_ref[...] = rows_of(ff_own, 0, LORA)
    blocks = [ats[0, 6 * LORA + LORA * t : 7 * LORA + LORA * t, :] for t in range(2)]
    blocks += [at_own[LORA * t : LORA * t + LORA, :] for t in range(4)]
    mine = jnp.concatenate(blocks, 1)
    bq_ref[...] = mine[:, 192:384]
    bkv_ref[0] = mine[:, 384:576]
    bkv_ref[1] = mine[:, 576:768]
    table_ref[...] = at_own[4 * LORA : 4 * LORA + 3, :BUCKETS]
    for j in range(4):
        there = jnp.bitwise_xor(m, j)
        quarters2[there] = rows_of(ffs.at[j], LORA, 2 * LORA)
        quarters1[there] = rows_of(ats.at[j], 0, LORA)
        low = rows_of(ffs.at[j], 0, 2 * LORA)
        out = [ats[j, 6 * LORA + LORA * t : 7 * LORA + LORA * t, :] for t in range(2)]
        out = jnp.concatenate(out, 1)[:, :192]
        for at in range(4):

            @pl.when(there == at)
            def _():
                aff_ref[:, MODEL_WIDTH * at : MODEL_WIDTH * at + MODEL_WIDTH] = low
                ao_ref[:, 192 * at : 192 * at + 192] = out

    for part in range(3):
        qkv_ref[part] = quarters1[part]
    ai_ref[...] = quarters2[0]
    bff_ref[...] = quarters2[1]
    bo_ref[...] = quarters2[2]
    r1_ref[...] = quarters1[3, :EXPERTS]
    r2_ref[...] = quarters2[3, :EXPERTS]
    total = jnp.zeros((8, LANES), f32)
    for j in range(4):
        total = total + ats[j, 8 * LORA : 8 * LORA + 8, :]
    gain1_ref[...] = total[:6]
    gain2_ref[...] = jnp.concatenate([quarters2[3, 16:17, LANES * t : LANES * t + LANES] for t in range(6)], 0)


def whole(array):
    return pl.BlockSpec(array.shape, lambda *_: (0,) * array.ndim)


def rows_block(array):
    return pl.BlockSpec((HALF_ROWS, array.shape[1]), lambda i, *_: (i, 0))


def token_block():
    return pl.BlockSpec((HALF_ROWS, MODEL_WIDTH), lambda i, place, *_: (place[0] + 4 * i, 0))


def shape(dims, dtype):
    return jax.ShapeDtypeStruct(dims, dtype)


def call(kernel, grid, scalars, inputs, in_specs, outs, out_specs, scratch=(), aliases=None, limit=VMEM_LIMIT):
    return pl.pallas_call(
        kernel,
        grid_spec=pltpu.PrefetchScalarGridSpec(
            num_scalar_prefetch=len(scalars),
            grid=grid,
            in_specs=in_specs,
            out_specs=out_specs,
            scratch_shapes=list(scratch),
        ),
        out_shape=outs,
        input_output_aliases=aliases or {},
        compiler_params=pltpu.CompilerParams(vmem_limit_bytes=limit),
        cost_estimate=pl.CostEstimate(flops=0, bytes_accessed=0, transcendentals=0),
    )(*scalars, *inputs)


def exchange(value, axis, size, mask):
    return lax.ppermute(value, axis, [(i, i ^ mask) for i in range(size)])


def scatter_over(flat, axis, size):
    pieces = lax.all_to_all(flat, axis, 0, 0)
    return jnp.sum(pieces.astype(f32), 0)


def gather_over(mine, axis, size):
    return lax.all_to_all(jnp.broadcast_to(mine[None], (size,) + mine.shape), axis, 0, 0)


def constants():
    group1 = np.zeros((LANES, LANES), np.float32)
    for i in range(3 * LORA):
        for j in range(LORA):
            group1[i, j] = float((i % LORA) // ADAPTER_RANK == j // ADAPTER_RANK)
    pick = np.zeros((LANES, LANES), np.float32)
    for e in range(EXPERTS):
        pick[ADAPTER_RANK * e, e] = 1.0
    turn = np.eye(LANES, dtype=np.float32)[::-1].copy()
    return tuple(jnp.asarray(c, bf16) for c in (group1, pick, turn))


def local(
    dp_size,
    mp_size,
    tokens,
    cotangent,
    attention_norm_gain,
    feedforward_norm_gain,
    query_projection_weight,
    key_value_weight,
    attention_output_weight,
    ffn_input_weight,
    ffn_output_weight,
    projection_down_weight,
    query_up_weight,
    key_value_up_weight,
    attention_output_down_weight,
    attention_output_up_weight,
    ffn_input_down_weight,
    ffn_input_up_weight,
    ffn_output_down_weight,
    ffn_output_up_weight,
    attention_router_weight,
    feedforward_router_weight,
    bucket_bias_table,
    offset_bucket_map,
    sequence_length_list,
):
    m = lax.axis_index("mp").astype(jnp.int32)
    d = lax.axis_index("dp").astype(jnp.int32)
    place = m.reshape(1)
    group, pick, turn = constants()

    def mp_swap(value, mask):
        return exchange(value, "mp", mp_size, mask)

    def pack_part(rows, index):
        return pl.BlockSpec((rows, MODEL_WIDTH), lambda *_: (index, 0))

    def element_part(rows, first):
        return pl.BlockSpec((pl.Element(rows), pl.Element(MODEL_WIDTH)), lambda *_: (first, 0))

    win0, wout0 = ffn_input_weight, ffn_output_weight
    half = (d & 1).reshape(1)
    inputs = [
        query_projection_weight.T,
        jnp.transpose(key_value_weight, (0, 2, 1)),
        query_up_weight,
        key_value_up_weight,
        bucket_bias_table.T,
        attention_output_weight,
        ffn_input_up_weight,
        win0,
    ]
    outs = [
        shape((rows, MODEL_WIDTH), bf16)
        for rows in (QK_ROWS, V_ROWS, SECOND_ROWS + HALF_SHARD, SECOND_ROWS + QK_ROWS + V_ROWS)
    ]
    *pack0, more0, both0 = call(
        pack_kernel,
        (1,),
        [half],
        inputs,
        [whole(a) for a in inputs[:-1]] + [pl.BlockSpec((HALF_SHARD, MODEL_WIDTH), lambda i, half: (half[0], 0))],
        outs,
        [whole(o) for o in outs],
    )
    pack2 = [mp_swap(p, 2) for p in pack0]
    both1 = mp_swap(both0, 1)
    more2 = mp_swap(more0, 2)
    wout2 = mp_swap(wout0, 2)

    gain1 = attention_norm_gain.reshape(1, -1)
    gain2 = feedforward_norm_gain.reshape(1, -1)
    downs_in = jnp.transpose(projection_down_weight, (0, 2, 1))
    router1, router2 = attention_router_weight.T, feedforward_router_weight.T
    rev_map = jnp.concatenate([offset_bucket_map[::-1], jnp.full((1,), -1, jnp.int32)]).reshape(1, -1)

    wide, narrow = shape((ROWS, MODEL_WIDTH), bf16), shape((ROWS, LANES), f32)
    narrow16 = shape((ROWS, LANES), bf16)

    joined_shape, ups_shape = shape((6, 384, MODEL_WIDTH), bf16), shape((6, LANES, 384), bf16)
    pair_outs = [wide, wide, wide, wide, shape((6, 8, 256), f32), shape((6, 7, LANES, 256), bf16), joined_shape, ups_shape]

    def pair_specs(first):
        specs = [pl.BlockSpec((ROWS, LANES), lambda p, *_: (0, first + p))] * 4
        for o in pair_outs[4:]:
            specs.append(pl.BlockSpec((1,) + o.shape[1:], lambda p, *_, n=len(o.shape): (first + p,) + (0,) * (n - 1)))
        return specs

    def half_of_rows(part):
        return pl.BlockSpec((HALF_ROWS, MODEL_WIDTH), lambda p, place, *_: (place[0] + 4 * part, 0))

    joined_scratch = [pltpu.VMEM((3, 384, MODEL_WIDTH), bf16), pltpu.VMEM((3, LANES, 384), bf16)]
    fixed = [wide, narrow16, narrow, narrow]
    *pair_state, normed1, mixed1, spread1, downs1 = call(
        first_kernel,
        (3,),
        [place, sequence_length_list],
        [tokens, tokens, gain1, downs_in, router1, *pack0, pack0[1], both1, both1, rev_map],
        [half_of_rows(0), half_of_rows(1), whole(gain1), whole(downs_in), whole(router1)]
        + [pack_part(384, 0), pack_part(192, 0), pack_part(48, 4), element_part(576, 240), pack_part(48, 17)]
        + [whole(rev_map)],
        pair_outs + fixed,
        pair_specs(0) + [whole(o) for o in fixed],
        scratch=joined_scratch + [pltpu.VMEM((256, MODEL_WIDTH), bf16)],
    )
    win1, wout1 = mp_swap(win0, 1), mp_swap(wout0, 1)
    pack2, normed1, win1, wout1 = lax.optimization_barrier((pack2, normed1, win1, wout1))
    pack3 = [mp_swap(p, 1) for p in pack2]
    inputs = [normed1, mixed1, *pack2, pack2[1], *pack3, pack3[1], rev_map]
    queries, keys, all_values, attended, lse, tiles, joined, ups = call(
        second_kernel,
        (3,),
        [place, sequence_length_list],
        inputs + pair_state,
        [whole(normed1), whole(mixed1)]
        + [pack_part(384, 0), pack_part(192, 0), pack_part(48, 4)] * 2
        + [whole(rev_map)]
        + [pl.BlockSpec(memory_space=pl.ANY)] * 8,
        pair_outs,
        pair_specs(3),
        scratch=joined_scratch,
        aliases={2 + len(inputs) + i: i for i in range(8)},
    )

    attended, more2 = lax.optimization_barrier((attended, more2))
    more3 = mp_swap(more2, 1)
    other2 = exchange(more2, "dp", dp_size, 1)
    mores = [more0, both1, more2, more3]
    ao_in, bo_in, bf_in = attention_output_down_weight.T, attention_output_up_weight, ffn_output_up_weight
    down_in, low_in = ffn_input_down_weight.T, ffn_output_down_weight.T

    def low_block(j):
        return pl.BlockSpec((LORA, MODEL_WIDTH), lambda i, place, *_: (0, jnp.bitwise_xor(place[0], j)))

    def small_inputs(first):
        values = [ao_in, bo_in, gain2, down_in, router2, bf_in]
        specs = [whole(a) for a in values]
        for j in (first, first + 1):
            values += [mores[j], low_in]
            specs += [pack_part(48, 4), low_block(j)]
        return values, specs

    hbm = pl.BlockSpec(memory_space=pltpu.HBM)
    shard_shape = shape((2, 2, LORA, MODEL_WIDTH), f32)
    wide_f32, wider, wider_f32 = shape((ROWS, MODEL_WIDTH), f32), shape((ROWS, WIDER), bf16), shape((ROWS, WIDER), f32)
    state_shapes = [wide_f32, wider, wider, shape((ROWS, 4 * LANES), f32), wider_f32, wider_f32]

    def held(array):
        return pltpu.VMEM(array.shape, array.dtype)

    map_scratch = [
        pltpu.VMEM((LANES, MODEL_WIDTH), bf16),
        pltpu.VMEM((LANES, MODEL_WIDTH), bf16),
        pltpu.VMEM((MODEL_WIDTH, MODEL_WIDTH), bf16),
        pltpu.VMEM((256, MODEL_WIDTH), bf16),
        pltpu.VMEM((LANES, MODEL_WIDTH), bf16),
        pltpu.VMEM((2, WIDER, MODEL_WIDTH), bf16),
        pltpu.VMEM((2, MODEL_WIDTH, WIDER), bf16),
    ]
    values, specs = small_inputs(0)
    inputs = [tokens, cotangent, attended] + mores + [spread1, win0, wout0, win1, wout1]
    *state, shard_grads = call(
        middle_kernel,
        (2,),
        [place],
        inputs + values,
        [token_block(), token_block(), rows_block(attended)]
        + [pack_part(192, 0)] * 4
        + [rows_block(spread1)]
        + [whole(a) for a in inputs[-4:]]
        + specs,
        state_shapes + [shard_shape],
        [rows_block(a) for a in state_shapes] + [whole(shard_shape)],
        scratch=map_scratch,
    )
    state[0], other2, wout2 = lax.optimization_barrier((state[0], other2, wout2))
    other3 = mp_swap(other2, 1)
    wout3 = mp_swap(wout2, 1)
    values, specs = small_inputs(2)
    ao_shape = shape((LORA, MODEL_WIDTH), f32)
    ff_shape = shape((dp_size, 4 * (FF_ALL + FF_OWN) // dp_size, LANES), bf16)
    inputs = [attended] + mores + [spread1, more2, other2, wout2, more3, other3, wout3] + state
    values += [group, pick, shard_grads]
    specs += [whole(a) for a in (group, pick, shard_grads)]
    outs = [wide, wide_f32, wide, narrow, ao_shape, ff_shape]
    result, ghidden, gatt, prod, ao_grad, ff_flat = call(
        post_kernel,
        (1,),
        [place, half],
        inputs + values,
        [hbm] * len(inputs) + specs,
        outs,
        [hbm] * 4 + [whole(o) for o in outs[4:]],
        scratch=[held(wide), held(narrow)]
        + [held(a) for a in state_shapes]
        + [held(wide), held(wide_f32), held(wide), held(narrow)]
        + map_scratch
        + [
            pltpu.VMEM((2, 2, LORA, MODEL_WIDTH), f32),
            pltpu.VMEM((256, MODEL_WIDTH), f32),
            pltpu.VMEM((LANES, MODEL_WIDTH), f32),
            pltpu.VMEM((LANES, MODEL_WIDTH), f32),
            pltpu.VMEM((LANES, MODEL_WIDTH), f32),
            pltpu.VMEM((1, MODEL_WIDTH), f32),
            pltpu.VMEM((4, FF_ROWS, MODEL_WIDTH), f32),
            pltpu.VMEM((FF_ALL + FF_OWN, LANES), f32),
            pltpu.SemaphoreType.DMA((18,)),
            pltpu.SemaphoreType.DMA((8,)),
        ],
    )
    result2 = mp_swap(result, 2)
    ff_pieces = lax.all_to_all(ff_flat, "dp", 0, 0)

    at_shapes = [shape((AT_ROWS, MODEL_WIDTH), f32)] + [shape((AT_ROWS, MODEL_WIDTH), bf16)] * 3
    gain_shape, up_shape = shape((1, MODEL_WIDTH), f32), shape((6 // PAIRS, LORA, 384 * PAIRS), f32)
    pair_shape, table_shape = shape((256, MODEL_WIDTH), f32), shape((6 // PAIRS, 8, LANES), f32)

    def part_call(kernel, part, more, outs, scratch):
        def block(array):
            return pl.BlockSpec((HALF_ROWS, array.shape[1]), lambda p, *_: (part, 0))

        pair = [pl.BlockSpec((HALF_ROWS, PAIRS * LANES), lambda p, *_: (part, p))] * 4
        if part == 0:
            tile = pl.BlockSpec((PAIRS, 1, LANES, 256), lambda p, *_: (p, 3, 0, 0))
        else:
            tile = pl.BlockSpec((PAIRS, 7, LANES, 256), lambda p, *_: (p, 0, 0, 0))
        three = [pl.BlockSpec((PAIRS,) + a.shape[1:], lambda p, *_: (p, 0, 0)) for a in (lse, joined, ups)]
        late = [normed1, spread1, downs1, prod, ghidden, tokens]
        fixed = [gain1, downs_in, router1, group, pick] + more
        return call(
            kernel,
            (6 // PAIRS,),
            [place, sequence_length_list],
            [queries, keys, all_values, gatt, lse, tiles, rev_map, turn, joined, ups, mixed1] + late + fixed,
            pair
            + [three[0], tile, whole(rev_map), whole(turn)]
            + three[1:]
            + [block(mixed1)]
            + [hbm] * len(late)
            + [whole(a) for a in fixed],
            outs,
            [whole(o) for o in outs],
            scratch=scratch
            + [
                pltpu.VMEM((HALF_ROWS, 384 * PAIRS), bf16),
                pltpu.VMEM((HALF_ROWS, LANES), f32),
                pltpu.VMEM((HALF_ROWS, MODEL_WIDTH), f32),
                pltpu.VMEM((256, MODEL_WIDTH), bf16),
            ]
            + [pltpu.VMEM((HALF_ROWS, a.shape[1]), a.dtype) for a in late]
            + [pltpu.SemaphoreType.DMA((len(late),))]
            + (
                [pltpu.VMEM((PAIRS, LONG_LEN, 1024), bf16)] * 2 + [pltpu.VMEM((PAIRS, 1024, LANES), bf16)] * 2
                if part == 1
                else []
            ),
        )

    early_shape = shape((FIRST_ROWS, MODEL_WIDTH), bf16)
    rest_shape = shape((ROWS - FIRST_ROWS, MODEL_WIDTH), bf16)
    gearly, *short_grads = part_call(
        short_kernel,
        0,
        [],
        [early_shape, shape((HALF_ROWS - FIRST_ROWS, MODEL_WIDTH), bf16), up_shape, pair_shape, gain_shape, table_shape],
        [],
    )
    gearly2 = mp_swap(gearly, 2)
    grest, ggain, *at_pieces = part_call(
        long_kernel,
        1,
        [ao_grad] + short_grads[1:] + short_grads[:1],
        [rest_shape, gain_shape] + at_shapes,
        [held(up_shape), held(table_shape), held(pair_shape), pltpu.VMEM((4, AT_ROWS, MODEL_WIDTH), f32)],
    )
    result2, gearly2, at_pieces, ff_pieces, ggain = lax.optimization_barrier(
        (result2, gearly2, at_pieces, ff_pieces, ggain)
    )
    at_parts = [at_pieces[0]] + [mp_swap(at_pieces[j], j) for j in (1, 2, 3)]
    ff_sums = jnp.sum(ff_pieces.astype(f32), 0).reshape(4, -1, LANES)
    ff_sum = ff_sums[0]
    for j in (1, 2, 3):
        ff_sum = ff_sum + mp_swap(ff_sums[j].astype(bf16), j).astype(f32)
    grest, at_parts, ff_sum = lax.optimization_barrier((grest, at_parts, ff_sum))
    grest2 = mp_swap(grest, 2)

    def spread_rows(layout, parts, onto=None):
        rows = sum(p.shape[0] for p in parts)
        inputs = list(parts) + ([] if onto is None else [onto])
        return call(
            functools.partial(spread_kernel, layout),
            (1,),
            [place],
            inputs,
            [hbm] * len(inputs),
            shape((4 * ROWS, MODEL_WIDTH), bf16),
            hbm,
            scratch=[
                pltpu.VMEM((rows, MODEL_WIDTH), bf16),
                pltpu.SemaphoreType.DMA((len(parts),)),
                pltpu.SemaphoreType.DMA((2 * len(parts),)),
            ],
            aliases=None if onto is None else {len(inputs): 0},
        )

    parts = at_parts + [ggain]
    flat_shape = shape((dp_size, (AT_ALL + AT_OWN) // dp_size, LANES), bf16)
    flat = call(
        sum_kernel,
        (1,),
        [],
        parts,
        [whole(a) for a in parts],
        flat_shape,
        whole(flat_shape),
        scratch=[pltpu.VMEM((AT_ALL + AT_OWN, LANES), f32)],
        limit=SMALL_LIMIT,
    )
    flat, result2 = lax.optimization_barrier((flat, result2))
    result1, result3 = mp_swap(result, 1), mp_swap(result2, 1)
    at_sum = scatter_over(flat, "dp", dp_size)
    gearly1, gearly3 = mp_swap(gearly, 1), mp_swap(gearly2, 1)
    at_sum, gearly1, gearly3 = lax.optimization_barrier((at_sum, gearly1, gearly3))
    ff_all, at_all = FF_ALL // dp_size, AT_ALL // dp_size
    mine = [ff_sum[:ff_all], at_sum[:at_all], ff_sum[ff_all:], at_sum[at_all:]]
    own = gather_over(jnp.concatenate(mine, 0).astype(bf16), "dp", dp_size)
    output = spread_rows([(0, 0), (1, 0), (2, 0), (3, 0)], [result, result1, result2, result3])
    grest1 = mp_swap(grest, 1)
    some = spread_rows(
        [(0, 0), (0, FIRST_ROWS), (1, 0), (1, FIRST_ROWS), (2, 0), (3, 0)],
        [gearly, grest, gearly1, grest1, gearly2, gearly3],
    )
    own, output, some, grest2 = lax.optimization_barrier((own, output, some, grest2))
    grest3 = mp_swap(grest2, 1)
    shared = own[:, : ff_all + at_all]
    two = mp_swap(shared, 2)
    one = mp_swap(shared, 1)
    grad_tokens = spread_rows([(2, FIRST_ROWS), (3, FIRST_ROWS)], [grest2, grest3], some)
    two, grad_tokens = lax.optimization_barrier((two, grad_tokens))
    three = mp_swap(two, 1)
    outs = [
        shape((6, LANES), f32),
        shape((6, LANES), f32),
        shape((3, LORA, MODEL_WIDTH), f32),
        shape((LORA, 192), f32),
        shape((2, LORA, 192), f32),
        shape((LORA, MODEL_WIDTH), f32),
        shape((LORA, MODEL_WIDTH), f32),
        shape((LORA, MODEL_WIDTH), f32),
        shape((LORA, MODEL_WIDTH), f32),
        shape((LORA, 4 * MODEL_WIDTH), f32),
        shape((LORA, MODEL_WIDTH), f32),
        shape((EXPERTS, MODEL_WIDTH), f32),
        shape((EXPERTS, MODEL_WIDTH), f32),
        shape((3, BUCKETS), f32),
    ]
    flats = [own, one, two, three]
    grads = call(
        unpack_kernel,
        (1,),
        [place],
        flats,
        [whole(a) for a in flats],
        outs,
        [whole(o) for o in outs],
        scratch=[pltpu.VMEM((4, LORA, MODEL_WIDTH), f32)] * 2
        + [pltpu.VMEM((4, FF_ALL, LANES), f32), pltpu.VMEM((4, AT_ALL, LANES), f32)]
        + [pltpu.VMEM((FF_OWN, LANES), f32), pltpu.VMEM((AT_OWN, LANES), f32)],
        limit=SMALL_LIMIT,
    )
    g1, g2, g_qkv, g_bq, g_bkv, g_ao, g_bo, g_ai, g_bi, g_aff, g_bff, g_r1, g_r2, g_table = grads
    return (
        output,
        grad_tokens,
        g1.reshape(-1),
        g2.reshape(-1),
        jnp.transpose(g_qkv, (0, 2, 1)),
        g_bq,
        g_bkv,
        g_ao.T,
        g_bo,
        g_ai.T,
        g_bi,
        g_aff.T,
        g_bff,
        g_r1.T,
        g_r2.T,
        g_table.T,
    )


def solution(mesh):
    in_specs = (
        P("dp", None),
        P("dp", None),
        P(),
        P(),
        P(None, "mp"),
        P(None, None, "mp"),
        P("mp", None),
        P(None, "mp"),
        P("mp", None),
        P(),
        P(None, "mp"),
        P(None, None, "mp"),
        P(),
        P(),
        P(),
        P(None, "mp"),
        P(),
        P(),
        P(),
        P(),
        P(None, "mp"),
        P(),
        P("dp"),
    )
    out_specs = (
        P("dp", None),
        P("dp", None),
        P(),
        P(),
        P(),
        P(None, "mp"),
        P(None, None, "mp"),
        P(),
        P(),
        P(),
        P(None, "mp"),
        P(),
        P(),
        P(),
        P(),
        P(None, "mp"),
    )
    step = functools.partial(local, mesh.shape["dp"], mesh.shape["mp"])
    return jax.shard_map(step, mesh=mesh, in_specs=in_specs, out_specs=out_specs, check_vma=False)
```
